32 devices in a mesh: tor: 2 (over x), pol: 16 (over z, y, core).
Axes of the slice: x: 2, y: 2, z: 4, core: 2. Of those that a mesh axis runs over, the one named last changes fastest.
Arguments:
- plasma_state: float32 [6, 2, 128, 256], P(None, 'tor', 'pol'), may hold values from -3 to 3
- right_side: float32 [6, 2, 128, 256], P(None, 'tor', 'pol'), may hold values from -12 to 12
- resistivity: float32 [2, 128, 256], P('tor', 'pol'), may hold values from 0.05 to 0.6
- jacobi_blocks: float32 [6, 6, 2, 128, 256], P(None, None, 'tor', 'pol'), may hold values from -0.6 to 1.6, as said below
Outputs:
- update: float32 [6, 2, 128, 256], P(None, 'tor', 'pol')
- estimates: float32 [3], replicated
The draws below stay inside these ranges and needn't reach their ends.
Inputs may be any that keep to these rules, and one draw needn't show every extreme that they name: `jacobi_blocks`: each block's diagonal entries lie in 0.4 to 1.6.
All inputs are finite; a program needn't handle non-finite values.
Results may differ from the reference program's by a relative error of at most 0.006.
Values may be sent and summed in bfloat16 or wider, within the bound.
No kernel may reach another device: no remote copies, remote signals or barrier semaphores. Data moves between devices by JAX's collectives and lax.ppermute only.
A program may use at most 64 MiB of HBM per device.

```python
import math
import jax
import jax.numpy as jnp
from jax import lax

DEPTH = 256
ITERS = 3
PLANES = 2
ROWS = 128


def draw_right_side(key, part):
    shape = (6, PLANES, ROWS, DEPTH)
    noise_key = jax.random.fold_in(key, 11)
    plane_pos = lax.broadcasted_iota(jnp.float32, shape, 1)
    row_pos = lax.broadcasted_iota(jnp.float32, shape, 2)
    envelope = 1.0 + plane_pos / max(PLANES - 1, 1) + row_pos / max(ROWS - 1, 1)
    noise = jnp.clip(jax.random.normal(noise_key, shape, jnp.float32), -4.0, 4.0)
    return noise * envelope


def draw_jacobi_blocks(key, part):
    shape = (6, 6, PLANES, ROWS, DEPTH)
    diag_key = jax.random.fold_in(key, 21)
    off_key = jax.random.fold_in(key, 22)
    on_diagonal = lax.broadcasted_iota(jnp.int32, shape, 0) == lax.broadcasted_iota(jnp.int32, shape, 1)
    diagonal = jax.random.uniform(diag_key, shape, jnp.float32, 0.6, 1.4)
    coupling = 0.12 * jnp.clip(jax.random.normal(off_key, shape, jnp.float32), -5.0, 5.0)
    return jnp.where(on_diagonal, diagonal, coupling)


def steps_of(stream_key, dims, shards, smallest, top_value):
    def one(position, blocks):
        heights = jax.random.uniform(jax.random.fold_in(jax.random.fold_in(stream_key, 6), position), (blocks,), jnp.float32, smallest / len(shards), top_value / len(shards))
        return jnp.repeat(jnp.exp(heights), dims[position] // blocks).reshape((-1,) + (1,) * (len(dims) - position - 1))

    factor_of = one(*shards[0])
    for cut in shards[1:]:
        factor_of = factor_of * one(*cut)
    return factor_of


def centred(own_key, extent, width, most, pieces=(), held_as=jnp.bfloat16):
    drawn = jax.random.normal(own_key, extent, jnp.float32) * width
    if len(pieces) > 0:
        drawn = steps_of(own_key, extent, pieces, -0.22, 0.18) * drawn
    return jnp.clip(drawn, min=-most, max=most).astype(held_as)


def setup_inputs(seed: int = 0) -> dict:
    splits = jax.random.split(jax.random.key(seed), 5)
    plasma_state = centred(splits[0], (6, PLANES, ROWS, DEPTH), 0.5, 3.0, ((1, 2), (2, 16)), jnp.float32)
    right_side = draw_right_side(jax.random.fold_in(splits[4], 71), 0)
    resistivity = jnp.clip(jnp.exp(math.log(0.6) - 2.4849067 * jax.random.uniform(splits[2], (PLANES, ROWS, DEPTH), jnp.float32) ** steps_of(splits[2], (PLANES, ROWS, DEPTH), ((0, 2), (1, 16)), -0.2, 0.2)), 0.05, 0.6)
    jacobi_blocks = draw_jacobi_blocks(jax.random.fold_in(splits[4], 71), 0)
    return dict(plasma_state=plasma_state, right_side=right_side, resistivity=resistivity, jacobi_blocks=jacobi_blocks)


inverse_step = 1.0
viscosity = 0.2
epsilon = 1e-06

def neighbour(values, array_axis, offset, periodic):
    if periodic:
        return jnp.roll(values, -offset, array_axis)
    length = values.shape[array_axis]
    widths = [(0, 0)] * values.ndim
    widths[array_axis] = (1, 1)
    padded = jnp.pad(values, widths)
    return lax.slice_in_dim(padded, 1 + offset, 1 + offset + length, axis=array_axis)

def linear_flux(plasma, tangent, direction):
    magnetic = plasma[0:3]
    velocity = plasma[3:6]
    tang_mag = tangent[0:3]
    tang_vel = tangent[3:6]
    pressure = lax.optimization_barrier(jnp.sum(magnetic * tang_mag, axis=0))
    components = []
    for inner_index in range(3):
        components.append(tang_vel[direction] * magnetic[inner_index] + velocity[direction] * tang_mag[inner_index] - tang_mag[direction] * velocity[inner_index] - magnetic[direction] * tang_vel[inner_index])
    for inner_index in range(3):
        moment = tang_vel[direction] * velocity[inner_index] + velocity[direction] * tang_vel[inner_index] - tang_mag[direction] * magnetic[inner_index] - magnetic[direction] * tang_mag[inner_index]
        if inner_index == direction:
            moment = moment + pressure
        components.append(moment)
    return jnp.stack(components)

def diffusion_field(resistivity):
    shape = (3,) + resistivity.shape
    return jnp.concatenate([jnp.broadcast_to(resistivity[None], shape), jnp.full(shape, viscosity, jnp.float32)])

def jacobian_product(plasma, tangent, resistivity):
    result_sum = inverse_step * tangent
    laplace_sum = jnp.zeros_like(tangent)
    for direction, periodic in ((0, True), (1, False), (2, False)):
        flux_term = linear_flux(plasma, tangent, direction)
        result_sum = result_sum + 0.5 * (neighbour(flux_term, direction + 1, 1, periodic) - neighbour(flux_term, direction + 1, -1, periodic))
        laplace_sum = laplace_sum + neighbour(tangent, direction + 1, 1, periodic) + neighbour(tangent, direction + 1, -1, periodic) - 2.0 * tangent
    return result_sum - diffusion_field(resistivity) * laplace_sum

def precondition(blocks, vector):
    return jnp.einsum('abpqr,bpqr->apqr', blocks, vector.astype(jnp.float32), precision=lax.Precision.HIGHEST)

def least_squares(columns, initial_norm):
    count = len(columns)
    rhs_list = [initial_norm] + [jnp.float32(0.0)] * count
    cosines = []
    sines = []
    triangle = []
    estimate_list = []
    for column in range(count):
        entries = list(columns[column])
        for inner_index in range(column):
            first_value = entries[inner_index]
            second_value = entries[inner_index + 1]
            entries[inner_index] = cosines[inner_index] * first_value + sines[inner_index] * second_value
            entries[inner_index + 1] = -sines[inner_index] * first_value + cosines[inner_index] * second_value
        first_value = entries[column]
        second_value = entries[column + 1]
        radius = jnp.sqrt(first_value * first_value + second_value * second_value)
        cosine = first_value / radius
        sine_value = second_value / radius
        cosines.append(cosine)
        sines.append(sine_value)
        entries[column] = radius
        triangle.append(entries[:column + 1])
        previous = rhs_list[column]
        rhs_list[column] = cosine * previous
        rhs_list[column + 1] = -sine_value * previous
        estimate_list.append(jnp.abs(rhs_list[column + 1]))
    weights = [jnp.float32(0.0)] * count
    for column in reversed(range(count)):
        partial_value = rhs_list[column]
        for later in range(column + 1, count):
            partial_value = partial_value - triangle[later][column] * weights[later]
        weights[column] = partial_value / triangle[column][column]
    return (weights, estimate_list)

def reference(plasma_state, right_side, resistivity, jacobi_blocks):
    cell_count = 6 * PLANES * ROWS * DEPTH
    initial_norm = jnp.sqrt(jnp.sum(right_side * right_side) + epsilon)
    krylov_basis = [(right_side / initial_norm).astype(jnp.bfloat16)]
    directions = []
    columns = []
    for column in range(ITERS):
        tangent = precondition(jacobi_blocks, krylov_basis[column])
        image = jacobian_product(plasma_state, tangent, resistivity)
        directions.append(tangent)
        coefficients = [jnp.sum(image * earlier.astype(jnp.float32)) for earlier in krylov_basis]
        remainder = image
        for inner_index in range(column + 1):
            remainder = remainder - coefficients[inner_index] * krylov_basis[inner_index].astype(jnp.float32)
        new_norm = jnp.sqrt(jnp.sum(remainder * remainder) + epsilon)
        columns.append(coefficients + [new_norm])
        if column + 1 < ITERS:
            krylov_basis.append((remainder / new_norm).astype(jnp.bfloat16))
    weights, estimate_list = least_squares(columns, initial_norm)
    update = weights[0] * directions[0]
    for column in range(1, ITERS):
        update = update + weights[column] * directions[column]
    estimates = jnp.stack(estimate_list) / jnp.sqrt(jnp.float32(cell_count))
    return (update, estimates)
```

```python
import functools

import jax
import jax.numpy as jnp
from jax import lax
from jax.experimental import pallas as pl
from jax.experimental.pallas import tpu as pltpu
from jax.sharding import PartitionSpec as P

ITERS = 3
SHIFTS = (1.0, 2.0, 3.0)
inverse_step = 1.0
viscosity = 0.2
epsilon = 1e-06
AXES = ("tor", "pol")
PAIRS = [(i, j) for i in range(ITERS + 1) for j in range(i, ITERS + 1)]
BF16 = jnp.bfloat16
F32 = jnp.float32


def linear_flux(plasma, tangent, direction):
    magnetic, velocity = plasma[0:3], plasma[3:6]
    tang_mag, tang_vel = tangent[0:3], tangent[3:6]
    pressure = magnetic[0] * tang_mag[0] + magnetic[1] * tang_mag[1] + magnetic[2] * tang_mag[2]
    components = []
    for i in range(3):
        components.append(
            tang_vel[direction] * magnetic[i]
            + velocity[direction] * tang_mag[i]
            - tang_mag[direction] * velocity[i]
            - magnetic[direction] * tang_vel[i]
        )
    for i in range(3):
        moment = (
            tang_vel[direction] * velocity[i]
            + velocity[direction] * tang_vel[i]
            - tang_mag[direction] * magnetic[i]
            - magnetic[direction] * tang_mag[i]
        )
        if i == direction:
            moment = moment + pressure
        components.append(moment)
    return components


def least_squares(columns, initial_norm):
    count = len(columns)
    rhs_list = [initial_norm] + [None] * count
    cosines = []
    sines = []
    triangle = []
    estimate_list = []
    for column in range(count):
        entries = list(columns[column])
        for i in range(column):
            first_value, second_value = entries[i], entries[i + 1]
            entries[i] = cosines[i] * first_value + sines[i] * second_value
            entries[i + 1] = -sines[i] * first_value + cosines[i] * second_value
        first_value, second_value = entries[column], entries[column + 1]
        radius = jnp.sqrt(first_value * first_value + second_value * second_value)
        cosine = first_value / radius
        sine_value = second_value / radius
        cosines.append(cosine)
        sines.append(sine_value)
        entries[column] = radius
        triangle.append(entries[: column + 1])
        previous = rhs_list[column]
        rhs_list[column] = cosine * previous
        rhs_list[column + 1] = -sine_value * previous
        estimate_list.append(jnp.abs(rhs_list[column + 1]))
    weights = [None] * count
    for column in reversed(range(count)):
        partial_value = rhs_list[column]
        for later in range(column + 1, count):
            partial_value = partial_value - triangle[later][column] * weights[later]
        weights[column] = partial_value / triangle[column][column]
    return weights, estimate_list


def solve_from_gram(gram):
    count = ITERS + 1

    def inner(left, right):
        total = None
        for i in range(count):
            row = None
            for j in range(count):
                if right[j] is None:
                    continue
                term = gram[(min(i, j), max(i, j))] * right[j]
                row = term if row is None else row + term
            if left[i] is None or row is None:
                continue
            term = left[i] * row
            total = term if total is None else total + term
        return total

    def minus(left, factor, right):
        out = []
        for a, b in zip(left, right):
            if b is None:
                out.append(a)
            else:
                out.append(a - factor * b)
        return out

    initial_norm = jnp.sqrt(gram[(0, 0)] + epsilon)
    basis = [[1.0 / initial_norm] + [None] * ITERS]
    columns = []
    for column in range(ITERS):
        vector = basis[column]
        image = []
        for i in range(count):
            entry = None
            if vector[i] is not None:
                entry = SHIFTS[i] * vector[i]
            if i > 0 and vector[i - 1] is not None:
                entry = vector[i - 1] if entry is None else entry + vector[i - 1]
            image.append(entry)
        coefficients = [inner(earlier, image) for earlier in basis]
        remainder = image
        for coefficient, earlier in zip(coefficients, basis):
            remainder = minus(remainder, coefficient, earlier)
        square = jnp.maximum(inner(remainder, remainder), 0.0)
        new_norm = jnp.sqrt(square + epsilon)
        columns.append(coefficients + [new_norm])
        if column + 1 < ITERS:
            scale = 1.0 / new_norm
            basis.append([None if r is None else r * scale for r in remainder])
    weights, estimate_list = least_squares(columns, initial_norm)
    factors = []
    for k in range(ITERS):
        total = None
        for weight, vector in zip(weights, basis):
            if vector[k] is not None:
                term = weight * vector[k]
                total = term if total is None else total + term
        factors.append(total)
    return factors, estimate_list


P_ROWS, Q_ROWS = 128, 64


def pack_kernel(plasma_ref, rhs_ref, blocks_ref, res_ref, t0_ref, bulk_ref, edge_ref, side_ref, scr_p, scr_q):
    vector = [rhs_ref[b] for b in range(6)]
    t0 = []
    for a in range(6):
        total = blocks_ref[a, 0] * vector[0]
        for b in range(1, 6):
            total = total + blocks_ref[a, b] * vector[b]
        t0_ref[a] = total
        t0.append(total)
    state = [plasma_ref[a] for a in range(6)]
    deep = t0 + state
    wide = [blocks_ref[i // 6, i % 6] for i in range(36)] + [res_ref[...]]
    fields = wide[:36] + deep + [wide[36], wide[36]]
    for g in range(25):
        pair = jnp.concatenate([fields[2 * g], fields[2 * g + 1]], axis=0)
        bulk_ref[pl.ds(16 * g, 16), :] = pair.astype(BF16)
    zeros = jnp.zeros((8, deep[0].shape[1]), F32)
    for side in range(2):
        scr_p[pl.ds(P_ROWS - 8, 8), :] = zeros
        scr_q[pl.ds(Q_ROWS - 8, 8), :] = zeros
        for f, value in enumerate(deep):
            scr_p[pl.ds(4 * f, 4), :] = value[0:4] if side == 0 else value[4:8]
            scr_q[pl.ds(2 * f, 2), :] = value[0:2] if side == 0 else value[6:8]
        for f, value in enumerate(wide):
            scr_p[pl.ds(48 + 2 * f, 2), :] = value[0:2] if side == 0 else value[6:8]
            scr_q[pl.ds(24 + f, 1), :] = value[0:1] if side == 0 else value[7:8]
        side_ref[side] = scr_p[...].astype(BF16)
        edge_ref[side] = scr_q[...].astype(BF16)


def krylov_kernel(
    plasma_ref, rhs_ref, blocks_ref, res_ref, t0_ref, bulk_ref, above_ref, below_ref,
    gram_ref, t_ref, up, down, blk_p, blk_q, st_p, st_q, res_s,
):
    width = rhs_ref.shape[-1]
    up[...] = above_ref[...].astype(F32)
    down[...] = below_ref[...].astype(F32)
    zeros = jnp.zeros((8, width), F32)

    def halo(ref, at, offset, rows):
        if rows < 4:
            ref[at, 8:16] = zeros
        ref[at, 8 : 8 + rows] = down[pl.ds(offset, rows), :]
        ref[at, 16 - rows : 16] = up[pl.ds(offset, rows), :]

    def other(field):
        pair = bulk_ref[pl.ds(16 * (field // 2), 16), :].astype(F32)
        return pair[0:8] if field % 2 == 0 else pair[8:16]

    for i in range(36):
        blk_p[i, 0:8] = blocks_ref[i // 6, i % 6]
        halo(blk_p, i, 48 + 2 * i, 2)
        blk_q[i, 0:8] = other(i)
        halo(blk_q, i, P_ROWS + 24 + i, 1)
    for i in range(12):
        st_p[i, 0:8] = t0_ref[i] if i < 6 else plasma_ref[i - 6]
        halo(st_p, i, 4 * i, 4)
        st_q[i, 0:8] = other(36 + i)
        halo(st_q, i, P_ROWS + 2 * i, 2)
    res_s[0, 0:8] = res_ref[...]
    halo(res_s, 0, 120, 2)
    res_s[1, 0:8] = other(48)
    halo(res_s, 1, P_ROWS + 60, 1)

    def lane(shape):
        return lax.broadcasted_iota(jnp.int32, shape, 1)

    def depth_next(x):
        return jnp.where(lane(x.shape) == width - 1, 0.0, pltpu.roll(x, width - 1, 1))

    def depth_prev(x):
        return jnp.where(lane(x.shape) == 0, 0.0, pltpu.roll(x, 1, 1))

    def jacobian(plasma, tangent, plasma_next, tangent_next, plasma_prev, tangent_prev, res, rows):
        flux_next = linear_flux(plasma_next, tangent_next, 0)
        flux_prev = linear_flux(plasma_prev, tangent_prev, 0)
        flux_rows = linear_flux(plasma, tangent, 1)
        own = [x[0:rows] for x in tangent]
        flux_depth = linear_flux([x[0:rows] for x in plasma], own, 2)
        out = []
        for i in range(6):
            total = inverse_step * own[i] + 0.5 * (flux_next[i][0:rows] - flux_prev[i][0:rows])
            laplace = tangent_next[i][0:rows] + tangent_prev[i][0:rows] - 2.0 * own[i]
            total = total + 0.5 * (
                pltpu.roll(flux_rows[i], 15, 0)[0:rows] - pltpu.roll(flux_rows[i], 1, 0)[0:rows]
            )
            laplace = laplace + (
                pltpu.roll(tangent[i], 15, 0)[0:rows] + pltpu.roll(tangent[i], 1, 0)[0:rows] - 2.0 * own[i]
            )
            total = total + 0.5 * (depth_next(flux_depth[i]) - depth_prev(flux_depth[i]))
            laplace = laplace + (depth_next(own[i]) + depth_prev(own[i]) - 2.0 * own[i])
            out.append(total - (res[0:rows] if i < 3 else viscosity) * laplace)
        return out

    def precondition(ref, vector, rows):
        out = []
        for a in range(6):
            total = ref[6 * a, 0:rows] * vector[0]
            for b in range(1, 6):
                total = total + ref[6 * a + b, 0:rows] * vector[b]
            out.append(total)
        return out

    plasma_p = [st_p[6 + i] for i in range(6)]
    plasma_q = [st_q[6 + i] for i in range(6)]
    half_p = [x[0:8] for x in plasma_p]
    half_q = [x[0:8] for x in plasma_q]
    krylov = [[rhs_ref[i] for i in range(6)]]
    tang_p = [st_p[i] for i in range(6)]
    tang_q = [st_q[i] for i in range(6)]
    for i in range(6):
        t_ref[i] = t0_ref[i]

    image_p = jacobian(plasma_p, tang_p, plasma_q, tang_q, plasma_q, tang_q, res_s[0], 16)
    image_q = jacobian(plasma_q, tang_q, plasma_p, tang_p, plasma_p, tang_p, res_s[1], 16)
    krylov.append([image_p[i][0:8] - SHIFTS[0] * krylov[0][i] for i in range(6)])
    next_p = [x - SHIFTS[0] * t for x, t in zip(precondition(blk_p, image_p, 16), tang_p)]
    next_q = [x - SHIFTS[0] * t for x, t in zip(precondition(blk_q, image_q, 16), tang_q)]
    for i in range(6):
        t_ref[6 + i] = next_p[i][0:8]

    image_p = jacobian(plasma_p, next_p, plasma_q, next_q, plasma_q, next_q, res_s[0], 16)
    image_q = jacobian(plasma_q, next_q, half_p, [x[0:8] for x in next_p], half_p, [x[0:8] for x in next_p], res_s[1], 8)
    krylov.append([image_p[i][0:8] - SHIFTS[1] * krylov[1][i] for i in range(6)])
    last_p = [x - SHIFTS[1] * t for x, t in zip(precondition(blk_p, image_p, 16), next_p)]
    last_q = [x - SHIFTS[1] * t[0:8] for x, t in zip(precondition(blk_q, image_q, 8), next_q)]
    for i in range(6):
        t_ref[12 + i] = last_p[i][0:8]

    image_p = jacobian(plasma_p, last_p, half_q, last_q, half_q, last_q, res_s[0], 8)
    krylov.append([image_p[i] - SHIFTS[2] * krylov[2][i] for i in range(6)])

    out = jnp.zeros((1, 128), F32)
    lanes = lax.broadcasted_iota(jnp.int32, (1, 128), 1)
    for k, (i, j) in enumerate(PAIRS):
        total = krylov[i][0] * krylov[j][0]
        for f in range(1, 6):
            total = total + krylov[i][f] * krylov[j][f]
        total = jnp.sum(jnp.sum(total, axis=0, keepdims=True), axis=1, keepdims=True)
        out = jnp.where(lanes == k, total, out)
    gram_ref[...] = jnp.broadcast_to(out[None], gram_ref.shape)


def finish_kernel(inverse_root, gram_ref, t_ref, update_ref, estimates_ref):
    gathered = gram_ref[...]
    sums = jnp.sum(gathered, axis=0)
    lanes = lax.broadcasted_iota(jnp.int32, sums.shape, 1)
    gram = {}
    for k, pair in enumerate(PAIRS):
        gram[pair] = jnp.sum(jnp.where(lanes == k, sums, 0.0), axis=1, keepdims=True)
    factors, estimate_list = solve_from_gram(gram)
    width = update_ref.shape[-1]
    wide = [jnp.broadcast_to(f, (8, width)) for f in factors]
    for i in range(6):
        update_ref[i] = wide[0] * t_ref[i] + wide[1] * t_ref[6 + i] + wide[2] * t_ref[12 + i]
    out = jnp.zeros((1, 128), F32)
    for k, value in enumerate(estimate_list):
        out = jnp.where(lanes == k, value * inverse_root, out)
    estimates_ref[...] = out


def two_planes(pol, plasma_state, right_side, resistivity, jacobi_blocks):
    rows, width = plasma_state.shape[2], plasma_state.shape[3]
    count = 2 * pol

    def pairs(partner):
        out = []
        for t in range(2):
            for p in range(pol):
                other = partner(t, p)
                if 0 <= other[1] < pol:
                    out.append((t * pol + p, other[0] * pol + other[1]))
        return out

    across = pairs(lambda t, p: (1 - t, p))
    core = pairs(lambda t, p: (t, p ^ 1))
    outer = pairs(lambda t, p: (t, p - 1 if p % 2 == 0 else p + 1))

    plasma = plasma_state.reshape(6, rows, width)
    rhs = right_side.reshape(6, rows, width)
    res = resistivity.reshape(rows, width)
    blocks = jacobi_blocks.reshape(6, 6, rows, width)
    vmem = pl.BlockSpec(memory_space=pltpu.VMEM)
    shape = jax.ShapeDtypeStruct
    t0, bulk, edge, side = pl.pallas_call(
        pack_kernel,
        out_shape=(
            shape((6, rows, width), F32),
            shape((400, width), BF16),
            shape((2, Q_ROWS, width), BF16),
            shape((2, P_ROWS, width), BF16),
        ),
        in_specs=[vmem] * 4,
        out_specs=(vmem,) * 4,
        scratch_shapes=[pltpu.VMEM((P_ROWS, width), F32), pltpu.VMEM((Q_ROWS, width), F32)],
    )(plasma, rhs, blocks, res)
    edge = lax.ppermute(edge, AXES, across)
    bulk = lax.ppermute(bulk, AXES, across)
    even = lax.axis_index("pol") % 2 == 0
    both = jnp.concatenate([side, edge], axis=1)
    from_core = lax.ppermute(jnp.where(even, both[1], both[0]), AXES, core)
    from_outer = lax.ppermute(jnp.where(even, both[0], both[1]), AXES, outer)
    above = jnp.where(even, from_outer, from_core)
    below = jnp.where(even, from_core, from_outer)
    slab = P_ROWS + Q_ROWS
    gram, tangents = pl.pallas_call(
        krylov_kernel,
        out_shape=(shape((count, 1, 128), F32), shape((18, rows, width), F32)),
        in_specs=[vmem] * 8,
        out_specs=(vmem,) * 2,
        scratch_shapes=[
            pltpu.VMEM((slab, width), F32),
            pltpu.VMEM((slab, width), F32),
            pltpu.VMEM((36, 16, width), F32),
            pltpu.VMEM((36, 16, width), F32),
            pltpu.VMEM((12, 16, width), F32),
            pltpu.VMEM((12, 16, width), F32),
            pltpu.VMEM((2, 16, width), F32),
        ],
    )(plasma, rhs, blocks, res, t0, bulk, above, below)
    gram = lax.all_to_all(gram, AXES, 0, 0, tiled=True)
    inverse_root = float((6.0 * count * rows * width) ** -0.5)
    update, estimates = pl.pallas_call(
        functools.partial(finish_kernel, inverse_root),
        out_shape=(shape((6, rows, width), F32), shape((1, 128), F32)),
        in_specs=[vmem] * 2,
        out_specs=(vmem,) * 2,
    )(gram, tangents)
    return update.reshape(plasma_state.shape), estimates[0, :ITERS]


def padded(cells, axis, dim, closed):
    count = lax.axis_size(axis)
    ends = count if closed else count - 1
    size = cells.shape[dim]
    head = lax.slice_in_dim(cells, 0, 1, axis=dim)
    tail = lax.slice_in_dim(cells, size - 1, size, axis=dim)
    before = lax.ppermute(tail, axis, [(i, (i + 1) % count) for i in range(ends)])
    after = lax.ppermute(head, axis, [((i + 1) % count, i) for i in range(ends)])
    return jnp.concatenate([before, cells, after], axis=dim)


def any_planes(plasma_state, right_side, resistivity, jacobi_blocks):
    cell_count = right_side.size * lax.axis_size("tor") * lax.axis_size("pol")
    fixed = jnp.full((3,) + resistivity.shape, viscosity, F32)
    diffusion = jnp.concatenate([jnp.broadcast_to(resistivity[None], fixed.shape), fixed])

    def around(cells):
        planes = padded(cells.astype(BF16), "tor", 1, True).astype(F32)
        planes = jnp.concatenate([planes[:, :1], cells, planes[:, -1:]], axis=1)
        deep = jnp.pad(cells, ((0, 0), (0, 0), (0, 0), (1, 1)))
        return planes, padded(cells, "pol", 2, False), deep

    plasma_around = around(plasma_state)
    vectors, tangents = [right_side], []
    for shift in SHIFTS:
        vector = vectors[-1]
        tangent = jnp.sum(jacobi_blocks * vector[None], axis=1)
        tangents.append(tangent)
        image = inverse_step * tangent
        laplace = jnp.zeros_like(tangent)
        for direction, (plasma, cells) in enumerate(zip(plasma_around, around(tangent))):
            dim = direction + 1
            flux = jnp.stack(linear_flux(plasma, cells, direction))
            size = cells.shape[dim]
            part = functools.partial(lax.slice_in_dim, axis=dim)
            image = image + 0.5 * (part(flux, 2, size) - part(flux, 0, size - 2))
            laplace = laplace + part(cells, 2, size) + part(cells, 0, size - 2) - 2.0 * tangent
        vectors.append(image - diffusion * laplace - shift * vector)
    local = jnp.stack([jnp.sum(vectors[i] * vectors[j]) for i, j in PAIRS])
    gram = lax.psum(local, AXES)
    factors, estimate_list = solve_from_gram({pair: gram[k] for k, pair in enumerate(PAIRS)})
    update = sum(factor * tangent for factor, tangent in zip(factors, tangents))
    return update, jnp.stack(estimate_list) / jnp.sqrt(F32(cell_count))


def solution(mesh):
    tor, pol = mesh.shape["tor"], mesh.shape["pol"]

    def shards(plasma_state, right_side, resistivity, jacobi_blocks):
        _, planes, rows, width = plasma_state.shape
        fast = tor == 2 and planes == 1 and pol % 2 == 0 and rows == 8 and width % 128 == 0
        if fast:
            return two_planes(pol, plasma_state, right_side, resistivity, jacobi_blocks)
        return any_planes(plasma_state, right_side, resistivity, jacobi_blocks)

    return jax.shard_map(
        shards,
        mesh=mesh,
        in_specs=(
            P(None, "tor", "pol", None),
            P(None, "tor", "pol", None),
            P("tor", "pol", None),
            P(None, None, "tor", "pol", None),
        ),
        out_specs=(P(None, "tor", "pol", None), P()),
        check_vma=False,
    )
```

```python
import functools

import jax
import jax.numpy as jnp
from jax import lax
from jax.experimental import pallas as pl
from jax.experimental.pallas import tpu as pltpu
from jax.sharding import PartitionSpec as P

ITERS = 3
SHIFTS = (1.0, 2.0, 3.0)
inverse_step = 1.0
viscosity = 0.2
epsilon = 1e-06
AXES = ("tor", "pol")
PAIRS = [(i, j) for i in range(ITERS + 1) for j in range(i, ITERS + 1)]
BF16 = jnp.bfloat16
F32 = jnp.float32


def linear_flux(plasma, tangent, direction):
    magnetic, velocity = plasma[0:3], plasma[3:6]
    tang_mag, tang_vel = tangent[0:3], tangent[3:6]
    pressure = magnetic[0] * tang_mag[0] + magnetic[1] * tang_mag[1] + magnetic[2] * tang_mag[2]
    components = []
    for i in range(3):
        components.append(
            tang_vel[direction] * magnetic[i]
            + velocity[direction] * tang_mag[i]
            - tang_mag[direction] * velocity[i]
            - magnetic[direction] * tang_vel[i]
        )
    for i in range(3):
        moment = (
            tang_vel[direction] * velocity[i]
            + velocity[direction] * tang_vel[i]
            - tang_mag[direction] * magnetic[i]
            - magnetic[direction] * tang_mag[i]
        )
        if i == direction:
            moment = moment + pressure
        components.append(moment)
    return components


def least_squares(columns, initial_norm):
    count = len(columns)
    rhs_list = [initial_norm] + [None] * count
    cosines = []
    sines = []
    triangle = []
    estimate_list = []
    for column in range(count):
        entries = list(columns[column])
        for i in range(column):
            first_value, second_value = entries[i], entries[i + 1]
            entries[i] = cosines[i] * first_value + sines[i] * second_value
            entries[i + 1] = -sines[i] * first_value + cosines[i] * second_value
        first_value, second_value = entries[column], entries[column + 1]
        radius = jnp.sqrt(first_value * first_value + second_value * second_value)
        cosine = first_value / radius
        sine_value = second_value / radius
        cosines.append(cosine)
        sines.append(sine_value)
        entries[column] = radius
        triangle.append(entries[: column + 1])
        previous = rhs_list[column]
        rhs_list[column] = cosine * previous
        rhs_list[column + 1] = -sine_value * previous
        estimate_list.append(jnp.abs(rhs_list[column + 1]))
    weights = [None] * count
    for column in reversed(range(count)):
        partial_value = rhs_list[column]
        for later in range(column + 1, count):
            partial_value = partial_value - triangle[later][column] * weights[later]
        weights[column] = partial_value / triangle[column][column]
    return weights, estimate_list


def solve_from_gram(gram):
    count = ITERS + 1

    def inner(left, right):
        total = None
        for i in range(count):
            row = None
            for j in range(count):
                if right[j] is None:
                    continue
                term = gram[(min(i, j), max(i, j))] * right[j]
                row = term if row is None else row + term
            if left[i] is None or row is None:
                continue
            term = left[i] * row
            total = term if total is None else total + term
        return total

    def minus(left, factor, right):
        out = []
        for a, b in zip(left, right):
            if b is None:
                out.append(a)
            else:
                out.append(a - factor * b)
        return out

    initial_norm = jnp.sqrt(gram[(0, 0)] + epsilon)
    basis = [[1.0 / initial_norm] + [None] * ITERS]
    columns = []
    for column in range(ITERS):
        vector = basis[column]
        image = []
        for i in range(count):
            entry = None
            if vector[i] is not None:
                entry = SHIFTS[i] * vector[i]
            if i > 0 and vector[i - 1] is not None:
                entry = vector[i - 1] if entry is None else entry + vector[i - 1]
            image.append(entry)
        coefficients = [inner(earlier, image) for earlier in basis]
        remainder = image
        for coefficient, earlier in zip(coefficients, basis):
            remainder = minus(remainder, coefficient, earlier)
        square = jnp.maximum(inner(remainder, remainder), 0.0)
        new_norm = jnp.sqrt(square + epsilon)
        columns.append(coefficients + [new_norm])
        if column + 1 < ITERS:
            scale = 1.0 / new_norm
            basis.append([None if r is None else r * scale for r in remainder])
    weights, estimate_list = least_squares(columns, initial_norm)
    factors = []
    for k in range(ITERS):
        total = None
        for weight, vector in zip(weights, basis):
            if vector[k] is not None:
                term = weight * vector[k]
                total = term if total is None else total + term
        factors.append(total)
    return factors, estimate_list


in_vmem = functools.partial(pltpu.with_memory_space_constraint, memory_space=pltpu.VMEM)
in_hbm = functools.partial(pltpu.with_memory_space_constraint, memory_space=pltpu.HBM)
vmem_array = pltpu.VMEM
P_ROWS, Q_ROWS = 128, 64


def pack_kernel(
    plasma_ref, rhs_ref, blocks_ref, res_ref,
    t0_ref, bulk_ref, edge_ref, side_ref, own_ref, scr_p, scr_q, blocks_in, res_in, state_in, rhs_in, sems,
):
    copies = [
        pltpu.make_async_copy(rhs_ref, rhs_in, sems.at[0]),
        pltpu.make_async_copy(plasma_ref, state_in, sems.at[1]),
        pltpu.make_async_copy(res_ref, res_in, sems.at[2]),
    ] + [pltpu.make_async_copy(blocks_ref.at[a], blocks_in.at[a], sems.at[3 + a]) for a in range(6)]
    for copy in copies:
        copy.start()
    for copy in copies[:3]:
        copy.wait()
    plasma_ref, rhs_ref, res_ref, blocks_ref = state_in, rhs_in, res_in, blocks_in
    vector = [rhs_ref[b] for b in range(6)]
    t0 = []
    for a in range(6):
        copies[3 + a].wait()
        total = blocks_ref[a, 0] * vector[0]
        for b in range(1, 6):
            total = total + blocks_ref[a, b] * vector[b]
        t0_ref[a] = total
        t0.append(total)
    state = [plasma_ref[a] for a in range(6)]
    deep = t0 + state
    wide = [blocks_ref[i // 6, i % 6] for i in range(36)] + [res_ref[...]]
    for f, value in enumerate(wide + state + vector):
        own_ref[f] = value
    fields = wide[:36] + deep + [wide[36], wide[36]]
    for g in range(25):
        pair = jnp.concatenate([fields[2 * g], fields[2 * g + 1]], axis=0)
        bulk_ref[pl.ds(16 * g, 16), :] = pair.astype(BF16)
    zeros = jnp.zeros((8, deep[0].shape[1]), F32)
    for side in range(2):
        scr_p[pl.ds(P_ROWS - 8, 8), :] = zeros
        scr_q[pl.ds(Q_ROWS - 8, 8), :] = zeros
        for f, value in enumerate(deep):
            scr_p[pl.ds(4 * f, 4), :] = value[0:4] if side == 0 else value[4:8]
            scr_q[pl.ds(2 * f, 2), :] = value[0:2] if side == 0 else value[6:8]
        for f, value in enumerate(wide):
            scr_p[pl.ds(48 + 2 * f, 2), :] = value[0:2] if side == 0 else value[6:8]
            scr_q[pl.ds(24 + f, 1), :] = value[0:1] if side == 0 else value[7:8]
        side_ref[side] = scr_p[...].astype(BF16)
        edge_ref[side] = scr_q[...].astype(BF16)


def unpack_kernel(bulk_ref, other_ref):
    for g in range(25):
        pair = bulk_ref[pl.ds(16 * g, 16), :].astype(F32)
        other_ref[2 * g] = pair[0:8]
        other_ref[2 * g + 1] = pair[8:16]


def krylov_kernel(
    own_ref, t0_ref, other_ref, outer_ref, core_ref,
    gram_ref, t_ref, up, down, blk_p, blk_q, st_p, st_q, res_s,
):
    width = own_ref.shape[-1]
    even = lax.axis_index("pol") % 2 == 0
    from_outer, from_core = outer_ref[...].astype(F32), core_ref[...].astype(F32)
    up[...] = jnp.where(even, from_outer, from_core)
    down[...] = jnp.where(even, from_core, from_outer)
    zeros = jnp.zeros((8, width), F32)

    def halo(ref, at, offset, rows):
        if rows < 4:
            ref[at, 8:16] = zeros
        ref[at, 8 : 8 + rows] = down[pl.ds(offset, rows), :]
        ref[at, 16 - rows : 16] = up[pl.ds(offset, rows), :]

    def other(field):
        return other_ref[field]

    for i in range(36):
        blk_p[i, 0:8] = own_ref[i]
        halo(blk_p, i, 48 + 2 * i, 2)
        blk_q[i, 0:8] = other(i)
        halo(blk_q, i, P_ROWS + 24 + i, 1)
    for i in range(12):
        st_p[i, 0:8] = t0_ref[i] if i < 6 else own_ref[31 + i]
        halo(st_p, i, 4 * i, 4)
        st_q[i, 0:8] = other(36 + i)
        halo(st_q, i, P_ROWS + 2 * i, 2)
    res_s[0, 0:8] = own_ref[36]
    halo(res_s, 0, 120, 2)
    res_s[1, 0:8] = other(48)
    halo(res_s, 1, P_ROWS + 60, 1)

    def lane(shape):
        return lax.broadcasted_iota(jnp.int32, shape, 1)

    def depth_next(x):
        return jnp.where(lane(x.shape) == width - 1, 0.0, pltpu.roll(x, width - 1, 1))

    def depth_prev(x):
        return jnp.where(lane(x.shape) == 0, 0.0, pltpu.roll(x, 1, 1))

    def jacobian(plasma, tangent, plasma_next, tangent_next, plasma_prev, tangent_prev, res, rows):
        flux_next = linear_flux(plasma_next, tangent_next, 0)
        flux_prev = linear_flux(plasma_prev, tangent_prev, 0)
        flux_rows = linear_flux(plasma, tangent, 1)
        own = [x[0:rows] for x in tangent]
        flux_depth = linear_flux([x[0:rows] for x in plasma], own, 2)
        out = []
        for i in range(6):
            total = inverse_step * own[i] + 0.5 * (flux_next[i][0:rows] - flux_prev[i][0:rows])
            laplace = tangent_next[i][0:rows] + tangent_prev[i][0:rows] - 2.0 * own[i]
            total = total + 0.5 * (
                pltpu.roll(flux_rows[i], 15, 0)[0:rows] - pltpu.roll(flux_rows[i], 1, 0)[0:rows]
            )
            laplace = laplace + (
                pltpu.roll(tangent[i], 15, 0)[0:rows] + pltpu.roll(tangent[i], 1, 0)[0:rows] - 2.0 * own[i]
            )
            total = total + 0.5 * (depth_next(flux_depth[i]) - depth_prev(flux_depth[i]))
            laplace = laplace + (depth_next(own[i]) + depth_prev(own[i]) - 2.0 * own[i])
            out.append(total - (res[0:rows] if i < 3 else viscosity) * laplace)
        return out

    def precondition(ref, vector, rows):
        out = []
        for a in range(6):
            total = ref[6 * a, 0:rows] * vector[0]
            for b in range(1, 6):
                total = total + ref[6 * a + b, 0:rows] * vector[b]
            out.append(total)
        return out

    plasma_p = [st_p[6 + i] for i in range(6)]
    plasma_q = [st_q[6 + i] for i in range(6)]
    half_p = [x[0:8] for x in plasma_p]
    half_q = [x[0:8] for x in plasma_q]
    krylov = [[own_ref[43 + i] for i in range(6)]]
    tang_p = [st_p[i] for i in range(6)]
    tang_q = [st_q[i] for i in range(6)]
    for i in range(6):
        t_ref[i] = t0_ref[i]

    image_p = jacobian(plasma_p, tang_p, plasma_q, tang_q, plasma_q, tang_q, res_s[0], 16)
    image_q = jacobian(plasma_q, tang_q, plasma_p, tang_p, plasma_p, tang_p, res_s[1], 16)
    krylov.append([image_p[i][0:8] - SHIFTS[0] * krylov[0][i] for i in range(6)])
    next_p = [x - SHIFTS[0] * t for x, t in zip(precondition(blk_p, image_p, 16), tang_p)]
    next_q = [x - SHIFTS[0] * t for x, t in zip(precondition(blk_q, image_q, 16), tang_q)]
    for i in range(6):
        t_ref[6 + i] = next_p[i][0:8]

    image_p = jacobian(plasma_p, next_p, plasma_q, next_q, plasma_q, next_q, res_s[0], 16)
    image_q = jacobian(plasma_q, next_q, half_p, [x[0:8] for x in next_p], half_p, [x[0:8] for x in next_p], res_s[1], 8)
    krylov.append([image_p[i][0:8] - SHIFTS[1] * krylov[1][i] for i in range(6)])
    last_p = [x - SHIFTS[1] * t for x, t in zip(precondition(blk_p, image_p, 16), next_p)]
    last_q = [x - SHIFTS[1] * t[0:8] for x, t in zip(precondition(blk_q, image_q, 8), next_q)]
    for i in range(6):
        t_ref[12 + i] = last_p[i][0:8]

    image_p = jacobian(plasma_p, last_p, half_q, last_q, half_q, last_q, res_s[0], 8)
    krylov.append([image_p[i] - SHIFTS[2] * krylov[2][i] for i in range(6)])

    out = jnp.zeros((1, 128), F32)
    lanes = lax.broadcasted_iota(jnp.int32, (1, 128), 1)
    for k, (i, j) in enumerate(PAIRS):
        total = krylov[i][0] * krylov[j][0]
        for f in range(1, 6):
            total = total + krylov[i][f] * krylov[j][f]
        total = jnp.sum(jnp.sum(total, axis=0, keepdims=True), axis=1, keepdims=True)
        out = jnp.where(lanes == k, total, out)
    gram_ref[...] = jnp.broadcast_to(out[None], gram_ref.shape)


def finish_kernel(inverse_root, gram_ref, t_ref, update_ref, estimates_ref):
    gathered = gram_ref[...]
    sums = jnp.sum(gathered, axis=0)
    lanes = lax.broadcasted_iota(jnp.int32, sums.shape, 1)
    gram = {}
    for k, pair in enumerate(PAIRS):
        gram[pair] = jnp.sum(jnp.where(lanes == k, sums, 0.0), axis=1, keepdims=True)
    factors, estimate_list = solve_from_gram(gram)
    width = update_ref.shape[-1]
    wide = [jnp.broadcast_to(f, (8, width)) for f in factors]
    for i in range(6):
        update_ref[i] = wide[0] * t_ref[i] + wide[1] * t_ref[6 + i] + wide[2] * t_ref[12 + i]
    for k, value in enumerate(estimate_list):
        estimates_ref[k] = jnp.sum(value * inverse_root)


def two_planes(pol, plasma_state, right_side, resistivity, jacobi_blocks):
    rows, width = plasma_state.shape[2], plasma_state.shape[3]
    count = 2 * pol

    def pairs(partner):
        out = []
        for t in range(2):
            for p in range(pol):
                other = partner(t, p)
                if 0 <= other[1] < pol:
                    out.append((t * pol + p, other[0] * pol + other[1]))
        return out

    across = pairs(lambda t, p: (1 - t, p))
    core = pairs(lambda t, p: (t, p ^ 1))
    outer = pairs(lambda t, p: (t, p - 1 if p % 2 == 0 else p + 1))

    plasma = plasma_state.reshape(6, rows, width)
    rhs = right_side.reshape(6, rows, width)
    res = resistivity.reshape(rows, width)
    blocks = jacobi_blocks.reshape(6, 6, rows, width)
    vmem = pl.BlockSpec(memory_space=pltpu.VMEM)
    shape = jax.ShapeDtypeStruct
    t0, bulk, edge, side, own = pl.pallas_call(
        pack_kernel,
        out_shape=(
            vmem_array((6, rows, width), F32),
            vmem_array((400, width), BF16),
            vmem_array((2, Q_ROWS, width), BF16),
            vmem_array((2, P_ROWS, width), BF16),
            vmem_array((49, rows, width), F32),
        ),
        in_specs=[pl.BlockSpec(memory_space=pltpu.HBM)] * 4,
        out_specs=(vmem,) * 5,
        scratch_shapes=[
            pltpu.VMEM((P_ROWS, width), F32),
            pltpu.VMEM((Q_ROWS, width), F32),
            pltpu.VMEM((6, 6, rows, width), F32),
            pltpu.VMEM((rows, width), F32),
            pltpu.VMEM((6, rows, width), F32),
            pltpu.VMEM((6, rows, width), F32),
            pltpu.SemaphoreType.DMA((9,)),
        ],
    )(*map(in_hbm, (plasma, rhs, blocks, res)))
    edge = lax.ppermute(edge, AXES, across)
    bulk = lax.ppermute(bulk, AXES, across)
    even = lax.axis_index("pol") % 2 == 0
    both = jnp.concatenate([side, edge], axis=1)
    from_core = lax.ppermute(jnp.where(even, both[1], both[0]), AXES, core)
    from_outer = lax.ppermute(jnp.where(even, both[0], both[1]), AXES, outer)
    other = pl.pallas_call(
        unpack_kernel, out_shape=vmem_array((50, rows, width), F32), in_specs=[vmem], out_specs=vmem
    )(in_vmem(bulk))
    slab = P_ROWS + Q_ROWS
    gram, tangents = pl.pallas_call(
        krylov_kernel,
        out_shape=(vmem_array((count, 1, 128), F32), vmem_array((18, rows, width), F32)),
        in_specs=[vmem] * 5,
        out_specs=(vmem,) * 2,
        scratch_shapes=[
            pltpu.VMEM((slab, width), F32),
            pltpu.VMEM((slab, width), F32),
            pltpu.VMEM((36, 16, width), F32),
            pltpu.VMEM((36, 16, width), F32),
            pltpu.VMEM((12, 16, width), F32),
            pltpu.VMEM((12, 16, width), F32),
            pltpu.VMEM((2, 16, width), F32),
        ],
    )(*map(in_vmem, (own, t0, other, from_outer, from_core)))
    gram = lax.all_to_all(gram, AXES, 0, 0, tiled=True)
    inverse_root = float((6.0 * count * rows * width) ** -0.5)
    update, estimates = pl.pallas_call(
        functools.partial(finish_kernel, inverse_root),
        out_shape=(shape((6, rows, width), F32), shape((ITERS,), F32)),
        in_specs=[vmem] * 2,
        out_specs=(vmem, pl.BlockSpec(memory_space=pltpu.SMEM)),
    )(in_vmem(gram), in_vmem(tangents))
    return update.reshape(plasma_state.shape), estimates


def padded(cells, axis, dim, closed):
    count = lax.axis_size(axis)
    ends = count if closed else count - 1
    size = cells.shape[dim]
    head = lax.slice_in_dim(cells, 0, 1, axis=dim)
    tail = lax.slice_in_dim(cells, size - 1, size, axis=dim)
    before = lax.ppermute(tail, axis, [(i, (i + 1) % count) for i in range(ends)])
    after = lax.ppermute(head, axis, [((i + 1) % count, i) for i in range(ends)])
    return jnp.concatenate([before, cells, after], axis=dim)


def any_planes(plasma_state, right_side, resistivity, jacobi_blocks):
    cell_count = right_side.size * lax.axis_size("tor") * lax.axis_size("pol")
    fixed = jnp.full((3,) + resistivity.shape, viscosity, F32)
    diffusion = jnp.concatenate([jnp.broadcast_to(resistivity[None], fixed.shape), fixed])

    def around(cells):
        planes = padded(cells.astype(BF16), "tor", 1, True).astype(F32)
        planes = jnp.concatenate([planes[:, :1], cells, planes[:, -1:]], axis=1)
        deep = jnp.pad(cells, ((0, 0), (0, 0), (0, 0), (1, 1)))
        return planes, padded(cells, "pol", 2, False), deep

    plasma_around = around(plasma_state)
    vectors, tangents = [right_side], []
    for shift in SHIFTS:
        vector = vectors[-1]
        tangent = jnp.sum(jacobi_blocks * vector[None], axis=1)
        tangents.append(tangent)
        image = inverse_step * tangent
        laplace = jnp.zeros_like(tangent)
        for direction, (plasma, cells) in enumerate(zip(plasma_around, around(tangent))):
            dim = direction + 1
            flux = jnp.stack(linear_flux(plasma, cells, direction))
            size = cells.shape[dim]
            part = functools.partial(lax.slice_in_dim, axis=dim)
            image = image + 0.5 * (part(flux, 2, size) - part(flux, 0, size - 2))
            laplace = laplace + part(cells, 2, size) + part(cells, 0, size - 2) - 2.0 * tangent
        vectors.append(image - diffusion * laplace - shift * vector)
    local = jnp.stack([jnp.sum(vectors[i] * vectors[j]) for i, j in PAIRS])
    gram = lax.psum(local, AXES)
    factors, estimate_list = solve_from_gram({pair: gram[k] for k, pair in enumerate(PAIRS)})
    update = sum(factor * tangent for factor, tangent in zip(factors, tangents))
    return update, jnp.stack(estimate_list) / jnp.sqrt(F32(cell_count))


def solution(mesh):
    tor, pol = mesh.shape["tor"], mesh.shape["pol"]

    def shards(plasma_state, right_side, resistivity, jacobi_blocks):
        _, planes, rows, width = plasma_state.shape
        fast = tor == 2 and planes == 1 and pol % 2 == 0 and rows == 8 and width % 128 == 0
        if fast:
            return two_planes(pol, plasma_state, right_side, resistivity, jacobi_blocks)
        return any_planes(plasma_state, right_side, resistivity, jacobi_blocks)

    return jax.shard_map(
        shards,
        mesh=mesh,
        in_specs=(
            P(None, "tor", "pol", None),
            P(None, "tor", "pol", None),
            P("tor", "pol", None),
            P(None, None, "tor", "pol", None),
        ),
        out_specs=(P(None, "tor", "pol", None), P()),
        check_vma=False,
    )
```

```python
import functools

import jax
import jax.numpy as jnp
from jax import lax
from jax.experimental import pallas as pl
from jax.experimental.pallas import tpu as pltpu
from jax.sharding import PartitionSpec as P

ITERS = 3
SHIFTS = (1.0, 2.0, 3.0)
inverse_step = 1.0
viscosity = 0.2
epsilon = 1e-06
AXES = ("tor", "pol")
PAIRS = [(i, j) for i in range(ITERS + 1) for j in range(i, ITERS + 1)]
BF16 = jnp.bfloat16
F32 = jnp.float32


def linear_flux(plasma, tangent, direction):
    magnetic, velocity = plasma[0:3], plasma[3:6]
    tang_mag, tang_vel = tangent[0:3], tangent[3:6]
    pressure = magnetic[0] * tang_mag[0] + magnetic[1] * tang_mag[1] + magnetic[2] * tang_mag[2]
    components = []
    for i in range(3):
        components.append(
            tang_vel[direction] * magnetic[i]
            + velocity[direction] * tang_mag[i]
            - tang_mag[direction] * velocity[i]
            - magnetic[direction] * tang_vel[i]
        )
    for i in range(3):
        moment = (
            tang_vel[direction] * velocity[i]
            + velocity[direction] * tang_vel[i]
            - tang_mag[direction] * magnetic[i]
            - magnetic[direction] * tang_mag[i]
        )
        if i == direction:
            moment = moment + pressure
        components.append(moment)
    return components


def least_squares(columns, initial_norm):
    count = len(columns)
    rhs_list = [initial_norm] + [None] * count
    cosines = []
    sines = []
    triangle = []
    estimate_list = []
    for column in range(count):
        entries = list(columns[column])
        for i in range(column):
            first_value, second_value = entries[i], entries[i + 1]
            entries[i] = cosines[i] * first_value + sines[i] * second_value
            entries[i + 1] = -sines[i] * first_value + cosines[i] * second_value
        first_value, second_value = entries[column], entries[column + 1]
        radius = jnp.sqrt(first_value * first_value + second_value * second_value)
        cosine = first_value / radius
        sine_value = second_value / radius
        cosines.append(cosine)
        sines.append(sine_value)
        entries[column] = radius
        triangle.append(entries[: column + 1])
        previous = rhs_list[column]
        rhs_list[column] = cosine * previous
        rhs_list[column + 1] = -sine_value * previous
        estimate_list.append(jnp.abs(rhs_list[column + 1]))
    weights = [None] * count
    for column in reversed(range(count)):
        partial_value = rhs_list[column]
        for later in range(column + 1, count):
            partial_value = partial_value - triangle[later][column] * weights[later]
        weights[column] = partial_value / triangle[column][column]
    return weights, estimate_list


def solve_from_gram(gram):
    count = ITERS + 1

    def inner(left, right):
        total = None
        for i in range(count):
            row = None
            for j in range(count):
                if right[j] is None:
                    continue
                term = gram[(min(i, j), max(i, j))] * right[j]
                row = term if row is None else row + term
            if left[i] is None or row is None:
                continue
            term = left[i] * row
            total = term if total is None else total + term
        return total

    def minus(left, factor, right):
        out = []
        for a, b in zip(left, right):
            if b is None:
                out.append(a)
            else:
                out.append(a - factor * b)
        return out

    initial_norm = jnp.sqrt(gram[(0, 0)] + epsilon)
    basis = [[1.0 / initial_norm] + [None] * ITERS]
    columns = []
    for column in range(ITERS):
        vector = basis[column]
        image = []
        for i in range(count):
            entry = None
            if vector[i] is not None:
                entry = SHIFTS[i] * vector[i]
            if i > 0 and vector[i - 1] is not None:
                entry = vector[i - 1] if entry is None else entry + vector[i - 1]
            image.append(entry)
        coefficients = [inner(earlier, image) for earlier in basis]
        remainder = image
        for coefficient, earlier in zip(coefficients, basis):
            remainder = minus(remainder, coefficient, earlier)
        square = jnp.maximum(inner(remainder, remainder), 0.0)
        new_norm = jnp.sqrt(square + epsilon)
        columns.append(coefficients + [new_norm])
        if column + 1 < ITERS:
            scale = 1.0 / new_norm
            basis.append([None if r is None else r * scale for r in remainder])
    weights, estimate_list = least_squares(columns, initial_norm)
    factors = []
    for k in range(ITERS):
        total = None
        for weight, vector in zip(weights, basis):
            if vector[k] is not None:
                term = weight * vector[k]
                total = term if total is None else total + term
        factors.append(total)
    return factors, estimate_list


in_vmem = functools.partial(pltpu.with_memory_space_constraint, memory_space=pltpu.VMEM)
in_hbm = functools.partial(pltpu.with_memory_space_constraint, memory_space=pltpu.HBM)
vmem_array = pltpu.VMEM
P_ROWS, Q_ROWS = 128, 64


def tile_rows(value, count, first):
    return jnp.where(first, value[0:count], value[8 - count : 8])


def fill_slab_q(scr, deep, wide, first):
    scr[pl.ds(Q_ROWS - 8, 8), :] = jnp.zeros((8, deep[0].shape[1]), F32)
    for f, value in enumerate(deep):
        scr[pl.ds(2 * f, 2), :] = tile_rows(value, 2, first)
    for f, value in enumerate(wide):
        scr[pl.ds(24 + f, 1), :] = tile_rows(value, 1, first)
    return scr[...].astype(BF16)


def fill_slab_p(scr, deep, wide, first):
    scr[pl.ds(P_ROWS - 8, 8), :] = jnp.zeros((8, deep[0].shape[1]), F32)
    for f, value in enumerate(deep):
        scr[pl.ds(4 * f, 4), :] = tile_rows(value, 4, first)
    for f, value in enumerate(wide):
        scr[pl.ds(48 + 2 * f, 2), :] = tile_rows(value, 2, first)
    return scr[...].astype(BF16)


def first_kernel(
    plasma_hbm, rhs_hbm, blocks_hbm, res_hbm,
    t0_ref, own_ref, edge_ref, scr, sems,
):
    copies = [
        pltpu.make_async_copy(rhs_hbm, own_ref.at[pl.ds(43, 6)], sems.at[0]),
        pltpu.make_async_copy(plasma_hbm, own_ref.at[pl.ds(37, 6)], sems.at[1]),
        pltpu.make_async_copy(res_hbm, own_ref.at[pl.ds(36, 1)], sems.at[2]),
    ] + [pltpu.make_async_copy(blocks_hbm.at[a], own_ref.at[pl.ds(6 * a, 6)], sems.at[3 + a]) for a in range(6)]
    for copy in copies:
        copy.start()
    even = lax.axis_index("pol") % 2 == 0
    for copy in copies[:3]:
        copy.wait()
    vector = [own_ref[43 + b] for b in range(6)]
    t0 = []
    for a in range(6):
        copies[3 + a].wait()
        total = own_ref[6 * a] * vector[0]
        for b in range(1, 6):
            total = total + own_ref[6 * a + b] * vector[b]
        t0_ref[a] = total
        t0.append(total)
    deep = t0 + [own_ref[37 + i] for i in range(6)]
    wide = [own_ref[i] for i in range(37)]
    edge_ref[...] = fill_slab_q(scr, deep, wide, even)


def pack_kernel(t0_ref, own_ref, bulk_ref, side_ref, core_ref, scr):
    even = lax.axis_index("pol") % 2 == 0
    deep = [t0_ref[i] for i in range(6)] + [own_ref[37 + i] for i in range(6)]
    wide = [own_ref[i] for i in range(37)]
    fields = wide[:36] + deep + [wide[36], wide[36]]
    for g in range(25):
        pair = jnp.concatenate([fields[2 * g], fields[2 * g + 1]], axis=0)
        bulk_ref[pl.ds(16 * g, 16), :] = pair.astype(BF16)
    side_ref[...] = fill_slab_p(scr, deep, wide, even)
    core_ref[...] = fill_slab_p(scr, deep, wide, jnp.logical_not(even))


def join_kernel(side_ref, edge_ref, slab_ref):
    slab_ref[pl.ds(0, P_ROWS), :] = side_ref[...]
    slab_ref[pl.ds(P_ROWS, Q_ROWS), :] = edge_ref[...]


def unpack_kernel(bulk_ref, core_ref, other_ref, slab_ref, scr):
    odd = lax.axis_index("pol") % 2 == 1
    for g in range(25):
        pair = bulk_ref[pl.ds(16 * g, 16), :].astype(F32)
        other_ref[2 * g] = pair[0:8]
        other_ref[2 * g + 1] = pair[8:16]
    deep = [other_ref[36 + i] for i in range(12)]
    wide = [other_ref[i] for i in range(36)] + [other_ref[48]]
    slab_ref[pl.ds(0, P_ROWS), :] = core_ref[...]
    slab_ref[pl.ds(P_ROWS, Q_ROWS), :] = fill_slab_q(scr, deep, wide, odd)


def krylov_kernel(
    own_ref, t0_ref, other_ref, outer_ref, core_ref,
    gram_ref, t_ref, up, down, blk_p, blk_q, st_p, st_q, res_s,
):
    width = own_ref.shape[-1]
    even = lax.axis_index("pol") % 2 == 0
    from_outer, from_core = outer_ref[...].astype(F32), core_ref[...].astype(F32)
    up[...] = jnp.where(even, from_outer, from_core)
    down[...] = jnp.where(even, from_core, from_outer)
    zeros = jnp.zeros((8, width), F32)

    def halo(ref, at, offset, rows):
        if rows < 4:
            ref[at, 8:16] = zeros
        ref[at, 8 : 8 + rows] = down[pl.ds(offset, rows), :]
        ref[at, 16 - rows : 16] = up[pl.ds(offset, rows), :]

    def other(field):
        return other_ref[field]

    for i in range(36):
        blk_p[i, 0:8] = own_ref[i]
        halo(blk_p, i, 48 + 2 * i, 2)
        blk_q[i, 0:8] = other(i)
        halo(blk_q, i, P_ROWS + 24 + i, 1)
    for i in range(12):
        st_p[i, 0:8] = t0_ref[i] if i < 6 else own_ref[31 + i]
        halo(st_p, i, 4 * i, 4)
        st_q[i, 0:8] = other(36 + i)
        halo(st_q, i, P_ROWS + 2 * i, 2)
    res_s[0, 0:8] = own_ref[36]
    halo(res_s, 0, 120, 2)
    res_s[1, 0:8] = other(48)
    halo(res_s, 1, P_ROWS + 60, 1)

    def lane(shape):
        return lax.broadcasted_iota(jnp.int32, shape, 1)

    def depth_next(x):
        return jnp.where(lane(x.shape) == width - 1, 0.0, pltpu.roll(x, width - 1, 1))

    def depth_prev(x):
        return jnp.where(lane(x.shape) == 0, 0.0, pltpu.roll(x, 1, 1))

    def jacobian(plasma, tangent, plasma_next, tangent_next, plasma_prev, tangent_prev, res, rows):
        flux_next = linear_flux(plasma_next, tangent_next, 0)
        flux_prev = linear_flux(plasma_prev, tangent_prev, 0)
        flux_rows = linear_flux(plasma, tangent, 1)
        own = [x[0:rows] for x in tangent]
        flux_depth = linear_flux([x[0:rows] for x in plasma], own, 2)
        out = []
        for i in range(6):
            total = inverse_step * own[i] + 0.5 * (flux_next[i][0:rows] - flux_prev[i][0:rows])
            laplace = tangent_next[i][0:rows] + tangent_prev[i][0:rows] - 2.0 * own[i]
            total = total + 0.5 * (
                pltpu.roll(flux_rows[i], 15, 0)[0:rows] - pltpu.roll(flux_rows[i], 1, 0)[0:rows]
            )
            laplace = laplace + (
                pltpu.roll(tangent[i], 15, 0)[0:rows] + pltpu.roll(tangent[i], 1, 0)[0:rows] - 2.0 * own[i]
            )
            total = total + 0.5 * (depth_next(flux_depth[i]) - depth_prev(flux_depth[i]))
            laplace = laplace + (depth_next(own[i]) + depth_prev(own[i]) - 2.0 * own[i])
            out.append(total - (res[0:rows] if i < 3 else viscosity) * laplace)
        return out

    def precondition(ref, vector, rows):
        out = []
        for a in range(6):
            total = ref[6 * a, 0:rows] * vector[0]
            for b in range(1, 6):
                total = total + ref[6 * a + b, 0:rows] * vector[b]
            out.append(total)
        return out

    plasma_p = [st_p[6 + i] for i in range(6)]
    plasma_q = [st_q[6 + i] for i in range(6)]
    half_p = [x[0:8] for x in plasma_p]
    half_q = [x[0:8] for x in plasma_q]
    krylov = [[own_ref[43 + i] for i in range(6)]]
    tang_p = [st_p[i] for i in range(6)]
    tang_q = [st_q[i] for i in range(6)]
    for i in range(6):
        t_ref[i] = t0_ref[i]

    image_p = jacobian(plasma_p, tang_p, plasma_q, tang_q, plasma_q, tang_q, res_s[0], 16)
    image_q = jacobian(plasma_q, tang_q, plasma_p, tang_p, plasma_p, tang_p, res_s[1], 16)
    krylov.append([image_p[i][0:8] - SHIFTS[0] * krylov[0][i] for i in range(6)])
    next_p = [x - SHIFTS[0] * t for x, t in zip(precondition(blk_p, image_p, 16), tang_p)]
    next_q = [x - SHIFTS[0] * t for x, t in zip(precondition(blk_q, image_q, 16), tang_q)]
    for i in range(6):
        t_ref[6 + i] = next_p[i][0:8]

    image_p = jacobian(plasma_p, next_p, plasma_q, next_q, plasma_q, next_q, res_s[0], 16)
    image_q = jacobian(plasma_q, next_q, half_p, [x[0:8] for x in next_p], half_p, [x[0:8] for x in next_p], res_s[1], 8)
    krylov.append([image_p[i][0:8] - SHIFTS[1] * krylov[1][i] for i in range(6)])
    last_p = [x - SHIFTS[1] * t for x, t in zip(precondition(blk_p, image_p, 16), next_p)]
    last_q = [x - SHIFTS[1] * t[0:8] for x, t in zip(precondition(blk_q, image_q, 8), next_q)]
    for i in range(6):
        t_ref[12 + i] = last_p[i][0:8]

    image_p = jacobian(plasma_p, last_p, half_q, last_q, half_q, last_q, res_s[0], 8)
    krylov.append([image_p[i] - SHIFTS[2] * krylov[2][i] for i in range(6)])

    out = jnp.zeros((1, 128), F32)
    lanes = lax.broadcasted_iota(jnp.int32, (1, 128), 1)
    for k, (i, j) in enumerate(PAIRS):
        total = krylov[i][0] * krylov[j][0]
        for f in range(1, 6):
            total = total + krylov[i][f] * krylov[j][f]
        total = jnp.sum(jnp.sum(total, axis=0, keepdims=True), axis=1, keepdims=True)
        out = jnp.where(lanes == k, total, out)
    gram_ref[...] = jnp.broadcast_to(out[None], gram_ref.shape)


def finish_kernel(inverse_root, gram_ref, t_ref, update_ref, estimates_ref):
    gathered = gram_ref[...]
    sums = jnp.sum(gathered, axis=0)
    lanes = lax.broadcasted_iota(jnp.int32, sums.shape, 1)
    gram = {}
    for k, pair in enumerate(PAIRS):
        gram[pair] = jnp.sum(jnp.where(lanes == k, sums, 0.0), axis=1, keepdims=True)
    factors, estimate_list = solve_from_gram(gram)
    width = update_ref.shape[-1]
    wide = [jnp.broadcast_to(f, (8, width)) for f in factors]
    for i in range(6):
        update_ref[i] = wide[0] * t_ref[i] + wide[1] * t_ref[6 + i] + wide[2] * t_ref[12 + i]
    for k, value in enumerate(estimate_list):
        estimates_ref[k] = jnp.sum(value * inverse_root)


def two_planes(pol, plasma_state, right_side, resistivity, jacobi_blocks):
    rows, width = plasma_state.shape[2], plasma_state.shape[3]
    count = 2 * pol

    def pairs(partner):
        out = []
        for t in range(2):
            for p in range(pol):
                other = partner(t, p)
                if 0 <= other[1] < pol:
                    out.append((t * pol + p, other[0] * pol + other[1]))
        return out

    across = pairs(lambda t, p: (1 - t, p))
    core = pairs(lambda t, p: (t, p ^ 1))
    outer = pairs(lambda t, p: (t, p - 1 if p % 2 == 0 else p + 1))

    plasma = plasma_state.reshape(6, rows, width)
    rhs = right_side.reshape(6, rows, width)
    res = resistivity.reshape(1, rows, width)
    blocks = jacobi_blocks.reshape(6, 6, rows, width)
    slab = P_ROWS + Q_ROWS
    vmem = pl.BlockSpec(memory_space=pltpu.VMEM)
    shape = jax.ShapeDtypeStruct
    t0, own, edge = pl.pallas_call(
        first_kernel,
        out_shape=(
            vmem_array((6, rows, width), F32),
            vmem_array((49, rows, width), F32),
            vmem_array((Q_ROWS, width), BF16),
        ),
        in_specs=[pl.BlockSpec(memory_space=pltpu.HBM)] * 4,
        out_specs=(vmem,) * 3,
        scratch_shapes=[pltpu.VMEM((Q_ROWS, width), F32), pltpu.SemaphoreType.DMA((9,))],
    )(*map(in_hbm, (plasma, rhs, blocks, res)))
    edge = lax.ppermute(edge, AXES, across)
    bulk, side, core_side = pl.pallas_call(
        pack_kernel,
        out_shape=(
            vmem_array((400, width), BF16),
            vmem_array((P_ROWS, width), BF16),
            vmem_array((P_ROWS, width), BF16),
        ),
        in_specs=[vmem] * 2,
        out_specs=(vmem,) * 3,
        scratch_shapes=[pltpu.VMEM((P_ROWS, width), F32)],
    )(in_vmem(t0), in_vmem(own))
    bulk = lax.ppermute(bulk, AXES, across)
    outer_slab = pl.pallas_call(
        join_kernel,
        out_shape=vmem_array((slab, width), BF16),
        in_specs=[vmem] * 2,
        out_specs=vmem,
        cost_estimate=pl.CostEstimate(flops=100_000_000_000, bytes_accessed=1_000_000, transcendentals=0),
    )(in_vmem(side), in_vmem(edge))
    from_outer = lax.ppermute(outer_slab, AXES, outer)
    other, core_slab = pl.pallas_call(
        unpack_kernel,
        out_shape=(vmem_array((50, rows, width), F32), vmem_array((slab, width), BF16)),
        in_specs=[vmem] * 2,
        out_specs=(vmem,) * 2,
        scratch_shapes=[pltpu.VMEM((Q_ROWS, width), F32)],
    )(in_vmem(bulk), in_vmem(core_side))
    from_core = lax.ppermute(core_slab, AXES, core)
    gram, tangents = pl.pallas_call(
        krylov_kernel,
        out_shape=(vmem_array((count, 1, 128), F32), vmem_array((18, rows, width), F32)),
        in_specs=[vmem] * 5,
        out_specs=(vmem,) * 2,
        scratch_shapes=[
            pltpu.VMEM((slab, width), F32),
            pltpu.VMEM((slab, width), F32),
            pltpu.VMEM((36, 16, width), F32),
            pltpu.VMEM((36, 16, width), F32),
            pltpu.VMEM((12, 16, width), F32),
            pltpu.VMEM((12, 16, width), F32),
            pltpu.VMEM((2, 16, width), F32),
        ],
    )(*map(in_vmem, (own, t0, other, from_outer, from_core)))
    gram = lax.all_to_all(gram, AXES, 0, 0, tiled=True)
    inverse_root = float((6.0 * count * rows * width) ** -0.5)
    update, estimates = pl.pallas_call(
        functools.partial(finish_kernel, inverse_root),
        out_shape=(shape((6, rows, width), F32), shape((ITERS,), F32)),
        in_specs=[vmem] * 2,
        out_specs=(vmem, pl.BlockSpec(memory_space=pltpu.SMEM)),
    )(in_vmem(gram), in_vmem(tangents))
    return update.reshape(plasma_state.shape), estimates


def padded(cells, axis, dim, closed):
    count = lax.axis_size(axis)
    ends = count if closed else count - 1
    size = cells.shape[dim]
    head = lax.slice_in_dim(cells, 0, 1, axis=dim)
    tail = lax.slice_in_dim(cells, size - 1, size, axis=dim)
    before = lax.ppermute(tail, axis, [(i, (i + 1) % count) for i in range(ends)])
    after = lax.ppermute(head, axis, [((i + 1) % count, i) for i in range(ends)])
    return jnp.concatenate([before, cells, after], axis=dim)


def any_planes(plasma_state, right_side, resistivity, jacobi_blocks):
    cell_count = right_side.size * lax.axis_size("tor") * lax.axis_size("pol")
    fixed = jnp.full((3,) + resistivity.shape, viscosity, F32)
    diffusion = jnp.concatenate([jnp.broadcast_to(resistivity[None], fixed.shape), fixed])

    def around(cells):
        planes = padded(cells.astype(BF16), "tor", 1, True).astype(F32)
        planes = jnp.concatenate([planes[:, :1], cells, planes[:, -1:]], axis=1)
        deep = jnp.pad(cells, ((0, 0), (0, 0), (0, 0), (1, 1)))
        return planes, padded(cells, "pol", 2, False), deep

    plasma_around = around(plasma_state)
    vectors, tangents = [right_side], []
    for shift in SHIFTS:
        vector = vectors[-1]
        tangent = jnp.sum(jacobi_blocks * vector[None], axis=1)
        tangents.append(tangent)
        image = inverse_step * tangent
        laplace = jnp.zeros_like(tangent)
        for direction, (plasma, cells) in enumerate(zip(plasma_around, around(tangent))):
            dim = direction + 1
            flux = jnp.stack(linear_flux(plasma, cells, direction))
            size = cells.shape[dim]
            part = functools.partial(lax.slice_in_dim, axis=dim)
            image = image + 0.5 * (part(flux, 2, size) - part(flux, 0, size - 2))
            laplace = laplace + part(cells, 2, size) + part(cells, 0, size - 2) - 2.0 * tangent
        vectors.append(image - diffusion * laplace - shift * vector)
    local = jnp.stack([jnp.sum(vectors[i] * vectors[j]) for i, j in PAIRS])
    gram = lax.psum(local, AXES)
    factors, estimate_list = solve_from_gram({pair: gram[k] for k, pair in enumerate(PAIRS)})
    update = sum(factor * tangent for factor, tangent in zip(factors, tangents))
    return update, jnp.stack(estimate_list) / jnp.sqrt(F32(cell_count))


def solution(mesh):
    tor, pol = mesh.shape["tor"], mesh.shape["pol"]

    def shards(plasma_state, right_side, resistivity, jacobi_blocks):
        _, planes, rows, width = plasma_state.shape
        fast = tor == 2 and planes == 1 and pol % 2 == 0 and rows == 8 and width % 128 == 0
        if fast:
            return two_planes(pol, plasma_state, right_side, resistivity, jacobi_blocks)
        return any_planes(plasma_state, right_side, resistivity, jacobi_blocks)

    return jax.shard_map(
        shards,
        mesh=mesh,
        in_specs=(
            P(None, "tor", "pol", None),
            P(None, "tor", "pol", None),
            P("tor", "pol", None),
            P(None, None, "tor", "pol", None),
        ),
        out_specs=(P(None, "tor", "pol", None), P()),
        check_vma=False,
    )
```

```python
import functools

import jax
import jax.numpy as jnp
from jax import lax
from jax.experimental import pallas as pl
from jax.experimental.pallas import tpu as pltpu
from jax.sharding import PartitionSpec as P

ITERS = 3
SHIFTS = (1.0, 2.0, 3.0)
inverse_step = 1.0
viscosity = 0.2
epsilon = 1e-06
AXES = ("tor", "pol")
PAIRS = [(i, j) for i in range(ITERS + 1) for j in range(i, ITERS + 1)]
BF16 = jnp.bfloat16
F32 = jnp.float32


def linear_flux(plasma, tangent, direction):
    magnetic, velocity = plasma[0:3], plasma[3:6]
    tang_mag, tang_vel = tangent[0:3], tangent[3:6]
    pressure = magnetic[0] * tang_mag[0] + magnetic[1] * tang_mag[1] + magnetic[2] * tang_mag[2]
    components = []
    for i in range(3):
        components.append(
            tang_vel[direction] * magnetic[i]
            + velocity[direction] * tang_mag[i]
            - tang_mag[direction] * velocity[i]
            - magnetic[direction] * tang_vel[i]
        )
    for i in range(3):
        moment = (
            tang_vel[direction] * velocity[i]
            + velocity[direction] * tang_vel[i]
            - tang_mag[direction] * magnetic[i]
            - magnetic[direction] * tang_mag[i]
        )
        if i == direction:
            moment = moment + pressure
        components.append(moment)
    return components


def least_squares(columns, initial_norm):
    count = len(columns)
    rhs_list = [initial_norm] + [None] * count
    cosines = []
    sines = []
    triangle = []
    estimate_list = []
    for column in range(count):
        entries = list(columns[column])
        for i in range(column):
            first_value, second_value = entries[i], entries[i + 1]
            entries[i] = cosines[i] * first_value + sines[i] * second_value
            entries[i + 1] = -sines[i] * first_value + cosines[i] * second_value
        first_value, second_value = entries[column], entries[column + 1]
        radius = jnp.sqrt(first_value * first_value + second_value * second_value)
        cosine = first_value / radius
        sine_value = second_value / radius
        cosines.append(cosine)
        sines.append(sine_value)
        entries[column] = radius
        triangle.append(entries[: column + 1])
        previous = rhs_list[column]
        rhs_list[column] = cosine * previous
        rhs_list[column + 1] = -sine_value * previous
        estimate_list.append(jnp.abs(rhs_list[column + 1]))
    weights = [None] * count
    for column in reversed(range(count)):
        partial_value = rhs_list[column]
        for later in range(column + 1, count):
            partial_value = partial_value - triangle[later][column] * weights[later]
        weights[column] = partial_value / triangle[column][column]
    return weights, estimate_list


def solve_from_gram(gram):
    count = ITERS + 1

    def inner(left, right):
        total = None
        for i in range(count):
            row = None
            for j in range(count):
                if right[j] is None:
                    continue
                term = gram[(min(i, j), max(i, j))] * right[j]
                row = term if row is None else row + term
            if left[i] is None or row is None:
                continue
            term = left[i] * row
            total = term if total is None else total + term
        return total

    def minus(left, factor, right):
        out = []
        for a, b in zip(left, right):
            if b is None:
                out.append(a)
            else:
                out.append(a - factor * b)
        return out

    initial_norm = jnp.sqrt(gram[(0, 0)] + epsilon)
    basis = [[1.0 / initial_norm] + [None] * ITERS]
    columns = []
    for column in range(ITERS):
        vector = basis[column]
        image = []
        for i in range(count):
            entry = None
            if vector[i] is not None:
                entry = SHIFTS[i] * vector[i]
            if i > 0 and vector[i - 1] is not None:
                entry = vector[i - 1] if entry is None else entry + vector[i - 1]
            image.append(entry)
        coefficients = [inner(earlier, image) for earlier in basis]
        remainder = image
        for coefficient, earlier in zip(coefficients, basis):
            remainder = minus(remainder, coefficient, earlier)
        square = jnp.maximum(inner(remainder, remainder), 0.0)
        new_norm = jnp.sqrt(square + epsilon)
        columns.append(coefficients + [new_norm])
        if column + 1 < ITERS:
            scale = 1.0 / new_norm
            basis.append([None if r is None else r * scale for r in remainder])
    weights, estimate_list = least_squares(columns, initial_norm)
    factors = []
    for k in range(ITERS):
        total = None
        for weight, vector in zip(weights, basis):
            if vector[k] is not None:
                term = weight * vector[k]
                total = term if total is None else total + term
        factors.append(total)
    return factors, estimate_list


in_vmem = functools.partial(pltpu.with_memory_space_constraint, memory_space=pltpu.VMEM)
in_hbm = functools.partial(pltpu.with_memory_space_constraint, memory_space=pltpu.HBM)
vmem_array = pltpu.VMEM
P_ROWS, Q_ROWS = 128, 64


def tile_rows(value, count, first):
    return jnp.where(first, value[0:count], value[8 - count : 8])


def fill_slab_q(scr, deep, wide, first):
    scr[pl.ds(Q_ROWS - 8, 8), :] = jnp.zeros((8, deep[0].shape[1]), F32)
    for f, value in enumerate(deep):
        scr[pl.ds(2 * f, 2), :] = tile_rows(value, 2, first)
    for f, value in enumerate(wide):
        scr[pl.ds(24 + f, 1), :] = tile_rows(value, 1, first)
    return scr[...].astype(BF16)


def fill_slab_p(scr, deep, wide, first):
    scr[pl.ds(P_ROWS - 8, 8), :] = jnp.zeros((8, deep[0].shape[1]), F32)
    for f, value in enumerate(deep):
        scr[pl.ds(4 * f, 4), :] = tile_rows(value, 4, first)
    for f, value in enumerate(wide):
        scr[pl.ds(48 + 2 * f, 2), :] = tile_rows(value, 2, first)
    return scr[...].astype(BF16)


def first_kernel(
    plasma_hbm, rhs_hbm, blocks_hbm, res_hbm,
    t0_ref, own_ref, edge_ref, scr, sems,
):
    copies = [
        pltpu.make_async_copy(rhs_hbm, own_ref.at[pl.ds(43, 6)], sems.at[0]),
        pltpu.make_async_copy(plasma_hbm, own_ref.at[pl.ds(37, 6)], sems.at[1]),
        pltpu.make_async_copy(res_hbm, own_ref.at[pl.ds(36, 1)], sems.at[2]),
    ] + [pltpu.make_async_copy(blocks_hbm.at[a], own_ref.at[pl.ds(6 * a, 6)], sems.at[3 + a]) for a in range(6)]
    for copy in copies:
        copy.start()
    even = lax.axis_index("pol") % 2 == 0
    for copy in copies[:3]:
        copy.wait()
    vector = [own_ref[43 + b] for b in range(6)]
    t0 = []
    for a in range(6):
        copies[3 + a].wait()
        total = own_ref[6 * a] * vector[0]
        for b in range(1, 6):
            total = total + own_ref[6 * a + b] * vector[b]
        t0_ref[a] = total
        t0.append(total)
    deep = t0 + [own_ref[37 + i] for i in range(6)]
    wide = [own_ref[i] for i in range(37)]
    edge_ref[...] = fill_slab_q(scr, deep, wide, even)


def bulk_kernel(t0_ref, own_ref, after_ref, bulk_ref):
    deep = [t0_ref[i] for i in range(6)] + [own_ref[37 + i] for i in range(6)]
    wide = [own_ref[i] for i in range(37)]
    fields = wide[:36] + deep + [wide[36], wide[36]]
    for g in range(25):
        pair = jnp.concatenate([fields[2 * g], fields[2 * g + 1]], axis=0)
        bulk_ref[pl.ds(16 * g, 16), :] = pair.astype(BF16)


def pack_kernel(t0_ref, own_ref, side_ref, core_ref, scr):
    even = lax.axis_index("pol") % 2 == 0
    deep = [t0_ref[i] for i in range(6)] + [own_ref[37 + i] for i in range(6)]
    wide = [own_ref[i] for i in range(37)]
    side_ref[...] = fill_slab_p(scr, deep, wide, even)
    core_ref[...] = fill_slab_p(scr, deep, wide, jnp.logical_not(even))


def join_kernel(side_ref, edge_ref, slab_ref):
    slab_ref[pl.ds(0, P_ROWS), :] = side_ref[...]
    slab_ref[pl.ds(P_ROWS, Q_ROWS), :] = edge_ref[...]


def unpack_kernel(bulk_ref, other_ref, slab_ref, scr):
    odd = lax.axis_index("pol") % 2 == 1
    for g in range(25):
        pair = bulk_ref[pl.ds(16 * g, 16), :].astype(F32)
        other_ref[2 * g] = pair[0:8]
        other_ref[2 * g + 1] = pair[8:16]
    deep = [other_ref[36 + i] for i in range(12)]
    wide = [other_ref[i] for i in range(36)] + [other_ref[48]]
    slab_ref[...] = fill_slab_q(scr, deep, wide, odd)


def krylov_kernel(
    own_ref, t0_ref, other_ref, outer_ref, core_p_ref, core_q_ref,
    gram_ref, t_ref, up, down, blk_p, blk_q, st_p, st_q, res_s,
):
    width = own_ref.shape[-1]
    even = lax.axis_index("pol") % 2 == 0
    from_outer = outer_ref[...].astype(F32)
    from_core = jnp.concatenate([core_p_ref[...], core_q_ref[...]], axis=0).astype(F32)
    up[...] = jnp.where(even, from_outer, from_core)
    down[...] = jnp.where(even, from_core, from_outer)
    zeros = jnp.zeros((8, width), F32)

    def halo(ref, at, offset, rows):
        if rows < 4:
            ref[at, 8:16] = zeros
        ref[at, 8 : 8 + rows] = down[pl.ds(offset, rows), :]
        ref[at, 16 - rows : 16] = up[pl.ds(offset, rows), :]

    def other(field):
        return other_ref[field]

    for i in range(36):
        blk_p[i, 0:8] = own_ref[i]
        halo(blk_p, i, 48 + 2 * i, 2)
        blk_q[i, 0:8] = other(i)
        halo(blk_q, i, P_ROWS + 24 + i, 1)
    for i in range(12):
        st_p[i, 0:8] = t0_ref[i] if i < 6 else own_ref[31 + i]
        halo(st_p, i, 4 * i, 4)
        st_q[i, 0:8] = other(36 + i)
        halo(st_q, i, P_ROWS + 2 * i, 2)
    res_s[0, 0:8] = own_ref[36]
    halo(res_s, 0, 120, 2)
    res_s[1, 0:8] = other(48)
    halo(res_s, 1, P_ROWS + 60, 1)

    def lane(shape):
        return lax.broadcasted_iota(jnp.int32, shape, 1)

    def depth_next(x):
        return jnp.where(lane(x.shape) == width - 1, 0.0, pltpu.roll(x, width - 1, 1))

    def depth_prev(x):
        return jnp.where(lane(x.shape) == 0, 0.0, pltpu.roll(x, 1, 1))

    def jacobian(plasma, tangent, plasma_next, tangent_next, plasma_prev, tangent_prev, res, rows):
        flux_next = linear_flux(plasma_next, tangent_next, 0)
        flux_prev = linear_flux(plasma_prev, tangent_prev, 0)
        flux_rows = linear_flux(plasma, tangent, 1)
        own = [x[0:rows] for x in tangent]
        flux_depth = linear_flux([x[0:rows] for x in plasma], own, 2)
        out = []
        for i in range(6):
            total = inverse_step * own[i] + 0.5 * (flux_next[i][0:rows] - flux_prev[i][0:rows])
            laplace = tangent_next[i][0:rows] + tangent_prev[i][0:rows] - 2.0 * own[i]
            total = total + 0.5 * (
                pltpu.roll(flux_rows[i], 15, 0)[0:rows] - pltpu.roll(flux_rows[i], 1, 0)[0:rows]
            )
            laplace = laplace + (
                pltpu.roll(tangent[i], 15, 0)[0:rows] + pltpu.roll(tangent[i], 1, 0)[0:rows] - 2.0 * own[i]
            )
            total = total + 0.5 * (depth_next(flux_depth[i]) - depth_prev(flux_depth[i]))
            laplace = laplace + (depth_next(own[i]) + depth_prev(own[i]) - 2.0 * own[i])
            out.append(total - (res[0:rows] if i < 3 else viscosity) * laplace)
        return out

    def precondition(ref, vector, rows):
        out = []
        for a in range(6):
            total = ref[6 * a, 0:rows] * vector[0]
            for b in range(1, 6):
                total = total + ref[6 * a + b, 0:rows] * vector[b]
            out.append(total)
        return out

    plasma_p = [st_p[6 + i] for i in range(6)]
    plasma_q = [st_q[6 + i] for i in range(6)]
    half_p = [x[0:8] for x in plasma_p]
    half_q = [x[0:8] for x in plasma_q]
    krylov = [[own_ref[43 + i] for i in range(6)]]
    tang_p = [st_p[i] for i in range(6)]
    tang_q = [st_q[i] for i in range(6)]
    for i in range(6):
        t_ref[i] = t0_ref[i]

    image_p = jacobian(plasma_p, tang_p, plasma_q, tang_q, plasma_q, tang_q, res_s[0], 16)
    image_q = jacobian(plasma_q, tang_q, plasma_p, tang_p, plasma_p, tang_p, res_s[1], 16)
    krylov.append([image_p[i][0:8] - SHIFTS[0] * krylov[0][i] for i in range(6)])
    next_p = [x - SHIFTS[0] * t for x, t in zip(precondition(blk_p, image_p, 16), tang_p)]
    next_q = [x - SHIFTS[0] * t for x, t in zip(precondition(blk_q, image_q, 16), tang_q)]
    for i in range(6):
        t_ref[6 + i] = next_p[i][0:8]

    image_p = jacobian(plasma_p, next_p, plasma_q, next_q, plasma_q, next_q, res_s[0], 16)
    image_q = jacobian(plasma_q, next_q, half_p, [x[0:8] for x in next_p], half_p, [x[0:8] for x in next_p], res_s[1], 8)
    krylov.append([image_p[i][0:8] - SHIFTS[1] * krylov[1][i] for i in range(6)])
    last_p = [x - SHIFTS[1] * t for x, t in zip(precondition(blk_p, image_p, 16), next_p)]
    last_q = [x - SHIFTS[1] * t[0:8] for x, t in zip(precondition(blk_q, image_q, 8), next_q)]
    for i in range(6):
        t_ref[12 + i] = last_p[i][0:8]

    image_p = jacobian(plasma_p, last_p, half_q, last_q, half_q, last_q, res_s[0], 8)
    krylov.append([image_p[i] - SHIFTS[2] * krylov[2][i] for i in range(6)])

    out = jnp.zeros((1, 128), F32)
    lanes = lax.broadcasted_iota(jnp.int32, (1, 128), 1)
    for k, (i, j) in enumerate(PAIRS):
        total = krylov[i][0] * krylov[j][0]
        for f in range(1, 6):
            total = total + krylov[i][f] * krylov[j][f]
        total = jnp.sum(jnp.sum(total, axis=0, keepdims=True), axis=1, keepdims=True)
        out = jnp.where(lanes == k, total, out)
    gram_ref[...] = jnp.broadcast_to(out[None], gram_ref.shape)


def finish_kernel(inverse_root, gram_ref, t_ref, update_ref, estimates_ref):
    gathered = gram_ref[...]
    sums = jnp.sum(gathered, axis=0)
    lanes = lax.broadcasted_iota(jnp.int32, sums.shape, 1)
    gram = {}
    for k, pair in enumerate(PAIRS):
        gram[pair] = jnp.sum(jnp.where(lanes == k, sums, 0.0), axis=1, keepdims=True)
    factors, estimate_list = solve_from_gram(gram)
    width = update_ref.shape[-1]
    wide = [jnp.broadcast_to(f, (8, width)) for f in factors]
    for i in range(6):
        update_ref[i] = wide[0] * t_ref[i] + wide[1] * t_ref[6 + i] + wide[2] * t_ref[12 + i]
    for k, value in enumerate(estimate_list):
        estimates_ref[k] = jnp.sum(value * inverse_root)


def two_planes(pol, plasma_state, right_side, resistivity, jacobi_blocks):
    rows, width = plasma_state.shape[2], plasma_state.shape[3]
    count = 2 * pol

    def pairs(partner):
        out = []
        for t in range(2):
            for p in range(pol):
                other = partner(t, p)
                if 0 <= other[1] < pol:
                    out.append((t * pol + p, other[0] * pol + other[1]))
        return out

    across = pairs(lambda t, p: (1 - t, p))
    core = pairs(lambda t, p: (t, p ^ 1))
    outer = pairs(lambda t, p: (t, p - 1 if p % 2 == 0 else p + 1))

    plasma = plasma_state.reshape(6, rows, width)
    rhs = right_side.reshape(6, rows, width)
    res = resistivity.reshape(1, rows, width)
    blocks = jacobi_blocks.reshape(6, 6, rows, width)
    slab = P_ROWS + Q_ROWS
    vmem = pl.BlockSpec(memory_space=pltpu.VMEM)
    shape = jax.ShapeDtypeStruct
    t0, own, edge = pl.pallas_call(
        first_kernel,
        out_shape=(
            vmem_array((6, rows, width), F32),
            vmem_array((49, rows, width), F32),
            vmem_array((Q_ROWS, width), BF16),
        ),
        in_specs=[pl.BlockSpec(memory_space=pltpu.HBM)] * 4,
        out_specs=(vmem,) * 3,
        scratch_shapes=[pltpu.VMEM((Q_ROWS, width), F32), pltpu.SemaphoreType.DMA((9,))],
    )(*map(in_hbm, (plasma, rhs, blocks, res)))
    edge = lax.ppermute(edge, AXES, across)
    side, core_side = pl.pallas_call(
        pack_kernel,
        out_shape=(vmem_array((P_ROWS, width), BF16), vmem_array((P_ROWS, width), BF16)),
        in_specs=[vmem] * 2,
        out_specs=(vmem,) * 2,
        scratch_shapes=[pltpu.VMEM((P_ROWS, width), F32)],
    )(in_vmem(t0), in_vmem(own))
    core_p = lax.ppermute(core_side, AXES, core)
    bulk = pl.pallas_call(
        bulk_kernel, out_shape=vmem_array((400, width), BF16), in_specs=[vmem] * 3, out_specs=vmem
    )(in_vmem(t0), in_vmem(own), in_vmem(core_p))
    bulk = lax.ppermute(bulk, AXES, across)
    outer_slab = pl.pallas_call(
        join_kernel,
        out_shape=vmem_array((slab, width), BF16),
        in_specs=[vmem] * 2,
        out_specs=vmem,
        cost_estimate=pl.CostEstimate(flops=100_000_000_000, bytes_accessed=1_000_000, transcendentals=0),
    )(in_vmem(side), in_vmem(edge))
    from_outer = lax.ppermute(outer_slab, AXES, outer)
    other, core_slab = pl.pallas_call(
        unpack_kernel,
        out_shape=(vmem_array((50, rows, width), F32), vmem_array((Q_ROWS, width), BF16)),
        in_specs=[vmem],
        out_specs=(vmem,) * 2,
        scratch_shapes=[pltpu.VMEM((Q_ROWS, width), F32)],
    )(in_vmem(bulk))
    core_q = lax.ppermute(core_slab, AXES, core)
    gram, tangents = pl.pallas_call(
        krylov_kernel,
        out_shape=(vmem_array((count, 1, 128), F32), vmem_array((18, rows, width), F32)),
        in_specs=[vmem] * 6,
        out_specs=(vmem,) * 2,
        scratch_shapes=[
            pltpu.VMEM((slab, width), F32),
            pltpu.VMEM((slab, width), F32),
            pltpu.VMEM((36, 16, width), F32),
            pltpu.VMEM((36, 16, width), F32),
            pltpu.VMEM((12, 16, width), F32),
            pltpu.VMEM((12, 16, width), F32),
            pltpu.VMEM((2, 16, width), F32),
        ],
    )(*map(in_vmem, (own, t0, other, from_outer, core_p, core_q)))
    gram = lax.all_to_all(gram, AXES, 0, 0, tiled=True)
    inverse_root = float((6.0 * count * rows * width) ** -0.5)
    update, estimates = pl.pallas_call(
        functools.partial(finish_kernel, inverse_root),
        out_shape=(shape((6, rows, width), F32), shape((ITERS,), F32)),
        in_specs=[vmem] * 2,
        out_specs=(vmem, pl.BlockSpec(memory_space=pltpu.SMEM)),
    )(in_vmem(gram), in_vmem(tangents))
    return update.reshape(plasma_state.shape), estimates


def padded(cells, axis, dim, closed):
    count = lax.axis_size(axis)
    ends = count if closed else count - 1
    size = cells.shape[dim]
    head = lax.slice_in_dim(cells, 0, 1, axis=dim)
    tail = lax.slice_in_dim(cells, size - 1, size, axis=dim)
    before = lax.ppermute(tail, axis, [(i, (i + 1) % count) for i in range(ends)])
    after = lax.ppermute(head, axis, [((i + 1) % count, i) for i in range(ends)])
    return jnp.concatenate([before, cells, after], axis=dim)


def any_planes(plasma_state, right_side, resistivity, jacobi_blocks):
    cell_count = right_side.size * lax.axis_size("tor") * lax.axis_size("pol")
    fixed = jnp.full((3,) + resistivity.shape, viscosity, F32)
    diffusion = jnp.concatenate([jnp.broadcast_to(resistivity[None], fixed.shape), fixed])

    def around(cells):
        planes = padded(cells.astype(BF16), "tor", 1, True).astype(F32)
        planes = jnp.concatenate([planes[:, :1], cells, planes[:, -1:]], axis=1)
        deep = jnp.pad(cells, ((0, 0), (0, 0), (0, 0), (1, 1)))
        return planes, padded(cells, "pol", 2, False), deep

    plasma_around = around(plasma_state)
    vectors, tangents = [right_side], []
    for shift in SHIFTS:
        vector = vectors[-1]
        tangent = jnp.sum(jacobi_blocks * vector[None], axis=1)
        tangents.append(tangent)
        image = inverse_step * tangent
        laplace = jnp.zeros_like(tangent)
        for direction, (plasma, cells) in enumerate(zip(plasma_around, around(tangent))):
            dim = direction + 1
            flux = jnp.stack(linear_flux(plasma, cells, direction))
            size = cells.shape[dim]
            part = functools.partial(lax.slice_in_dim, axis=dim)
            image = image + 0.5 * (part(flux, 2, size) - part(flux, 0, size - 2))
            laplace = laplace + part(cells, 2, size) + part(cells, 0, size - 2) - 2.0 * tangent
        vectors.append(image - diffusion * laplace - shift * vector)
    local = jnp.stack([jnp.sum(vectors[i] * vectors[j]) for i, j in PAIRS])
    gram = lax.psum(local, AXES)
    factors, estimate_list = solve_from_gram({pair: gram[k] for k, pair in enumerate(PAIRS)})
    update = sum(factor * tangent for factor, tangent in zip(factors, tangents))
    return update, jnp.stack(estimate_list) / jnp.sqrt(F32(cell_count))


def solution(mesh):
    tor, pol = mesh.shape["tor"], mesh.shape["pol"]

    def shards(plasma_state, right_side, resistivity, jacobi_blocks):
        _, planes, rows, width = plasma_state.shape
        fast = tor == 2 and planes == 1 and pol % 2 == 0 and rows == 8 and width % 128 == 0
        if fast:
            return two_planes(pol, plasma_state, right_side, resistivity, jacobi_blocks)
        return any_planes(plasma_state, right_side, resistivity, jacobi_blocks)

    return jax.shard_map(
        shards,
        mesh=mesh,
        in_specs=(
            P(None, "tor", "pol", None),
            P(None, "tor", "pol", None),
            P("tor", "pol", None),
            P(None, None, "tor", "pol", None),
        ),
        out_specs=(P(None, "tor", "pol", None), P()),
        check_vma=False,
    )
```

```python
import functools

import jax
import jax.numpy as jnp
from jax import lax
from jax.experimental import pallas as pl
from jax.experimental.pallas import tpu as pltpu
from jax.sharding import PartitionSpec as P

ITERS = 3
SHIFTS = (1.0, 2.0, 3.0)
inverse_step = 1.0
viscosity = 0.2
epsilon = 1e-06
AXES = ("tor", "pol")
PAIRS = [(i, j) for i in range(ITERS + 1) for j in range(i, ITERS + 1)]
BF16 = jnp.bfloat16
F32 = jnp.float32


def linear_flux(plasma, tangent, direction):
    magnetic, velocity = plasma[0:3], plasma[3:6]
    tang_mag, tang_vel = tangent[0:3], tangent[3:6]
    pressure = magnetic[0] * tang_mag[0] + magnetic[1] * tang_mag[1] + magnetic[2] * tang_mag[2]
    components = []
    for i in range(3):
        components.append(
            tang_vel[direction] * magnetic[i]
            + velocity[direction] * tang_mag[i]
            - tang_mag[direction] * velocity[i]
            - magnetic[direction] * tang_vel[i]
        )
    for i in range(3):
        moment = (
            tang_vel[direction] * velocity[i]
            + velocity[direction] * tang_vel[i]
            - tang_mag[direction] * magnetic[i]
            - magnetic[direction] * tang_mag[i]
        )
        if i == direction:
            moment = moment + pressure
        components.append(moment)
    return components


def least_squares(columns, initial_norm):
    count = len(columns)
    rhs_list = [initial_norm] + [None] * count
    cosines = []
    sines = []
    triangle = []
    estimate_list = []
    for column in range(count):
        entries = list(columns[column])
        for i in range(column):
            first_value, second_value = entries[i], entries[i + 1]
            entries[i] = cosines[i] * first_value + sines[i] * second_value
            entries[i + 1] = -sines[i] * first_value + cosines[i] * second_value
        first_value, second_value = entries[column], entries[column + 1]
        radius = jnp.sqrt(first_value * first_value + second_value * second_value)
        cosine = first_value / radius
        sine_value = second_value / radius
        cosines.append(cosine)
        sines.append(sine_value)
        entries[column] = radius
        triangle.append(entries[: column + 1])
        previous = rhs_list[column]
        rhs_list[column] = cosine * previous
        rhs_list[column + 1] = -sine_value * previous
        estimate_list.append(jnp.abs(rhs_list[column + 1]))
    weights = [None] * count
    for column in reversed(range(count)):
        partial_value = rhs_list[column]
        for later in range(column + 1, count):
            partial_value = partial_value - triangle[later][column] * weights[later]
        weights[column] = partial_value / triangle[column][column]
    return weights, estimate_list


def solve_from_gram(gram):
    count = ITERS + 1

    def inner(left, right):
        total = None
        for i in range(count):
            row = None
            for j in range(count):
                if right[j] is None:
                    continue
                term = gram[(min(i, j), max(i, j))] * right[j]
                row = term if row is None else row + term
            if left[i] is None or row is None:
                continue
            term = left[i] * row
            total = term if total is None else total + term
        return total

    def minus(left, factor, right):
        out = []
        for a, b in zip(left, right):
            if b is None:
                out.append(a)
            else:
                out.append(a - factor * b)
        return out

    initial_norm = jnp.sqrt(gram[(0, 0)] + epsilon)
    basis = [[1.0 / initial_norm] + [None] * ITERS]
    columns = []
    for column in range(ITERS):
        vector = basis[column]
        image = []
        for i in range(count):
            entry = None
            if vector[i] is not None:
                entry = SHIFTS[i] * vector[i]
            if i > 0 and vector[i - 1] is not None:
                entry = vector[i - 1] if entry is None else entry + vector[i - 1]
            image.append(entry)
        coefficients = [inner(earlier, image) for earlier in basis]
        remainder = image
        for coefficient, earlier in zip(coefficients, basis):
            remainder = minus(remainder, coefficient, earlier)
        square = jnp.maximum(inner(remainder, remainder), 0.0)
        new_norm = jnp.sqrt(square + epsilon)
        columns.append(coefficients + [new_norm])
        if column + 1 < ITERS:
            scale = 1.0 / new_norm
            basis.append([None if r is None else r * scale for r in remainder])
    weights, estimate_list = least_squares(columns, initial_norm)
    factors = []
    for k in range(ITERS):
        total = None
        for weight, vector in zip(weights, basis):
            if vector[k] is not None:
                term = weight * vector[k]
                total = term if total is None else total + term
        factors.append(total)
    return factors, estimate_list


in_vmem = functools.partial(pltpu.with_memory_space_constraint, memory_space=pltpu.VMEM)
in_hbm = functools.partial(pltpu.with_memory_space_constraint, memory_space=pltpu.HBM)
vmem_array = pltpu.VMEM
P_ROWS, Q_ROWS = 128, 64


def tile_rows(value, count, first):
    return jnp.where(first, value[0:count], value[8 - count : 8])


def fill_slab_q(scr, deep, wide, first):
    scr[pl.ds(Q_ROWS - 8, 8), :] = jnp.zeros((8, deep[0].shape[1]), F32)
    for f, value in enumerate(deep):
        scr[pl.ds(2 * f, 2), :] = tile_rows(value, 2, first)
    for f, value in enumerate(wide):
        scr[pl.ds(24 + f, 1), :] = tile_rows(value, 1, first)
    return scr[...].astype(BF16)


def fill_slab_p(scr, deep, wide, first):
    scr[pl.ds(P_ROWS - 8, 8), :] = jnp.zeros((8, deep[0].shape[1]), F32)
    for f, value in enumerate(deep):
        scr[pl.ds(4 * f, 4), :] = tile_rows(value, 4, first)
    for f, value in enumerate(wide):
        scr[pl.ds(48 + 2 * f, 2), :] = tile_rows(value, 2, first)
    return scr[...].astype(BF16)


def first_kernel(
    plasma_hbm, rhs_hbm, blocks_hbm, res_hbm,
    t0_ref, own_ref, bulk_ref, edge_ref, inner_ref, scr, sems,
):
    copies = [
        pltpu.make_async_copy(rhs_hbm, own_ref.at[pl.ds(43, 6)], sems.at[0]),
        pltpu.make_async_copy(plasma_hbm, own_ref.at[pl.ds(37, 6)], sems.at[1]),
        pltpu.make_async_copy(res_hbm, own_ref.at[pl.ds(36, 1)], sems.at[2]),
    ] + [pltpu.make_async_copy(blocks_hbm.at[a], own_ref.at[pl.ds(6 * a, 6)], sems.at[3 + a]) for a in range(6)]
    for copy in copies:
        copy.start()
    even = lax.axis_index("pol") % 2 == 0
    for copy in copies[:3]:
        copy.wait()
    vector = [own_ref[43 + b] for b in range(6)]
    t0 = []
    for a in range(6):
        copies[3 + a].wait()
        total = own_ref[6 * a] * vector[0]
        for b in range(1, 6):
            total = total + own_ref[6 * a + b] * vector[b]
        t0_ref[a] = total
        t0.append(total)
    deep = t0 + [own_ref[37 + i] for i in range(6)]
    wide = [own_ref[i] for i in range(37)]
    fields = wide[:36] + deep + [wide[36], wide[36]]
    for g in range(25):
        pair = jnp.concatenate([fields[2 * g], fields[2 * g + 1]], axis=0)
        bulk_ref[pl.ds(16 * g, 16), :] = pair.astype(BF16)
    edge_ref[...] = fill_slab_q(scr, deep, wide, even)
    inner_ref[...] = fill_slab_q(scr, deep, wide, jnp.logical_not(even))


def pack_kernel(t0_ref, own_ref, side_ref, core_ref, scr):
    even = lax.axis_index("pol") % 2 == 0
    deep = [t0_ref[i] for i in range(6)] + [own_ref[37 + i] for i in range(6)]
    wide = [own_ref[i] for i in range(37)]
    side_ref[...] = fill_slab_p(scr, deep, wide, even)
    core_ref[...] = fill_slab_p(scr, deep, wide, jnp.logical_not(even))


def krylov_kernel(
    own_ref, t0_ref, bulk_ref, outer_p_ref, outer_q_ref, core_p_ref, core_q_ref,
    gram_ref, t_ref, up, down, blk_p, blk_q, st_p, st_q, res_s,
):
    width = own_ref.shape[-1]
    even = lax.axis_index("pol") % 2 == 0
    from_outer = jnp.concatenate([outer_p_ref[...], outer_q_ref[...]], axis=0).astype(F32)
    from_core = jnp.concatenate([core_p_ref[...], core_q_ref[...]], axis=0).astype(F32)
    place = lax.axis_index("pol")
    edge = jnp.logical_or(place == 0, place == lax.axis_size("pol") - 1)
    from_outer = jnp.where(edge, 0.0, from_outer)
    up[...] = jnp.where(even, from_outer, from_core)
    down[...] = jnp.where(even, from_core, from_outer)
    zeros = jnp.zeros((8, width), F32)

    def halo(ref, at, offset, rows):
        if rows < 4:
            ref[at, 8:16] = zeros
        ref[at, 8 : 8 + rows] = down[pl.ds(offset, rows), :]
        ref[at, 16 - rows : 16] = up[pl.ds(offset, rows), :]

    def other(field):
        pair = bulk_ref[pl.ds(16 * (field // 2), 16), :].astype(F32)
        return pair[0:8] if field % 2 == 0 else pair[8:16]

    for i in range(36):
        blk_p[i, 0:8] = own_ref[i]
        halo(blk_p, i, 48 + 2 * i, 2)
        blk_q[i, 0:8] = other(i)
        halo(blk_q, i, P_ROWS + 24 + i, 1)
    for i in range(12):
        st_p[i, 0:8] = t0_ref[i] if i < 6 else own_ref[31 + i]
        halo(st_p, i, 4 * i, 4)
        st_q[i, 0:8] = other(36 + i)
        halo(st_q, i, P_ROWS + 2 * i, 2)
    res_s[0, 0:8] = own_ref[36]
    halo(res_s, 0, 120, 2)
    res_s[1, 0:8] = other(48)
    halo(res_s, 1, P_ROWS + 60, 1)

    def lane(shape):
        return lax.broadcasted_iota(jnp.int32, shape, 1)

    def depth_next(x):
        return jnp.where(lane(x.shape) == width - 1, 0.0, pltpu.roll(x, width - 1, 1))

    def depth_prev(x):
        return jnp.where(lane(x.shape) == 0, 0.0, pltpu.roll(x, 1, 1))

    def jacobian(plasma, tangent, plasma_next, tangent_next, plasma_prev, tangent_prev, res, rows):
        flux_next = linear_flux(plasma_next, tangent_next, 0)
        flux_prev = linear_flux(plasma_prev, tangent_prev, 0)
        flux_rows = linear_flux(plasma, tangent, 1)
        own = [x[0:rows] for x in tangent]
        flux_depth = linear_flux([x[0:rows] for x in plasma], own, 2)
        out = []
        for i in range(6):
            total = inverse_step * own[i] + 0.5 * (flux_next[i][0:rows] - flux_prev[i][0:rows])
            laplace = tangent_next[i][0:rows] + tangent_prev[i][0:rows] - 2.0 * own[i]
            total = total + 0.5 * (
                pltpu.roll(flux_rows[i], 15, 0)[0:rows] - pltpu.roll(flux_rows[i], 1, 0)[0:rows]
            )
            laplace = laplace + (
                pltpu.roll(tangent[i], 15, 0)[0:rows] + pltpu.roll(tangent[i], 1, 0)[0:rows] - 2.0 * own[i]
            )
            total = total + 0.5 * (depth_next(flux_depth[i]) - depth_prev(flux_depth[i]))
            laplace = laplace + (depth_next(own[i]) + depth_prev(own[i]) - 2.0 * own[i])
            out.append(total - (res[0:rows] if i < 3 else viscosity) * laplace)
        return out

    def precondition(ref, vector, rows):
        out = []
        for a in range(6):
            total = ref[6 * a, 0:rows] * vector[0]
            for b in range(1, 6):
                total = total + ref[6 * a + b, 0:rows] * vector[b]
            out.append(total)
        return out

    plasma_p = [st_p[6 + i] for i in range(6)]
    plasma_q = [st_q[6 + i] for i in range(6)]
    half_p = [x[0:8] for x in plasma_p]
    half_q = [x[0:8] for x in plasma_q]
    krylov = [[own_ref[43 + i] for i in range(6)]]
    tang_p = [st_p[i] for i in range(6)]
    tang_q = [st_q[i] for i in range(6)]
    for i in range(6):
        t_ref[i] = t0_ref[i]

    image_p = jacobian(plasma_p, tang_p, plasma_q, tang_q, plasma_q, tang_q, res_s[0], 16)
    image_q = jacobian(plasma_q, tang_q, plasma_p, tang_p, plasma_p, tang_p, res_s[1], 16)
    krylov.append([image_p[i][0:8] - SHIFTS[0] * krylov[0][i] for i in range(6)])
    next_p = [x - SHIFTS[0] * t for x, t in zip(precondition(blk_p, image_p, 16), tang_p)]
    next_q = [x - SHIFTS[0] * t for x, t in zip(precondition(blk_q, image_q, 16), tang_q)]
    for i in range(6):
        t_ref[6 + i] = next_p[i][0:8]

    image_p = jacobian(plasma_p, next_p, plasma_q, next_q, plasma_q, next_q, res_s[0], 16)
    image_q = jacobian(plasma_q, next_q, half_p, [x[0:8] for x in next_p], half_p, [x[0:8] for x in next_p], res_s[1], 8)
    krylov.append([image_p[i][0:8] - SHIFTS[1] * krylov[1][i] for i in range(6)])
    last_p = [x - SHIFTS[1] * t for x, t in zip(precondition(blk_p, image_p, 16), next_p)]
    last_q = [x - SHIFTS[1] * t[0:8] for x, t in zip(precondition(blk_q, image_q, 8), next_q)]
    for i in range(6):
        t_ref[12 + i] = last_p[i][0:8]

    image_p = jacobian(plasma_p, last_p, half_q, last_q, half_q, last_q, res_s[0], 8)
    krylov.append([image_p[i] - SHIFTS[2] * krylov[2][i] for i in range(6)])

    out = jnp.zeros((1, 128), F32)
    lanes = lax.broadcasted_iota(jnp.int32, (1, 128), 1)
    for k, (i, j) in enumerate(PAIRS):
        total = krylov[i][0] * krylov[j][0]
        for f in range(1, 6):
            total = total + krylov[i][f] * krylov[j][f]
        total = jnp.sum(jnp.sum(total, axis=0, keepdims=True), axis=1, keepdims=True)
        out = jnp.where(lanes == k, total, out)
    gram_ref[...] = jnp.broadcast_to(out[None], gram_ref.shape)


def finish_kernel(inverse_root, gram_ref, t_ref, update_ref, estimates_ref):
    gathered = gram_ref[...]
    sums = jnp.sum(gathered, axis=0)
    lanes = lax.broadcasted_iota(jnp.int32, sums.shape, 1)
    gram = {}
    for k, pair in enumerate(PAIRS):
        gram[pair] = jnp.sum(jnp.where(lanes == k, sums, 0.0), axis=1, keepdims=True)
    factors, estimate_list = solve_from_gram(gram)
    width = update_ref.shape[-1]
    wide = [jnp.broadcast_to(f, (8, width)) for f in factors]
    for i in range(6):
        update_ref[i] = wide[0] * t_ref[i] + wide[1] * t_ref[6 + i] + wide[2] * t_ref[12 + i]
    for k, value in enumerate(estimate_list):
        estimates_ref[k] = jnp.sum(value * inverse_root)


def two_planes(pol, plasma_state, right_side, resistivity, jacobi_blocks):
    rows, width = plasma_state.shape[2], plasma_state.shape[3]
    count = 2 * pol

    def pairs(partner):
        return [(t * pol + p, q * pol + r) for t in range(2) for p in range(pol) for q, r in [partner(t, p)]]

    def beyond(t, p, far):
        r = p - 1 if p % 2 == 0 else p + 1
        return (far, r) if 0 <= r < pol else (1 - t, p)

    across = pairs(lambda t, p: (1 - t, p))
    core = pairs(lambda t, p: (t, p ^ 1))
    outer = pairs(lambda t, p: beyond(t, p, t))
    corner = pairs(lambda t, p: beyond(t, p, 1 - t))
    across_core = pairs(lambda t, p: (1 - t, p ^ 1))

    plasma = plasma_state.reshape(6, rows, width)
    rhs = right_side.reshape(6, rows, width)
    res = resistivity.reshape(1, rows, width)
    blocks = jacobi_blocks.reshape(6, 6, rows, width)
    slab = P_ROWS + Q_ROWS
    vmem = pl.BlockSpec(memory_space=pltpu.VMEM)
    shape = jax.ShapeDtypeStruct
    t0, own, bulk, edge, inner = pl.pallas_call(
        first_kernel,
        out_shape=(
            vmem_array((6, rows, width), F32),
            vmem_array((49, rows, width), F32),
            vmem_array((400, width), BF16),
            vmem_array((Q_ROWS, width), BF16),
            vmem_array((Q_ROWS, width), BF16),
        ),
        in_specs=[pl.BlockSpec(memory_space=pltpu.HBM)] * 4,
        out_specs=(vmem,) * 5,
        scratch_shapes=[pltpu.VMEM((Q_ROWS, width), F32), pltpu.SemaphoreType.DMA((9,))],
    )(*map(in_hbm, (plasma, rhs, blocks, res)))
    bulk = lax.ppermute(bulk, AXES, across)
    outer_q = lax.ppermute(edge, AXES, corner)
    side, core_side = pl.pallas_call(
        pack_kernel,
        out_shape=(vmem_array((P_ROWS, width), BF16), vmem_array((P_ROWS, width), BF16)),
        in_specs=[vmem] * 2,
        out_specs=(vmem,) * 2,
        scratch_shapes=[pltpu.VMEM((P_ROWS, width), F32)],
    )(in_vmem(t0), in_vmem(own))
    outer_p = lax.ppermute(side, AXES, outer)
    core_q = lax.ppermute(inner, AXES, across_core)
    core_p = lax.ppermute(core_side, AXES, core)
    gram, tangents = pl.pallas_call(
        krylov_kernel,
        out_shape=(vmem_array((count, 1, 128), F32), vmem_array((18, rows, width), F32)),
        in_specs=[vmem] * 7,
        out_specs=(vmem,) * 2,
        scratch_shapes=[
            pltpu.VMEM((slab, width), F32),
            pltpu.VMEM((slab, width), F32),
            pltpu.VMEM((36, 16, width), F32),
            pltpu.VMEM((36, 16, width), F32),
            pltpu.VMEM((12, 16, width), F32),
            pltpu.VMEM((12, 16, width), F32),
            pltpu.VMEM((2, 16, width), F32),
        ],
    )(*map(in_vmem, (own, t0, bulk, outer_p, outer_q, core_p, core_q)))
    gram = lax.all_to_all(gram, AXES, 0, 0, tiled=True)
    inverse_root = float((6.0 * count * rows * width) ** -0.5)
    update, estimates = pl.pallas_call(
        functools.partial(finish_kernel, inverse_root),
        out_shape=(shape((6, rows, width), F32), shape((ITERS,), F32)),
        in_specs=[vmem] * 2,
        out_specs=(vmem, pl.BlockSpec(memory_space=pltpu.SMEM)),
    )(in_vmem(gram), in_vmem(tangents))
    return update.reshape(plasma_state.shape), estimates


def padded(cells, axis, dim, closed):
    count = lax.axis_size(axis)
    ends = count if closed else count - 1
    size = cells.shape[dim]
    head = lax.slice_in_dim(cells, 0, 1, axis=dim)
    tail = lax.slice_in_dim(cells, size - 1, size, axis=dim)
    before = lax.ppermute(tail, axis, [(i, (i + 1) % count) for i in range(ends)])
    after = lax.ppermute(head, axis, [((i + 1) % count, i) for i in range(ends)])
    return jnp.concatenate([before, cells, after], axis=dim)


def any_planes(plasma_state, right_side, resistivity, jacobi_blocks):
    cell_count = right_side.size * lax.axis_size("tor") * lax.axis_size("pol")
    fixed = jnp.full((3,) + resistivity.shape, viscosity, F32)
    diffusion = jnp.concatenate([jnp.broadcast_to(resistivity[None], fixed.shape), fixed])

    def around(cells):
        planes = padded(cells.astype(BF16), "tor", 1, True).astype(F32)
        planes = jnp.concatenate([planes[:, :1], cells, planes[:, -1:]], axis=1)
        deep = jnp.pad(cells, ((0, 0), (0, 0), (0, 0), (1, 1)))
        return planes, padded(cells, "pol", 2, False), deep

    plasma_around = around(plasma_state)
    vectors, tangents = [right_side], []
    for shift in SHIFTS:
        vector = vectors[-1]
        tangent = jnp.sum(jacobi_blocks * vector[None], axis=1)
        tangents.append(tangent)
        image = inverse_step * tangent
        laplace = jnp.zeros_like(tangent)
        for direction, (plasma, cells) in enumerate(zip(plasma_around, around(tangent))):
            dim = direction + 1
            flux = jnp.stack(linear_flux(plasma, cells, direction))
            size = cells.shape[dim]
            part = functools.partial(lax.slice_in_dim, axis=dim)
            image = image + 0.5 * (part(flux, 2, size) - part(flux, 0, size - 2))
            laplace = laplace + part(cells, 2, size) + part(cells, 0, size - 2) - 2.0 * tangent
        vectors.append(image - diffusion * laplace - shift * vector)
    local = jnp.stack([jnp.sum(vectors[i] * vectors[j]) for i, j in PAIRS])
    gram = lax.psum(local, AXES)
    factors, estimate_list = solve_from_gram({pair: gram[k] for k, pair in enumerate(PAIRS)})
    update = sum(factor * tangent for factor, tangent in zip(factors, tangents))
    return update, jnp.stack(estimate_list) / jnp.sqrt(F32(cell_count))


def solution(mesh):
    tor, pol = mesh.shape["tor"], mesh.shape["pol"]

    def shards(plasma_state, right_side, resistivity, jacobi_blocks):
        _, planes, rows, width = plasma_state.shape
        fast = tor == 2 and planes == 1 and pol % 2 == 0 and rows == 8 and width % 128 == 0
        if fast:
            return two_planes(pol, plasma_state, right_side, resistivity, jacobi_blocks)
        return any_planes(plasma_state, right_side, resistivity, jacobi_blocks)

    return jax.shard_map(
        shards,
        mesh=mesh,
        in_specs=(
            P(None, "tor", "pol", None),
            P(None, "tor", "pol", None),
            P("tor", "pol", None),
            P(None, None, "tor", "pol", None),
        ),
        out_specs=(P(None, "tor", "pol", None), P()),
        check_vma=False,
    )
```

```python
import functools

import jax
import jax.numpy as jnp
from jax import lax
from jax.experimental import pallas as pl
from jax.experimental.pallas import tpu as pltpu
from jax.sharding import PartitionSpec as P

ITERS = 3
SHIFTS = (1.0, 2.0, 3.0)
inverse_step = 1.0
viscosity = 0.2
epsilon = 1e-06
AXES = ("tor", "pol")
PAIRS = [(i, j) for i in range(ITERS + 1) for j in range(i, ITERS + 1)]
BF16 = jnp.bfloat16
F32 = jnp.float32


def linear_flux(plasma, tangent, direction):
    magnetic, velocity = plasma[0:3], plasma[3:6]
    tang_mag, tang_vel = tangent[0:3], tangent[3:6]
    pressure = magnetic[0] * tang_mag[0] + magnetic[1] * tang_mag[1] + magnetic[2] * tang_mag[2]
    components = []
    for i in range(3):
        components.append(
            tang_vel[direction] * magnetic[i]
            + velocity[direction] * tang_mag[i]
            - tang_mag[direction] * velocity[i]
            - magnetic[direction] * tang_vel[i]
        )
    for i in range(3):
        moment = (
            tang_vel[direction] * velocity[i]
            + velocity[direction] * tang_vel[i]
            - tang_mag[direction] * magnetic[i]
            - magnetic[direction] * tang_mag[i]
        )
        if i == direction:
            moment = moment + pressure
        components.append(moment)
    return components


def least_squares(columns, initial_norm):
    count = len(columns)
    rhs_list = [initial_norm] + [None] * count
    cosines = []
    sines = []
    triangle = []
    estimate_list = []
    for column in range(count):
        entries = list(columns[column])
        for i in range(column):
            first_value, second_value = entries[i], entries[i + 1]
            entries[i] = cosines[i] * first_value + sines[i] * second_value
            entries[i + 1] = -sines[i] * first_value + cosines[i] * second_value
        first_value, second_value = entries[column], entries[column + 1]
        radius = jnp.sqrt(first_value * first_value + second_value * second_value)
        cosine = first_value / radius
        sine_value = second_value / radius
        cosines.append(cosine)
        sines.append(sine_value)
        entries[column] = radius
        triangle.append(entries[: column + 1])
        previous = rhs_list[column]
        rhs_list[column] = cosine * previous
        rhs_list[column + 1] = -sine_value * previous
        estimate_list.append(jnp.abs(rhs_list[column + 1]))
    weights = [None] * count
    for column in reversed(range(count)):
        partial_value = rhs_list[column]
        for later in range(column + 1, count):
            partial_value = partial_value - triangle[later][column] * weights[later]
        weights[column] = partial_value / triangle[column][column]
    return weights, estimate_list


def solve_from_gram(gram):
    count = ITERS + 1

    def inner(left, right):
        total = None
        for i in range(count):
            row = None
            for j in range(count):
                if right[j] is None:
                    continue
                term = gram[(min(i, j), max(i, j))] * right[j]
                row = term if row is None else row + term
            if left[i] is None or row is None:
                continue
            term = left[i] * row
            total = term if total is None else total + term
        return total

    def minus(left, factor, right):
        out = []
        for a, b in zip(left, right):
            if b is None:
                out.append(a)
            else:
                out.append(a - factor * b)
        return out

    initial_norm = jnp.sqrt(gram[(0, 0)] + epsilon)
    basis = [[1.0 / initial_norm] + [None] * ITERS]
    columns = []
    for column in range(ITERS):
        vector = basis[column]
        image = []
        for i in range(count):
            entry = None
            if vector[i] is not None:
                entry = SHIFTS[i] * vector[i]
            if i > 0 and vector[i - 1] is not None:
                entry = vector[i - 1] if entry is None else entry + vector[i - 1]
            image.append(entry)
        coefficients = [inner(earlier, image) for earlier in basis]
        remainder = image
        for coefficient, earlier in zip(coefficients, basis):
            remainder = minus(remainder, coefficient, earlier)
        square = jnp.maximum(inner(remainder, remainder), 0.0)
        new_norm = jnp.sqrt(square + epsilon)
        columns.append(coefficients + [new_norm])
        if column + 1 < ITERS:
            scale = 1.0 / new_norm
            basis.append([None if r is None else r * scale for r in remainder])
    weights, estimate_list = least_squares(columns, initial_norm)
    factors = []
    for k in range(ITERS):
        total = None
        for weight, vector in zip(weights, basis):
            if vector[k] is not None:
                term = weight * vector[k]
                total = term if total is None else total + term
        factors.append(total)
    return factors, estimate_list


in_vmem = functools.partial(pltpu.with_memory_space_constraint, memory_space=pltpu.VMEM)
in_hbm = functools.partial(pltpu.with_memory_space_constraint, memory_space=pltpu.HBM)
vmem_array = pltpu.VMEM
P_ROWS, Q_ROWS = 128, 64


def tile_rows(value, count, first):
    return jnp.where(first, value[0:count], value[8 - count : 8])


def fill_slab_q(scr, deep, wide, first):
    scr[pl.ds(Q_ROWS - 8, 8), :] = jnp.zeros((8, deep[0].shape[1]), F32)
    for f, value in enumerate(deep):
        scr[pl.ds(2 * f, 2), :] = tile_rows(value, 2, first)
    for f, value in enumerate(wide):
        scr[pl.ds(24 + f, 1), :] = tile_rows(value, 1, first)
    return scr[...].astype(BF16)


def fill_slab_p(scr, deep, wide, first):
    scr[pl.ds(P_ROWS - 8, 8), :] = jnp.zeros((8, deep[0].shape[1]), F32)
    for f, value in enumerate(deep):
        scr[pl.ds(4 * f, 4), :] = tile_rows(value, 4, first)
    for f, value in enumerate(wide):
        scr[pl.ds(48 + 2 * f, 2), :] = tile_rows(value, 2, first)
    return scr[...].astype(BF16)


def first_kernel(
    plasma_hbm, rhs_hbm, blocks_hbm, res_hbm,
    t0_ref, own_ref, bulk_ref, edge_ref, inner_ref, scr, sems,
):
    copies = [
        pltpu.make_async_copy(rhs_hbm, own_ref.at[pl.ds(43, 6)], sems.at[0]),
        pltpu.make_async_copy(plasma_hbm, own_ref.at[pl.ds(37, 6)], sems.at[1]),
        pltpu.make_async_copy(res_hbm, own_ref.at[pl.ds(36, 1)], sems.at[2]),
    ] + [pltpu.make_async_copy(blocks_hbm.at[a], own_ref.at[pl.ds(6 * a, 6)], sems.at[3 + a]) for a in range(6)]
    for copy in copies:
        copy.start()
    even = lax.axis_index("pol") % 2 == 0
    for copy in copies[:3]:
        copy.wait()
    vector = [own_ref[43 + b] for b in range(6)]
    t0 = []
    for a in range(6):
        copies[3 + a].wait()
        total = own_ref[6 * a] * vector[0]
        for b in range(1, 6):
            total = total + own_ref[6 * a + b] * vector[b]
        t0_ref[a] = total
        t0.append(total)
    deep = t0 + [own_ref[37 + i] for i in range(6)]
    wide = [own_ref[i] for i in range(37)]
    fields = wide[:36] + deep + [wide[36], wide[36]]
    for g in range(25):
        pair = jnp.concatenate([fields[2 * g], fields[2 * g + 1]], axis=0)
        bulk_ref[pl.ds(16 * g, 16), :] = pair.astype(BF16)
    edge_ref[...] = fill_slab_q(scr, deep, wide, even)
    inner_ref[...] = fill_slab_q(scr, deep, wide, jnp.logical_not(even))


def pack_kernel(t0_ref, own_ref, side_ref, core_ref, scr):
    even = lax.axis_index("pol") % 2 == 0
    deep = [t0_ref[i] for i in range(6)] + [own_ref[37 + i] for i in range(6)]
    wide = [own_ref[i] for i in range(37)]
    side_ref[...] = fill_slab_p(scr, deep, wide, even)
    core_ref[...] = fill_slab_p(scr, deep, wide, jnp.logical_not(even))


def depth_next(x):
    width = x.shape[1]
    lanes = lax.broadcasted_iota(jnp.int32, x.shape, 1)
    return jnp.where(lanes == width - 1, 0.0, pltpu.roll(x, width - 1, 1))


def depth_prev(x):
    lanes = lax.broadcasted_iota(jnp.int32, x.shape, 1)
    return jnp.where(lanes == 0, 0.0, pltpu.roll(x, 1, 1))


def sums_of(plasma):
    magnetic, velocity = plasma[0:3], plasma[3:6]
    return (
        [0.25 * (v + b) for v, b in zip(velocity, magnetic)]
        + [0.25 * (v - b) for v, b in zip(velocity, magnetic)]
        + [0.5 * b for b in magnetic]
    )


def tangent_sums(state, tangent):
    tang_mag, tang_vel = tangent[0:3], tangent[3:6]
    half_pressure = state[6] * tang_mag[0] + state[7] * tang_mag[1] + state[8] * tang_mag[2]
    return (
        [w + b for w, b in zip(tang_vel, tang_mag)]
        + [w - b for w, b in zip(tang_vel, tang_mag)]
        + [half_pressure]
    )


def first_rows(values, rows):
    return [x[0:rows] for x in values]


def half_flux(state, sums, k):
    magnetic, velocity = [], []
    for i in range(3):
        plus = sums[3 + k] * state[i] + state[3 + k] * sums[i]
        minus = sums[k] * state[3 + i] + state[k] * sums[3 + i]
        magnetic.append(plus - minus)
        velocity.append(plus + minus + sums[6] if i == k else plus + minus)
    return magnetic + velocity


def row_next(x, rows):
    if rows == 16:
        return pltpu.roll(x, 15, 0)
    own = x[0:8]
    sublanes = lax.broadcasted_iota(jnp.int32, own.shape, 0)
    return pltpu.roll(jnp.where(sublanes == 0, x[8:16], own), 7, 0)


def row_prev(x, rows):
    if rows == 16:
        return pltpu.roll(x, 1, 0)
    own = x[0:8]
    sublanes = lax.broadcasted_iota(jnp.int32, own.shape, 0)
    return pltpu.roll(jnp.where(sublanes == 7, x[8:16], own), 1, 0)


def around(res):
    return res, row_prev(res, 16), row_next(res, 16), depth_prev(res), depth_next(res)


def in_plane(state, tangent, sums, diffusion, rows):
    flux_rows = half_flux(state, sums, 1)
    own = first_rows(tangent, rows)
    flux_depth = half_flux(first_rows(state, rows), first_rows(sums, rows), 2)
    out = []
    for i in range(6):
        here, above, below, west, east = diffusion if i < 3 else (viscosity,) * 5
        if i < 3:
            here, west, east = first_rows((here, west, east), rows)
        total = (inverse_step + 4.0 * here) * own[i]
        total = total + row_next(flux_rows[i] - above * tangent[i], rows)
        total = total - row_prev(flux_rows[i] + below * tangent[i], rows)
        total = total + depth_next(flux_depth[i] - west * own[i])
        total = total - depth_prev(flux_depth[i] + east * own[i])
        out.append(total)
    return out


def between_planes(image, tangent, after, before, res):
    rows = image[0].shape[0]
    (state_next, next_t, sums_next), (state_prev, prev_t, sums_prev) = [
        [first_rows(values, rows) for values in plane] for plane in (after, before)
    ]
    flux_next = half_flux(state_next, sums_next, 0)
    flux_prev = half_flux(state_prev, sums_prev, 0)
    out = []
    for i in range(6):
        laplace = next_t[i] + prev_t[i] - 2.0 * tangent[i][0:rows]
        total = image[i] + (flux_next[i] - flux_prev[i])
        out.append(total - (res[0:rows] if i < 3 else viscosity) * laplace)
    return out


def precondition(ref, vector):
    rows = vector[0].shape[0]
    out = []
    for a in range(6):
        total = ref[6 * a, 0:rows] * vector[0]
        for b in range(1, 6):
            total = total + ref[6 * a + b, 0:rows] * vector[b]
        out.append(total)
    return out


def put_halo(ref, at, below, above, offset, rows):
    if rows < 4:
        ref[at, 8:16] = jnp.zeros((8, ref.shape[-1]), F32)
    ref[at, 8 : 8 + rows] = below[pl.ds(offset, rows), :]
    ref[at, 16 - rows : 16] = above[pl.ds(offset, rows), :]


def sort_slabs(outer_ref, core_ref, below, above):
    place = lax.axis_index("pol")
    even = place % 2 == 0
    edge = jnp.logical_or(place == 0, place == lax.axis_size("pol") - 1)
    from_outer = jnp.where(edge, 0.0, outer_ref[...].astype(F32))
    from_core = core_ref[...].astype(F32)
    above[...] = jnp.where(even, from_outer, from_core)
    below[...] = jnp.where(even, from_core, from_outer)


def own_plane_kernel(own_ref, t0_ref, outer_ref, core_ref, plane_ref, image_ref, below, above):
    sort_slabs(outer_ref, core_ref, below, above)
    for i in range(37):
        plane_ref[i, 0:8] = own_ref[i]
        put_halo(plane_ref, i, below, above, 48 + 2 * i, 2)
    for i in range(6):
        plane_ref[37 + i, 0:8] = own_ref[37 + i]
        put_halo(plane_ref, 37 + i, below, above, 24 + 4 * i, 4)
        plane_ref[43 + i, 0:8] = t0_ref[i]
        put_halo(plane_ref, 43 + i, below, above, 4 * i, 4)
    state = sums_of([plane_ref[37 + i] for i in range(6)])
    for i, value in enumerate(state):
        plane_ref[49 + i] = value
    tangent = [plane_ref[43 + i] for i in range(6)]
    sums = tangent_sums(state, tangent)
    for i, value in enumerate(in_plane(state, tangent, sums, around(plane_ref[36]), 16)):
        image_ref[i] = value


def krylov_kernel(
    own_ref, plane_ref, image_ref, bulk_ref, outer_ref, core_ref,
    gram_ref, t_ref, below, above, other_s,
):
    sort_slabs(outer_ref, core_ref, below, above)

    def other(field):
        pair = bulk_ref[pl.ds(16 * (field // 2), 16), :].astype(F32)
        return pair[0:8] if field % 2 == 0 else pair[8:16]

    for i in range(37):
        other_s[i, 0:8] = other(i if i < 36 else 48)
        put_halo(other_s, i, below, above, 24 + i, 1)
    for i in range(6):
        other_s[37 + i, 0:8] = other(42 + i)
        put_halo(other_s, 37 + i, below, above, 12 + 2 * i, 2)
        other_s[43 + i, 0:8] = other(36 + i)
        put_halo(other_s, 43 + i, below, above, 2 * i, 2)

    res_p, res_q = plane_ref[36], other_s[36]
    diffusion_p, diffusion_q = around(res_p), around(res_q)
    state_p = [plane_ref[49 + i] for i in range(9)]
    state_q = sums_of([other_s[37 + i] for i in range(6)])
    tang_p = [plane_ref[43 + i] for i in range(6)]
    tang_q = [other_s[43 + i] for i in range(6)]
    krylov = [[own_ref[43 + i] for i in range(6)]]
    for i in range(6):
        t_ref[i] = tang_p[i][0:8]

    def shifted(tangents, shift, earlier):
        return [t - shift * e[0 : t.shape[0]] for t, e in zip(tangents, earlier)]

    plane_p = (state_p, tang_p, tangent_sums(state_p, tang_p))
    plane_q = (state_q, tang_q, tangent_sums(state_q, tang_q))
    image_p = [image_ref[i] for i in range(6)]
    image_q = in_plane(*plane_q, diffusion_q, 16)
    image_p = between_planes(image_p, tang_p, plane_q, plane_q, res_p)
    image_q = between_planes(image_q, tang_q, plane_p, plane_p, res_q)
    krylov.append([image_p[i][0:8] - SHIFTS[0] * krylov[0][i] for i in range(6)])
    next_p = shifted(precondition(plane_ref, image_p), SHIFTS[0], tang_p)
    next_q = shifted(precondition(other_s, image_q), SHIFTS[0], tang_q)
    for i in range(6):
        t_ref[6 + i] = next_p[i][0:8]

    plane_p = (state_p, next_p, tangent_sums(state_p, next_p))
    plane_q = (state_q, next_q, tangent_sums(state_q, next_q))
    image_p = in_plane(*plane_p, diffusion_p, 16)
    image_q = in_plane(*plane_q, diffusion_q, 8)
    image_p = between_planes(image_p, next_p, plane_q, plane_q, res_p)
    image_q = between_planes(image_q, next_q, plane_p, plane_p, res_q)
    krylov.append([image_p[i][0:8] - SHIFTS[1] * krylov[1][i] for i in range(6)])
    last_p = shifted(precondition(plane_ref, image_p), SHIFTS[1], next_p)
    last_q = shifted(precondition(other_s, image_q), SHIFTS[1], next_q)
    for i in range(6):
        t_ref[12 + i] = last_p[i][0:8]

    plane_p = (state_p, last_p, tangent_sums(state_p, last_p))
    half_q = first_rows(state_q, 8)
    plane_q = (half_q, last_q, tangent_sums(half_q, last_q))
    image_p = in_plane(*plane_p, diffusion_p, 8)
    image_p = between_planes(image_p, last_p, plane_q, plane_q, res_p)
    krylov.append([image_p[i] - SHIFTS[2] * krylov[2][i] for i in range(6)])

    rows = lax.broadcasted_iota(jnp.int32, (16, 128), 0)
    lanes = lax.broadcasted_iota(jnp.int32, (16, 128), 1)
    table = jnp.zeros((16, 128), F32)
    for k, (i, j) in enumerate(PAIRS):
        total = krylov[i][0] * krylov[j][0]
        for f in range(1, 6):
            total = total + krylov[i][f] * krylov[j][f]
        line = total[:, 0:128]
        for start in range(128, total.shape[1], 128):
            line = line + total[:, start : start + 128]
        table = jnp.where(rows == k, jnp.sum(line, axis=0, keepdims=True), table)
    sums = jnp.sum(table, axis=1, keepdims=True)
    out = jnp.sum(jnp.where(rows == lanes, sums, 0.0), axis=0, keepdims=True)
    gram_ref[...] = jnp.broadcast_to(out[None], gram_ref.shape)


def finish_kernel(inverse_root, gram_ref, t_ref, update_ref, estimates_ref):
    gathered = gram_ref[...]
    sums = jnp.sum(gathered, axis=0)
    lanes = lax.broadcasted_iota(jnp.int32, sums.shape, 1)
    gram = {}
    for k, pair in enumerate(PAIRS):
        gram[pair] = jnp.sum(jnp.where(lanes == k, sums, 0.0), axis=1, keepdims=True)
    factors, estimate_list = solve_from_gram(gram)
    width = update_ref.shape[-1]
    wide = [jnp.broadcast_to(f, (8, width)) for f in factors]
    for i in range(6):
        update_ref[i] = wide[0] * t_ref[i] + wide[1] * t_ref[6 + i] + wide[2] * t_ref[12 + i]
    for k, value in enumerate(estimate_list):
        estimates_ref[k] = jnp.sum(value * inverse_root)


def two_planes(pol, plasma_state, right_side, resistivity, jacobi_blocks):
    rows, width = plasma_state.shape[2], plasma_state.shape[3]
    count = 2 * pol

    def pairs(partner):
        return [(t * pol + p, q * pol + r) for t in range(2) for p in range(pol) for q, r in [partner(t, p)]]

    def beyond(t, p, far):
        r = p - 1 if p % 2 == 0 else p + 1
        return (far, r) if 0 <= r < pol else (1 - t, p)

    across = pairs(lambda t, p: (1 - t, p))
    core = pairs(lambda t, p: (t, p ^ 1))
    outer = pairs(lambda t, p: beyond(t, p, t))
    corner = pairs(lambda t, p: beyond(t, p, 1 - t))
    across_core = pairs(lambda t, p: (1 - t, p ^ 1))

    plasma = plasma_state.reshape(6, rows, width)
    rhs = right_side.reshape(6, rows, width)
    res = resistivity.reshape(1, rows, width)
    blocks = jacobi_blocks.reshape(6, 6, rows, width)
    vmem = pl.BlockSpec(memory_space=pltpu.VMEM)
    shape = jax.ShapeDtypeStruct
    t0, own, bulk, edge, inner = pl.pallas_call(
        first_kernel,
        out_shape=(
            vmem_array((6, rows, width), F32),
            vmem_array((49, rows, width), F32),
            vmem_array((400, width), BF16),
            vmem_array((Q_ROWS, width), BF16),
            vmem_array((Q_ROWS, width), BF16),
        ),
        in_specs=[pl.BlockSpec(memory_space=pltpu.HBM)] * 4,
        out_specs=(vmem,) * 5,
        scratch_shapes=[pltpu.VMEM((Q_ROWS, width), F32), pltpu.SemaphoreType.DMA((9,))],
    )(*map(in_hbm, (plasma, rhs, blocks, res)))
    bulk = lax.ppermute(bulk, AXES, across)
    outer_q = lax.ppermute(edge, AXES, corner)
    side, core_side = pl.pallas_call(
        pack_kernel,
        out_shape=(vmem_array((P_ROWS, width), BF16), vmem_array((P_ROWS, width), BF16)),
        in_specs=[vmem] * 2,
        out_specs=(vmem,) * 2,
        scratch_shapes=[pltpu.VMEM((P_ROWS, width), F32)],
    )(in_vmem(t0), in_vmem(own))
    outer_p = lax.ppermute(side, AXES, outer)
    core_q = lax.ppermute(inner, AXES, across_core)
    core_p = lax.ppermute(core_side, AXES, core)
    plane, image = pl.pallas_call(
        own_plane_kernel,
        out_shape=(vmem_array((58, 16, width), F32), vmem_array((6, 16, width), F32)),
        in_specs=[vmem] * 4,
        out_specs=(vmem,) * 2,
        scratch_shapes=[pltpu.VMEM((P_ROWS, width), F32)] * 2,
        cost_estimate=pl.CostEstimate(flops=0, bytes_accessed=1_000_000, transcendentals=0),
    )(*map(in_vmem, (own, t0, outer_p, core_p)))
    gram, tangents = pl.pallas_call(
        krylov_kernel,
        out_shape=(vmem_array((count, 1, 128), F32), vmem_array((18, rows, width), F32)),
        in_specs=[vmem] * 6,
        out_specs=(vmem,) * 2,
        scratch_shapes=[pltpu.VMEM((Q_ROWS, width), F32)] * 2 + [pltpu.VMEM((49, 16, width), F32)],
    )(*map(in_vmem, (own, plane, image, bulk, outer_q, core_q)))
    gram = lax.all_to_all(gram, AXES, 0, 0, tiled=True)
    inverse_root = float((6.0 * count * rows * width) ** -0.5)
    update, estimates = pl.pallas_call(
        functools.partial(finish_kernel, inverse_root),
        out_shape=(shape((6, rows, width), F32), shape((ITERS,), F32)),
        in_specs=[vmem] * 2,
        out_specs=(vmem, pl.BlockSpec(memory_space=pltpu.SMEM)),
    )(in_vmem(gram), in_vmem(tangents))
    return update.reshape(plasma_state.shape), estimates


def padded(cells, axis, dim, closed):
    count = lax.axis_size(axis)
    ends = count if closed else count - 1
    size = cells.shape[dim]
    head = lax.slice_in_dim(cells, 0, 1, axis=dim)
    tail = lax.slice_in_dim(cells, size - 1, size, axis=dim)
    before = lax.ppermute(tail, axis, [(i, (i + 1) % count) for i in range(ends)])
    after = lax.ppermute(head, axis, [((i + 1) % count, i) for i in range(ends)])
    return jnp.concatenate([before, cells, after], axis=dim)


def any_planes(plasma_state, right_side, resistivity, jacobi_blocks):
    cell_count = right_side.size * lax.axis_size("tor") * lax.axis_size("pol")
    fixed = jnp.full((3,) + resistivity.shape, viscosity, F32)
    diffusion = jnp.concatenate([jnp.broadcast_to(resistivity[None], fixed.shape), fixed])

    def around(cells):
        planes = padded(cells.astype(BF16), "tor", 1, True).astype(F32)
        planes = jnp.concatenate([planes[:, :1], cells, planes[:, -1:]], axis=1)
        deep = jnp.pad(cells, ((0, 0), (0, 0), (0, 0), (1, 1)))
        return planes, padded(cells, "pol", 2, False), deep

    plasma_around = around(plasma_state)
    vectors, tangents = [right_side], []
    for shift in SHIFTS:
        vector = vectors[-1]
        tangent = jnp.sum(jacobi_blocks * vector[None], axis=1)
        tangents.append(tangent)
        image = inverse_step * tangent
        laplace = jnp.zeros_like(tangent)
        for direction, (plasma, cells) in enumerate(zip(plasma_around, around(tangent))):
            dim = direction + 1
            flux = jnp.stack(linear_flux(plasma, cells, direction))
            size = cells.shape[dim]
            part = functools.partial(lax.slice_in_dim, axis=dim)
            image = image + 0.5 * (part(flux, 2, size) - part(flux, 0, size - 2))
            laplace = laplace + part(cells, 2, size) + part(cells, 0, size - 2) - 2.0 * tangent
        vectors.append(image - diffusion * laplace - shift * vector)
    local = jnp.stack([jnp.sum(vectors[i] * vectors[j]) for i, j in PAIRS])
    gram = lax.psum(local, AXES)
    factors, estimate_list = solve_from_gram({pair: gram[k] for k, pair in enumerate(PAIRS)})
    update = sum(factor * tangent for factor, tangent in zip(factors, tangents))
    return update, jnp.stack(estimate_list) / jnp.sqrt(F32(cell_count))


def solution(mesh):
    tor, pol = mesh.shape["tor"], mesh.shape["pol"]

    def shards(plasma_state, right_side, resistivity, jacobi_blocks):
        _, planes, rows, width = plasma_state.shape
        fast = tor == 2 and planes == 1 and pol % 2 == 0 and rows == 8 and width % 128 == 0
        if fast:
            return two_planes(pol, plasma_state, right_side, resistivity, jacobi_blocks)
        return any_planes(plasma_state, right_side, resistivity, jacobi_blocks)

    return jax.shard_map(
        shards,
        mesh=mesh,
        in_specs=(
            P(None, "tor", "pol", None),
            P(None, "tor", "pol", None),
            P("tor", "pol", None),
            P(None, None, "tor", "pol", None),
        ),
        out_specs=(P(None, "tor", "pol", None), P()),
        check_vma=False,
    )
```

```python
import functools

import jax
import jax.numpy as jnp
from jax import lax
from jax.experimental import pallas as pl
from jax.experimental.pallas import tpu as pltpu
from jax.sharding import PartitionSpec as P

ITERS = 3
SHIFTS = (1.0, 2.0, 3.0)
inverse_step = 1.0
viscosity = 0.2
epsilon = 1e-06
AXES = ("tor", "pol")
PAIRS = [(i, j) for i in range(ITERS + 1) for j in range(i, ITERS + 1)]
BF16 = jnp.bfloat16
F32 = jnp.float32


def linear_flux(plasma, tangent, direction):
    magnetic, velocity = plasma[0:3], plasma[3:6]
    tang_mag, tang_vel = tangent[0:3], tangent[3:6]
    pressure = magnetic[0] * tang_mag[0] + magnetic[1] * tang_mag[1] + magnetic[2] * tang_mag[2]
    components = []
    for i in range(3):
        components.append(
            tang_vel[direction] * magnetic[i]
            + velocity[direction] * tang_mag[i]
            - tang_mag[direction] * velocity[i]
            - magnetic[direction] * tang_vel[i]
        )
    for i in range(3):
        moment = (
            tang_vel[direction] * velocity[i]
            + velocity[direction] * tang_vel[i]
            - tang_mag[direction] * magnetic[i]
            - magnetic[direction] * tang_mag[i]
        )
        if i == direction:
            moment = moment + pressure
        components.append(moment)
    return components


def least_squares(columns, initial_norm):
    count = len(columns)
    rhs_list = [initial_norm] + [None] * count
    cosines = []
    sines = []
    triangle = []
    estimate_list = []
    for column in range(count):
        entries = list(columns[column])
        for i in range(column):
            first_value, second_value = entries[i], entries[i + 1]
            entries[i] = cosines[i] * first_value + sines[i] * second_value
            entries[i + 1] = -sines[i] * first_value + cosines[i] * second_value
        first_value, second_value = entries[column], entries[column + 1]
        radius = jnp.sqrt(first_value * first_value + second_value * second_value)
        cosine = first_value / radius
        sine_value = second_value / radius
        cosines.append(cosine)
        sines.append(sine_value)
        entries[column] = radius
        triangle.append(entries[: column + 1])
        previous = rhs_list[column]
        rhs_list[column] = cosine * previous
        rhs_list[column + 1] = -sine_value * previous
        estimate_list.append(jnp.abs(rhs_list[column + 1]))
    weights = [None] * count
    for column in reversed(range(count)):
        partial_value = rhs_list[column]
        for later in range(column + 1, count):
            partial_value = partial_value - triangle[later][column] * weights[later]
        weights[column] = partial_value / triangle[column][column]
    return weights, estimate_list


def solve_from_gram(gram):
    count = ITERS + 1

    def inner(left, right):
        total = None
        for i in range(count):
            row = None
            for j in range(count):
                if right[j] is None:
                    continue
                term = gram[(min(i, j), max(i, j))] * right[j]
                row = term if row is None else row + term
            if left[i] is None or row is None:
                continue
            term = left[i] * row
            total = term if total is None else total + term
        return total

    def minus(left, factor, right):
        out = []
        for a, b in zip(left, right):
            if b is None:
                out.append(a)
            else:
                out.append(a - factor * b)
        return out

    initial_norm = jnp.sqrt(gram[(0, 0)] + epsilon)
    basis = [[1.0 / initial_norm] + [None] * ITERS]
    columns = []
    for column in range(ITERS):
        vector = basis[column]
        image = []
        for i in range(count):
            entry = None
            if vector[i] is not None:
                entry = SHIFTS[i] * vector[i]
            if i > 0 and vector[i - 1] is not None:
                entry = vector[i - 1] if entry is None else entry + vector[i - 1]
            image.append(entry)
        coefficients = [inner(earlier, image) for earlier in basis]
        remainder = image
        for coefficient, earlier in zip(coefficients, basis):
            remainder = minus(remainder, coefficient, earlier)
        square = jnp.maximum(inner(remainder, remainder), 0.0)
        new_norm = jnp.sqrt(square + epsilon)
        columns.append(coefficients + [new_norm])
        if column + 1 < ITERS:
            scale = 1.0 / new_norm
            basis.append([None if r is None else r * scale for r in remainder])
    weights, estimate_list = least_squares(columns, initial_norm)
    factors = []
    for k in range(ITERS):
        total = None
        for weight, vector in zip(weights, basis):
            if vector[k] is not None:
                term = weight * vector[k]
                total = term if total is None else total + term
        factors.append(total)
    return factors, estimate_list


in_vmem = functools.partial(pltpu.with_memory_space_constraint, memory_space=pltpu.VMEM)
in_hbm = functools.partial(pltpu.with_memory_space_constraint, memory_space=pltpu.HBM)
vmem_array = pltpu.VMEM
P_ROWS, Q_ROWS = 128, 64


def tile_rows(value, count, first):
    return jnp.where(first, value[0:count], value[8 - count : 8])


def fill_slab_q(scr, deep, wide, first):
    scr[pl.ds(Q_ROWS - 8, 8), :] = jnp.zeros((8, deep[0].shape[1]), F32)
    for f, value in enumerate(deep):
        scr[pl.ds(2 * f, 2), :] = tile_rows(value, 2, first)
    for f, value in enumerate(wide):
        scr[pl.ds(24 + f, 1), :] = tile_rows(value, 1, first)
    return scr[...].astype(BF16)


def fill_slab_p(scr, deep, wide, first):
    scr[pl.ds(P_ROWS - 8, 8), :] = jnp.zeros((8, deep[0].shape[1]), F32)
    for f, value in enumerate(deep):
        scr[pl.ds(4 * f, 4), :] = tile_rows(value, 4, first)
    for f, value in enumerate(wide):
        scr[pl.ds(48 + 2 * f, 2), :] = tile_rows(value, 2, first)
    return scr[...].astype(BF16)


def first_kernel(
    plasma_hbm, rhs_hbm, blocks_hbm, res_hbm,
    t0_ref, own_ref, bulk_ref, sems,
):
    copies = [
        pltpu.make_async_copy(rhs_hbm, own_ref.at[pl.ds(43, 6)], sems.at[0]),
        pltpu.make_async_copy(plasma_hbm, own_ref.at[pl.ds(37, 6)], sems.at[1]),
        pltpu.make_async_copy(res_hbm, own_ref.at[pl.ds(36, 1)], sems.at[2]),
    ] + [pltpu.make_async_copy(blocks_hbm.at[a], own_ref.at[pl.ds(6 * a, 6)], sems.at[3 + a]) for a in range(6)]
    for copy in copies:
        copy.start()
    for copy in copies[:3]:
        copy.wait()
    vector = [own_ref[43 + b] for b in range(6)]
    t0 = []
    for a in range(6):
        copies[3 + a].wait()
        total = own_ref[6 * a] * vector[0]
        for b in range(1, 6):
            total = total + own_ref[6 * a + b] * vector[b]
        t0_ref[a] = total
        t0.append(total)
    deep = t0 + [own_ref[37 + i] for i in range(6)]
    wide = [own_ref[i] for i in range(37)]
    fields = wide[:36] + deep + [wide[36], wide[36]]
    for g in range(25):
        pair = jnp.concatenate([fields[2 * g], fields[2 * g + 1]], axis=0)
        bulk_ref[pl.ds(16 * g, 16), :] = pair.astype(BF16)


def pack_kernel(t0_ref, own_ref, side_ref, core_ref, edge_ref, inner_ref, scr, scr_q):
    even = lax.axis_index("pol") % 2 == 0
    deep = [t0_ref[i] for i in range(6)] + [own_ref[37 + i] for i in range(6)]
    wide = [own_ref[i] for i in range(37)]
    side_ref[...] = fill_slab_p(scr, deep, wide, even)
    core_ref[...] = fill_slab_p(scr, deep, wide, jnp.logical_not(even))
    edge_ref[...] = fill_slab_q(scr_q, deep, wide, even)
    inner_ref[...] = fill_slab_q(scr_q, deep, wide, jnp.logical_not(even))


def depth_next(x):
    width = x.shape[1]
    lanes = lax.broadcasted_iota(jnp.int32, x.shape, 1)
    return jnp.where(lanes == width - 1, 0.0, pltpu.roll(x, width - 1, 1))


def depth_prev(x):
    lanes = lax.broadcasted_iota(jnp.int32, x.shape, 1)
    return jnp.where(lanes == 0, 0.0, pltpu.roll(x, 1, 1))


def sums_of(plasma):
    magnetic, velocity = plasma[0:3], plasma[3:6]
    return (
        [0.25 * (v + b) for v, b in zip(velocity, magnetic)]
        + [0.25 * (v - b) for v, b in zip(velocity, magnetic)]
        + [0.5 * b for b in magnetic]
    )


def tangent_sums(state, tangent):
    tang_mag, tang_vel = tangent[0:3], tangent[3:6]
    half_pressure = state[6] * tang_mag[0] + state[7] * tang_mag[1] + state[8] * tang_mag[2]
    return (
        [w + b for w, b in zip(tang_vel, tang_mag)]
        + [w - b for w, b in zip(tang_vel, tang_mag)]
        + [half_pressure]
    )


def first_rows(values, rows):
    return [x[0:rows] for x in values]


def half_flux(state, sums, k):
    magnetic, velocity = [], []
    for i in range(3):
        plus = sums[3 + k] * state[i] + state[3 + k] * sums[i]
        minus = sums[k] * state[3 + i] + state[k] * sums[3 + i]
        magnetic.append(plus - minus)
        velocity.append(plus + minus + sums[6] if i == k else plus + minus)
    return magnetic + velocity


def row_next(x, rows):
    if rows == 16:
        return pltpu.roll(x, 15, 0)
    own = x[0:8]
    sublanes = lax.broadcasted_iota(jnp.int32, own.shape, 0)
    return pltpu.roll(jnp.where(sublanes == 0, x[8:16], own), 7, 0)


def row_prev(x, rows):
    if rows == 16:
        return pltpu.roll(x, 1, 0)
    own = x[0:8]
    sublanes = lax.broadcasted_iota(jnp.int32, own.shape, 0)
    return pltpu.roll(jnp.where(sublanes == 7, x[8:16], own), 1, 0)


def around(res):
    return res, row_prev(res, 16), row_next(res, 16), depth_prev(res), depth_next(res)


def in_plane(state, tangent, sums, diffusion, rows):
    flux_rows = half_flux(state, sums, 1)
    own = first_rows(tangent, rows)
    flux_depth = half_flux(first_rows(state, rows), first_rows(sums, rows), 2)
    out = []
    for i in range(6):
        here, above, below, west, east = diffusion if i < 3 else (viscosity,) * 5
        if i < 3:
            here, west, east = first_rows((here, west, east), rows)
        total = (inverse_step + 4.0 * here) * own[i]
        total = total + row_next(flux_rows[i] - above * tangent[i], rows)
        total = total - row_prev(flux_rows[i] + below * tangent[i], rows)
        total = total + depth_next(flux_depth[i] - west * own[i])
        total = total - depth_prev(flux_depth[i] + east * own[i])
        out.append(total)
    return out


def between_planes(image, tangent, after, before, res):
    rows = image[0].shape[0]
    (state_next, next_t, sums_next), (state_prev, prev_t, sums_prev) = [
        [first_rows(values, rows) for values in plane] for plane in (after, before)
    ]
    flux_next = half_flux(state_next, sums_next, 0)
    flux_prev = half_flux(state_prev, sums_prev, 0)
    out = []
    for i in range(6):
        laplace = next_t[i] + prev_t[i] - 2.0 * tangent[i][0:rows]
        total = image[i] + (flux_next[i] - flux_prev[i])
        out.append(total - (res[0:rows] if i < 3 else viscosity) * laplace)
    return out


def precondition(ref, vector):
    rows = vector[0].shape[0]
    out = []
    for a in range(6):
        total = ref[6 * a, 0:rows] * vector[0]
        for b in range(1, 6):
            total = total + ref[6 * a + b, 0:rows] * vector[b]
        out.append(total)
    return out


def put_halo(ref, at, below, above, offset, rows):
    if rows < 4:
        ref[at, 8:16] = jnp.zeros((8, ref.shape[-1]), F32)
    ref[at, 8 : 8 + rows] = below[pl.ds(offset, rows), :]
    ref[at, 16 - rows : 16] = above[pl.ds(offset, rows), :]


def sort_slabs(outer_ref, core_ref, below, above):
    place = lax.axis_index("pol")
    even = place % 2 == 0
    edge = jnp.logical_or(place == 0, place == lax.axis_size("pol") - 1)
    from_outer = jnp.where(edge, 0.0, outer_ref[...].astype(F32))
    from_core = core_ref[...].astype(F32)
    above[...] = jnp.where(even, from_outer, from_core)
    below[...] = jnp.where(even, from_core, from_outer)


def own_plane_kernel(own_ref, t0_ref, outer_ref, core_ref, plane_ref, image_ref, below, above):
    sort_slabs(outer_ref, core_ref, below, above)
    for i in range(37):
        plane_ref[i, 0:8] = own_ref[i]
        put_halo(plane_ref, i, below, above, 48 + 2 * i, 2)
    for i in range(6):
        plane_ref[37 + i, 0:8] = own_ref[37 + i]
        put_halo(plane_ref, 37 + i, below, above, 24 + 4 * i, 4)
        plane_ref[43 + i, 0:8] = t0_ref[i]
        put_halo(plane_ref, 43 + i, below, above, 4 * i, 4)
    state = sums_of([plane_ref[37 + i] for i in range(6)])
    for i, value in enumerate(state):
        plane_ref[49 + i] = value
    tangent = [plane_ref[43 + i] for i in range(6)]
    sums = tangent_sums(state, tangent)
    for i, value in enumerate(in_plane(state, tangent, sums, around(plane_ref[36]), 16)):
        image_ref[i] = value


def krylov_kernel(
    own_ref, plane_ref, image_ref, bulk_ref, outer_ref, core_ref,
    gram_ref, t_ref, below, above, other_s,
):
    sort_slabs(outer_ref, core_ref, below, above)

    def other(field):
        pair = bulk_ref[pl.ds(16 * (field // 2), 16), :].astype(F32)
        return pair[0:8] if field % 2 == 0 else pair[8:16]

    for i in range(37):
        other_s[i, 0:8] = other(i if i < 36 else 48)
        put_halo(other_s, i, below, above, 24 + i, 1)
    for i in range(6):
        other_s[37 + i, 0:8] = other(42 + i)
        put_halo(other_s, 37 + i, below, above, 12 + 2 * i, 2)
        other_s[43 + i, 0:8] = other(36 + i)
        put_halo(other_s, 43 + i, below, above, 2 * i, 2)

    res_p, res_q = plane_ref[36], other_s[36]
    diffusion_p, diffusion_q = around(res_p), around(res_q)
    state_p = [plane_ref[49 + i] for i in range(9)]
    state_q = sums_of([other_s[37 + i] for i in range(6)])
    tang_p = [plane_ref[43 + i] for i in range(6)]
    tang_q = [other_s[43 + i] for i in range(6)]
    krylov = [[own_ref[43 + i] for i in range(6)]]
    for i in range(6):
        t_ref[i] = tang_p[i][0:8]

    def shifted(tangents, shift, earlier):
        return [t - shift * e[0 : t.shape[0]] for t, e in zip(tangents, earlier)]

    plane_p = (state_p, tang_p, tangent_sums(state_p, tang_p))
    plane_q = (state_q, tang_q, tangent_sums(state_q, tang_q))
    image_p = [image_ref[i] for i in range(6)]
    image_q = in_plane(*plane_q, diffusion_q, 16)
    image_p = between_planes(image_p, tang_p, plane_q, plane_q, res_p)
    image_q = between_planes(image_q, tang_q, plane_p, plane_p, res_q)
    krylov.append([image_p[i][0:8] - SHIFTS[0] * krylov[0][i] for i in range(6)])
    next_p = shifted(precondition(plane_ref, image_p), SHIFTS[0], tang_p)
    next_q = shifted(precondition(other_s, image_q), SHIFTS[0], tang_q)
    for i in range(6):
        t_ref[6 + i] = next_p[i][0:8]

    plane_p = (state_p, next_p, tangent_sums(state_p, next_p))
    plane_q = (state_q, next_q, tangent_sums(state_q, next_q))
    image_p = in_plane(*plane_p, diffusion_p, 16)
    image_q = in_plane(*plane_q, diffusion_q, 8)
    image_p = between_planes(image_p, next_p, plane_q, plane_q, res_p)
    image_q = between_planes(image_q, next_q, plane_p, plane_p, res_q)
    krylov.append([image_p[i][0:8] - SHIFTS[1] * krylov[1][i] for i in range(6)])
    last_p = shifted(precondition(plane_ref, image_p), SHIFTS[1], next_p)
    last_q = shifted(precondition(other_s, image_q), SHIFTS[1], next_q)
    for i in range(6):
        t_ref[12 + i] = last_p[i][0:8]

    plane_p = (state_p, last_p, tangent_sums(state_p, last_p))
    half_q = first_rows(state_q, 8)
    plane_q = (half_q, last_q, tangent_sums(half_q, last_q))
    image_p = in_plane(*plane_p, diffusion_p, 8)
    image_p = between_planes(image_p, last_p, plane_q, plane_q, res_p)
    krylov.append([image_p[i] - SHIFTS[2] * krylov[2][i] for i in range(6)])

    rows = lax.broadcasted_iota(jnp.int32, (16, 128), 0)
    lanes = lax.broadcasted_iota(jnp.int32, (16, 128), 1)
    table = jnp.zeros((16, 128), F32)
    for k, (i, j) in enumerate(PAIRS):
        total = krylov[i][0] * krylov[j][0]
        for f in range(1, 6):
            total = total + krylov[i][f] * krylov[j][f]
        line = total[:, 0:128]
        for start in range(128, total.shape[1], 128):
            line = line + total[:, start : start + 128]
        table = jnp.where(rows == k, jnp.sum(line, axis=0, keepdims=True), table)
    sums = jnp.sum(table, axis=1, keepdims=True)
    out = jnp.sum(jnp.where(rows == lanes, sums, 0.0), axis=0, keepdims=True)
    gram_ref[...] = jnp.broadcast_to(out[None], gram_ref.shape)


def finish_kernel(inverse_root, gram_ref, t_ref, update_ref, estimates_ref):
    gathered = gram_ref[...]
    sums = jnp.sum(gathered, axis=0)
    lanes = lax.broadcasted_iota(jnp.int32, sums.shape, 1)
    gram = {}
    for k, pair in enumerate(PAIRS):
        gram[pair] = jnp.sum(jnp.where(lanes == k, sums, 0.0), axis=1, keepdims=True)
    factors, estimate_list = solve_from_gram(gram)
    width = update_ref.shape[-1]
    wide = [jnp.broadcast_to(f, (8, width)) for f in factors]
    for i in range(6):
        update_ref[i] = wide[0] * t_ref[i] + wide[1] * t_ref[6 + i] + wide[2] * t_ref[12 + i]
    for k, value in enumerate(estimate_list):
        estimates_ref[k] = jnp.sum(value * inverse_root)


def two_planes(pol, plasma_state, right_side, resistivity, jacobi_blocks):
    rows, width = plasma_state.shape[2], plasma_state.shape[3]
    count = 2 * pol

    def pairs(partner):
        return [(t * pol + p, q * pol + r) for t in range(2) for p in range(pol) for q, r in [partner(t, p)]]

    def beyond(t, p, far):
        r = p - 1 if p % 2 == 0 else p + 1
        return (far, r) if 0 <= r < pol else (1 - t, p)

    across = pairs(lambda t, p: (1 - t, p))
    core = pairs(lambda t, p: (t, p ^ 1))
    outer = pairs(lambda t, p: beyond(t, p, t))
    corner = pairs(lambda t, p: beyond(t, p, 1 - t))
    across_core = pairs(lambda t, p: (1 - t, p ^ 1))

    plasma = plasma_state.reshape(6, rows, width)
    rhs = right_side.reshape(6, rows, width)
    res = resistivity.reshape(1, rows, width)
    blocks = jacobi_blocks.reshape(6, 6, rows, width)
    vmem = pl.BlockSpec(memory_space=pltpu.VMEM)
    shape = jax.ShapeDtypeStruct
    t0, own, bulk = pl.pallas_call(
        first_kernel,
        out_shape=(
            vmem_array((6, rows, width), F32),
            vmem_array((49, rows, width), F32),
            vmem_array((400, width), BF16),
        ),
        in_specs=[pl.BlockSpec(memory_space=pltpu.HBM)] * 4,
        out_specs=(vmem,) * 3,
        scratch_shapes=[pltpu.SemaphoreType.DMA((9,))],
    )(*map(in_hbm, (plasma, rhs, blocks, res)))
    bulk = lax.ppermute(bulk, AXES, across)
    slabs = (P_ROWS, P_ROWS, Q_ROWS, Q_ROWS)
    side, core_side, edge, inner = pl.pallas_call(
        pack_kernel,
        out_shape=tuple(vmem_array((size, width), BF16) for size in slabs),
        in_specs=[vmem] * 2,
        out_specs=(vmem,) * 4,
        scratch_shapes=[pltpu.VMEM((P_ROWS, width), F32), pltpu.VMEM((Q_ROWS, width), F32)],
    )(in_vmem(t0), in_vmem(own))
    outer_p = lax.ppermute(side, AXES, outer)
    core_p = lax.ppermute(core_side, AXES, core)
    outer_q = lax.ppermute(edge, AXES, corner)
    core_q = lax.ppermute(inner, AXES, across_core)
    plane, image = pl.pallas_call(
        own_plane_kernel,
        out_shape=(vmem_array((58, 16, width), F32), vmem_array((6, 16, width), F32)),
        in_specs=[vmem] * 4,
        out_specs=(vmem,) * 2,
        scratch_shapes=[pltpu.VMEM((P_ROWS, width), F32)] * 2,
        cost_estimate=pl.CostEstimate(flops=0, bytes_accessed=1_000_000, transcendentals=0),
    )(*map(in_vmem, (own, t0, outer_p, core_p)))
    gram, tangents = pl.pallas_call(
        krylov_kernel,
        out_shape=(vmem_array((count, 1, 128), F32), vmem_array((18, rows, width), F32)),
        in_specs=[vmem] * 6,
        out_specs=(vmem,) * 2,
        scratch_shapes=[pltpu.VMEM((Q_ROWS, width), F32)] * 2 + [pltpu.VMEM((49, 16, width), F32)],
    )(*map(in_vmem, (own, plane, image, bulk, outer_q, core_q)))
    gram = lax.all_to_all(gram, AXES, 0, 0, tiled=True)
    inverse_root = float((6.0 * count * rows * width) ** -0.5)
    update, estimates = pl.pallas_call(
        functools.partial(finish_kernel, inverse_root),
        out_shape=(shape((6, rows, width), F32), shape((ITERS,), F32)),
        in_specs=[vmem] * 2,
        out_specs=(vmem, pl.BlockSpec(memory_space=pltpu.SMEM)),
    )(in_vmem(gram), in_vmem(tangents))
    return update.reshape(plasma_state.shape), estimates


def padded(cells, axis, dim, closed):
    count = lax.axis_size(axis)
    ends = count if closed else count - 1
    size = cells.shape[dim]
    head = lax.slice_in_dim(cells, 0, 1, axis=dim)
    tail = lax.slice_in_dim(cells, size - 1, size, axis=dim)
    before = lax.ppermute(tail, axis, [(i, (i + 1) % count) for i in range(ends)])
    after = lax.ppermute(head, axis, [((i + 1) % count, i) for i in range(ends)])
    return jnp.concatenate([before, cells, after], axis=dim)


def any_planes(plasma_state, right_side, resistivity, jacobi_blocks):
    cell_count = right_side.size * lax.axis_size("tor") * lax.axis_size("pol")
    fixed = jnp.full((3,) + resistivity.shape, viscosity, F32)
    diffusion = jnp.concatenate([jnp.broadcast_to(resistivity[None], fixed.shape), fixed])

    def around(cells):
        planes = padded(cells.astype(BF16), "tor", 1, True).astype(F32)
        planes = jnp.concatenate([planes[:, :1], cells, planes[:, -1:]], axis=1)
        deep = jnp.pad(cells, ((0, 0), (0, 0), (0, 0), (1, 1)))
        return planes, padded(cells, "pol", 2, False), deep

    plasma_around = around(plasma_state)
    vectors, tangents = [right_side], []
    for shift in SHIFTS:
        vector = vectors[-1]
        tangent = jnp.sum(jacobi_blocks * vector[None], axis=1)
        tangents.append(tangent)
        image = inverse_step * tangent
        laplace = jnp.zeros_like(tangent)
        for direction, (plasma, cells) in enumerate(zip(plasma_around, around(tangent))):
            dim = direction + 1
            flux = jnp.stack(linear_flux(plasma, cells, direction))
            size = cells.shape[dim]
            part = functools.partial(lax.slice_in_dim, axis=dim)
            image = image + 0.5 * (part(flux, 2, size) - part(flux, 0, size - 2))
            laplace = laplace + part(cells, 2, size) + part(cells, 0, size - 2) - 2.0 * tangent
        vectors.append(image - diffusion * laplace - shift * vector)
    local = jnp.stack([jnp.sum(vectors[i] * vectors[j]) for i, j in PAIRS])
    gram = lax.psum(local, AXES)
    factors, estimate_list = solve_from_gram({pair: gram[k] for k, pair in enumerate(PAIRS)})
    update = sum(factor * tangent for factor, tangent in zip(factors, tangents))
    return update, jnp.stack(estimate_list) / jnp.sqrt(F32(cell_count))


def solution(mesh):
    tor, pol = mesh.shape["tor"], mesh.shape["pol"]

    def shards(plasma_state, right_side, resistivity, jacobi_blocks):
        _, planes, rows, width = plasma_state.shape
        fast = tor == 2 and planes == 1 and pol % 2 == 0 and rows == 8 and width % 128 == 0
        if fast:
            return two_planes(pol, plasma_state, right_side, resistivity, jacobi_blocks)
        return any_planes(plasma_state, right_side, resistivity, jacobi_blocks)

    return jax.shard_map(
        shards,
        mesh=mesh,
        in_specs=(
            P(None, "tor", "pol", None),
            P(None, "tor", "pol", None),
            P("tor", "pol", None),
            P(None, None, "tor", "pol", None),
        ),
        out_specs=(P(None, "tor", "pol", None), P()),
        check_vma=False,
    )
```

```python
import functools

import jax
import jax.numpy as jnp
from jax import lax
from jax.experimental import pallas as pl
from jax.experimental.pallas import tpu as pltpu
from jax.sharding import PartitionSpec as P

ITERS = 3
SHIFTS = (1.0, 2.0, 3.0)
inverse_step = 1.0
viscosity = 0.2
epsilon = 1e-06
AXES = ("tor", "pol")
PAIRS = [(i, j) for i in range(ITERS + 1) for j in range(i, ITERS + 1)]
BF16 = jnp.bfloat16
F32 = jnp.float32


def linear_flux(plasma, tangent, direction):
    magnetic, velocity = plasma[0:3], plasma[3:6]
    tang_mag, tang_vel = tangent[0:3], tangent[3:6]
    pressure = magnetic[0] * tang_mag[0] + magnetic[1] * tang_mag[1] + magnetic[2] * tang_mag[2]
    components = []
    for i in range(3):
        components.append(
            tang_vel[direction] * magnetic[i]
            + velocity[direction] * tang_mag[i]
            - tang_mag[direction] * velocity[i]
            - magnetic[direction] * tang_vel[i]
        )
    for i in range(3):
        moment = (
            tang_vel[direction] * velocity[i]
            + velocity[direction] * tang_vel[i]
            - tang_mag[direction] * magnetic[i]
            - magnetic[direction] * tang_mag[i]
        )
        if i == direction:
            moment = moment + pressure
        components.append(moment)
    return components


def least_squares(columns, initial_norm):
    count = len(columns)
    rhs_list = [initial_norm] + [None] * count
    cosines = []
    sines = []
    triangle = []
    estimate_list = []
    for column in range(count):
        entries = list(columns[column])
        for i in range(column):
            first_value, second_value = entries[i], entries[i + 1]
            entries[i] = cosines[i] * first_value + sines[i] * second_value
            entries[i + 1] = -sines[i] * first_value + cosines[i] * second_value
        first_value, second_value = entries[column], entries[column + 1]
        radius = jnp.sqrt(first_value * first_value + second_value * second_value)
        cosine = first_value / radius
        sine_value = second_value / radius
        cosines.append(cosine)
        sines.append(sine_value)
        entries[column] = radius
        triangle.append(entries[: column + 1])
        previous = rhs_list[column]
        rhs_list[column] = cosine * previous
        rhs_list[column + 1] = -sine_value * previous
        estimate_list.append(jnp.abs(rhs_list[column + 1]))
    weights = [None] * count
    for column in reversed(range(count)):
        partial_value = rhs_list[column]
        for later in range(column + 1, count):
            partial_value = partial_value - triangle[later][column] * weights[later]
        weights[column] = partial_value / triangle[column][column]
    return weights, estimate_list


def solve_from_gram(gram):
    count = ITERS + 1

    def inner(left, right):
        total = None
        for i in range(count):
            row = None
            for j in range(count):
                if right[j] is None:
                    continue
                term = gram[(min(i, j), max(i, j))] * right[j]
                row = term if row is None else row + term
            if left[i] is None or row is None:
                continue
            term = left[i] * row
            total = term if total is None else total + term
        return total

    def minus(left, factor, right):
        out = []
        for a, b in zip(left, right):
            if b is None:
                out.append(a)
            else:
                out.append(a - factor * b)
        return out

    initial_norm = jnp.sqrt(gram[(0, 0)] + epsilon)
    basis = [[1.0 / initial_norm] + [None] * ITERS]
    columns = []
    for column in range(ITERS):
        vector = basis[column]
        image = []
        for i in range(count):
            entry = None
            if vector[i] is not None:
                entry = SHIFTS[i] * vector[i]
            if i > 0 and vector[i - 1] is not None:
                entry = vector[i - 1] if entry is None else entry + vector[i - 1]
            image.append(entry)
        coefficients = [inner(earlier, image) for earlier in basis]
        remainder = image
        for coefficient, earlier in zip(coefficients, basis):
            remainder = minus(remainder, coefficient, earlier)
        square = jnp.maximum(inner(remainder, remainder), 0.0)
        new_norm = jnp.sqrt(square + epsilon)
        columns.append(coefficients + [new_norm])
        if column + 1 < ITERS:
            scale = 1.0 / new_norm
            basis.append([None if r is None else r * scale for r in remainder])
    weights, estimate_list = least_squares(columns, initial_norm)
    factors = []
    for k in range(ITERS):
        total = None
        for weight, vector in zip(weights, basis):
            if vector[k] is not None:
                term = weight * vector[k]
                total = term if total is None else total + term
        factors.append(total)
    return factors, estimate_list


in_vmem = functools.partial(pltpu.with_memory_space_constraint, memory_space=pltpu.VMEM)
in_hbm = functools.partial(pltpu.with_memory_space_constraint, memory_space=pltpu.HBM)
vmem_array = pltpu.VMEM
P_ROWS, Q_ROWS = 128, 64
M_ROWS = 272


def tile_rows(value, count, first):
    return jnp.where(first, value[0:count], value[8 - count : 8])


def fill_slab_q(scr, deep, wide, first):
    scr[pl.ds(Q_ROWS - 8, 8), :] = jnp.zeros((8, deep[0].shape[1]), F32)
    for f, value in enumerate(deep):
        scr[pl.ds(2 * f, 2), :] = tile_rows(value, 2, first)
    for f, value in enumerate(wide):
        scr[pl.ds(24 + f, 1), :] = tile_rows(value, 1, first)
    return scr[...].astype(BF16)


def fill_slab_p(scr, deep, wide, first):
    scr[pl.ds(P_ROWS - 8, 8), :] = jnp.zeros((8, deep[0].shape[1]), F32)
    for f, value in enumerate(deep):
        scr[pl.ds(4 * f, 4), :] = tile_rows(value, 4, first)
    for f, value in enumerate(wide):
        scr[pl.ds(48 + 2 * f, 2), :] = tile_rows(value, 2, first)
    return scr[...].astype(BF16)


def first_kernel(
    plasma_hbm, rhs_hbm, blocks_hbm, res_hbm,
    t0_ref, own_ref, ends_ref, scr, sems,
):
    copies = [
        pltpu.make_async_copy(rhs_hbm, own_ref.at[pl.ds(43, 6)], sems.at[0]),
        pltpu.make_async_copy(plasma_hbm, own_ref.at[pl.ds(37, 6)], sems.at[1]),
        pltpu.make_async_copy(res_hbm, own_ref.at[pl.ds(36, 1)], sems.at[2]),
    ] + [pltpu.make_async_copy(blocks_hbm.at[a], own_ref.at[pl.ds(6 * a, 6)], sems.at[3 + a]) for a in range(6)]
    for copy in copies:
        copy.start()
    for copy in copies[:3]:
        copy.wait()
    vector = [own_ref[43 + b] for b in range(6)]
    t0 = []
    for a in range(6):
        copies[3 + a].wait()
        total = own_ref[6 * a] * vector[0]
        for b in range(1, 6):
            total = total + own_ref[6 * a + b] * vector[b]
        t0_ref[a] = total
        t0.append(total)
    deep = t0 + [own_ref[37 + i] for i in range(6)]
    wide = [own_ref[i] for i in range(37)]
    even = lax.axis_index("pol") % 2 == 0
    ends_ref[pl.ds(0, Q_ROWS), :] = fill_slab_q(scr, deep, wide, even)
    ends_ref[pl.ds(Q_ROWS, Q_ROWS), :] = fill_slab_q(scr, deep, wide, jnp.logical_not(even))


def pack_kernel(t0_ref, own_ref, middle_ref, side_ref, core_ref, scr, scr_m):
    even = lax.axis_index("pol") % 2 == 0
    deep = [t0_ref[i] for i in range(6)] + [own_ref[37 + i] for i in range(6)]
    wide = [own_ref[i] for i in range(37)]
    side_ref[...] = fill_slab_p(scr, deep, wide, even)
    core_ref[...] = fill_slab_p(scr, deep, wide, jnp.logical_not(even))
    scr_m[pl.ds(M_ROWS - 8, 8), :] = jnp.zeros((8, scr_m.shape[1]), F32)
    for f, value in enumerate(deep):
        scr_m[pl.ds(4 * f, 4), :] = value[2:6]
    for f, value in enumerate(wide):
        scr_m[pl.ds(48 + 6 * f, 6), :] = value[1:7]
    middle_ref[...] = scr_m[...].astype(BF16)


def depth_next(x):
    width = x.shape[1]
    lanes = lax.broadcasted_iota(jnp.int32, x.shape, 1)
    return jnp.where(lanes == width - 1, 0.0, pltpu.roll(x, width - 1, 1))


def depth_prev(x):
    lanes = lax.broadcasted_iota(jnp.int32, x.shape, 1)
    return jnp.where(lanes == 0, 0.0, pltpu.roll(x, 1, 1))


def sums_of(plasma):
    magnetic, velocity = plasma[0:3], plasma[3:6]
    return (
        [0.25 * (v + b) for v, b in zip(velocity, magnetic)]
        + [0.25 * (v - b) for v, b in zip(velocity, magnetic)]
        + [0.5 * b for b in magnetic]
    )


def tangent_sums(state, tangent):
    tang_mag, tang_vel = tangent[0:3], tangent[3:6]
    half_pressure = state[6] * tang_mag[0] + state[7] * tang_mag[1] + state[8] * tang_mag[2]
    return (
        [w + b for w, b in zip(tang_vel, tang_mag)]
        + [w - b for w, b in zip(tang_vel, tang_mag)]
        + [half_pressure]
    )


def first_rows(values, rows):
    return [x[0:rows] for x in values]


def half_flux(state, sums, k):
    magnetic, velocity = [], []
    for i in range(3):
        plus = sums[3 + k] * state[i] + state[3 + k] * sums[i]
        minus = sums[k] * state[3 + i] + state[k] * sums[3 + i]
        magnetic.append(plus - minus)
        velocity.append(plus + minus + sums[6] if i == k else plus + minus)
    return magnetic + velocity


def row_next(x, rows):
    if rows == 16:
        return pltpu.roll(x, 15, 0)
    own = x[0:8]
    sublanes = lax.broadcasted_iota(jnp.int32, own.shape, 0)
    return pltpu.roll(jnp.where(sublanes == 0, x[8:16], own), 7, 0)


def row_prev(x, rows):
    if rows == 16:
        return pltpu.roll(x, 1, 0)
    own = x[0:8]
    sublanes = lax.broadcasted_iota(jnp.int32, own.shape, 0)
    return pltpu.roll(jnp.where(sublanes == 7, x[8:16], own), 1, 0)


def around(res):
    return res, row_prev(res, 16), row_next(res, 16), depth_prev(res), depth_next(res)


def in_plane(state, tangent, sums, diffusion, rows):
    flux_rows = half_flux(state, sums, 1)
    own = first_rows(tangent, rows)
    flux_depth = half_flux(first_rows(state, rows), first_rows(sums, rows), 2)
    out = []
    for i in range(6):
        here, above, below, west, east = diffusion if i < 3 else (viscosity,) * 5
        if i < 3:
            here, west, east = first_rows((here, west, east), rows)
        total = (inverse_step + 4.0 * here) * own[i]
        total = total + row_next(flux_rows[i] - above * tangent[i], rows)
        total = total - row_prev(flux_rows[i] + below * tangent[i], rows)
        total = total + depth_next(flux_depth[i] - west * own[i])
        total = total - depth_prev(flux_depth[i] + east * own[i])
        out.append(total)
    return out


def between_planes(image, tangent, after, before, res):
    rows = image[0].shape[0]
    (state_next, next_t, sums_next), (state_prev, prev_t, sums_prev) = [
        [first_rows(values, rows) for values in plane] for plane in (after, before)
    ]
    flux_next = half_flux(state_next, sums_next, 0)
    flux_prev = half_flux(state_prev, sums_prev, 0)
    out = []
    for i in range(6):
        laplace = next_t[i] + prev_t[i] - 2.0 * tangent[i][0:rows]
        total = image[i] + (flux_next[i] - flux_prev[i])
        out.append(total - (res[0:rows] if i < 3 else viscosity) * laplace)
    return out


def precondition(ref, vector):
    rows = vector[0].shape[0]
    out = []
    for a in range(6):
        total = ref[6 * a, 0:rows] * vector[0]
        for b in range(1, 6):
            total = total + ref[6 * a + b, 0:rows] * vector[b]
        out.append(total)
    return out


def put_halo(ref, at, below, above, offset, rows):
    if rows < 4:
        ref[at, 8:16] = jnp.zeros((8, ref.shape[-1]), F32)
    ref[at, 8 : 8 + rows] = below[pl.ds(offset, rows), :]
    ref[at, 16 - rows : 16] = above[pl.ds(offset, rows), :]


def sort_slabs(outer_ref, core_ref, below, above):
    place = lax.axis_index("pol")
    even = place % 2 == 0
    edge = jnp.logical_or(place == 0, place == lax.axis_size("pol") - 1)
    from_outer = jnp.where(edge, 0.0, outer_ref[...].astype(F32))
    from_core = core_ref[...].astype(F32)
    above[...] = jnp.where(even, from_outer, from_core)
    below[...] = jnp.where(even, from_core, from_outer)


def own_plane_kernel(own_ref, t0_ref, outer_ref, core_ref, plane_ref, image_ref, below, above):
    sort_slabs(outer_ref, core_ref, below, above)
    for i in range(37):
        plane_ref[i, 0:8] = own_ref[i]
        put_halo(plane_ref, i, below, above, 48 + 2 * i, 2)
    for i in range(6):
        plane_ref[37 + i, 0:8] = own_ref[37 + i]
        put_halo(plane_ref, 37 + i, below, above, 24 + 4 * i, 4)
        plane_ref[43 + i, 0:8] = t0_ref[i]
        put_halo(plane_ref, 43 + i, below, above, 4 * i, 4)
    state = sums_of([plane_ref[37 + i] for i in range(6)])
    for i, value in enumerate(state):
        plane_ref[49 + i] = value
    tangent = [plane_ref[43 + i] for i in range(6)]
    sums = tangent_sums(state, tangent)
    for i, value in enumerate(in_plane(state, tangent, sums, around(plane_ref[36]), 16)):
        image_ref[i] = value


def other_plane_kernel(middle_ref, ends_ref, other_ref, scr_e, scr_m):
    even = lax.axis_index("pol") % 2 == 0
    outer, inner = ends_ref[pl.ds(0, Q_ROWS), :].astype(F32), ends_ref[pl.ds(Q_ROWS, Q_ROWS), :].astype(F32)
    scr_e[pl.ds(0, Q_ROWS), :] = jnp.where(even, outer, inner)
    scr_e[pl.ds(Q_ROWS, Q_ROWS), :] = jnp.where(even, inner, outer)
    scr_m[...] = middle_ref[...].astype(F32)
    for f in range(12):
        at = 43 + f if f < 6 else 31 + f
        other_ref[at, 0:2] = scr_e[pl.ds(2 * f, 2), :]
        other_ref[at, 2:6] = scr_m[pl.ds(4 * f, 4), :]
        other_ref[at, 6:8] = scr_e[pl.ds(Q_ROWS + 2 * f, 2), :]
    for i in range(37):
        other_ref[i, 0:1] = scr_e[pl.ds(24 + i, 1), :]
        other_ref[i, 1:7] = scr_m[pl.ds(48 + 6 * i, 6), :]
        other_ref[i, 7:8] = scr_e[pl.ds(Q_ROWS + 24 + i, 1), :]


def krylov_kernel(
    own_ref, plane_ref, image_ref, other_ref, outer_ref, core_ref,
    gram_ref, t_ref, below, above, other_s,
):
    sort_slabs(outer_ref, core_ref, below, above)

    for i in range(49):
        other_s[i, 0:8] = other_ref[i]
        if i < 37:
            put_halo(other_s, i, below, above, 24 + i, 1)
        else:
            put_halo(other_s, i, below, above, 2 * (i - 31) if i < 43 else 2 * (i - 43), 2)

    res_p, res_q = plane_ref[36], other_s[36]
    diffusion_p, diffusion_q = around(res_p), around(res_q)
    state_p = [plane_ref[49 + i] for i in range(9)]
    state_q = sums_of([other_s[37 + i] for i in range(6)])
    tang_p = [plane_ref[43 + i] for i in range(6)]
    tang_q = [other_s[43 + i] for i in range(6)]
    krylov = [[own_ref[43 + i] for i in range(6)]]
    for i in range(6):
        t_ref[i] = tang_p[i][0:8]

    def shifted(tangents, shift, earlier):
        return [t - shift * e[0 : t.shape[0]] for t, e in zip(tangents, earlier)]

    plane_p = (state_p, tang_p, tangent_sums(state_p, tang_p))
    plane_q = (state_q, tang_q, tangent_sums(state_q, tang_q))
    image_p = [image_ref[i] for i in range(6)]
    image_q = in_plane(*plane_q, diffusion_q, 16)
    image_p = between_planes(image_p, tang_p, plane_q, plane_q, res_p)
    image_q = between_planes(image_q, tang_q, plane_p, plane_p, res_q)
    krylov.append([image_p[i][0:8] - SHIFTS[0] * krylov[0][i] for i in range(6)])
    next_p = shifted(precondition(plane_ref, image_p), SHIFTS[0], tang_p)
    next_q = shifted(precondition(other_s, image_q), SHIFTS[0], tang_q)
    for i in range(6):
        t_ref[6 + i] = next_p[i][0:8]

    plane_p = (state_p, next_p, tangent_sums(state_p, next_p))
    plane_q = (state_q, next_q, tangent_sums(state_q, next_q))
    image_p = in_plane(*plane_p, diffusion_p, 16)
    image_q = in_plane(*plane_q, diffusion_q, 8)
    image_p = between_planes(image_p, next_p, plane_q, plane_q, res_p)
    image_q = between_planes(image_q, next_q, plane_p, plane_p, res_q)
    krylov.append([image_p[i][0:8] - SHIFTS[1] * krylov[1][i] for i in range(6)])
    last_p = shifted(precondition(plane_ref, image_p), SHIFTS[1], next_p)
    last_q = shifted(precondition(other_s, image_q), SHIFTS[1], next_q)
    for i in range(6):
        t_ref[12 + i] = last_p[i][0:8]

    plane_p = (state_p, last_p, tangent_sums(state_p, last_p))
    half_q = first_rows(state_q, 8)
    plane_q = (half_q, last_q, tangent_sums(half_q, last_q))
    image_p = in_plane(*plane_p, diffusion_p, 8)
    image_p = between_planes(image_p, last_p, plane_q, plane_q, res_p)
    krylov.append([image_p[i] - SHIFTS[2] * krylov[2][i] for i in range(6)])

    rows = lax.broadcasted_iota(jnp.int32, (16, 128), 0)
    lanes = lax.broadcasted_iota(jnp.int32, (16, 128), 1)
    table = jnp.zeros((16, 128), F32)
    for k, (i, j) in enumerate(PAIRS):
        total = krylov[i][0] * krylov[j][0]
        for f in range(1, 6):
            total = total + krylov[i][f] * krylov[j][f]
        line = total[:, 0:128]
        for start in range(128, total.shape[1], 128):
            line = line + total[:, start : start + 128]
        table = jnp.where(rows == k, jnp.sum(line, axis=0, keepdims=True), table)
    sums = jnp.sum(table, axis=1, keepdims=True)
    out = jnp.sum(jnp.where(rows == lanes, sums, 0.0), axis=0, keepdims=True)
    gram_ref[...] = jnp.broadcast_to(out[None], gram_ref.shape)


def finish_kernel(inverse_root, gram_ref, t_ref, update_ref, estimates_ref):
    gathered = gram_ref[...]
    sums = jnp.sum(gathered, axis=0)
    lanes = lax.broadcasted_iota(jnp.int32, sums.shape, 1)
    gram = {}
    for k, pair in enumerate(PAIRS):
        gram[pair] = jnp.sum(jnp.where(lanes == k, sums, 0.0), axis=1, keepdims=True)
    factors, estimate_list = solve_from_gram(gram)
    width = update_ref.shape[-1]
    wide = [jnp.broadcast_to(f, (8, width)) for f in factors]
    for i in range(6):
        update_ref[i] = wide[0] * t_ref[i] + wide[1] * t_ref[6 + i] + wide[2] * t_ref[12 + i]
    for k, value in enumerate(estimate_list):
        estimates_ref[k] = jnp.sum(value * inverse_root)


def two_planes(pol, plasma_state, right_side, resistivity, jacobi_blocks):
    rows, width = plasma_state.shape[2], plasma_state.shape[3]
    count = 2 * pol

    def pairs(partner):
        return [(t * pol + p, q * pol + r) for t in range(2) for p in range(pol) for q, r in [partner(t, p)]]

    def beyond(t, p, far):
        r = p - 1 if p % 2 == 0 else p + 1
        return (far, r) if 0 <= r < pol else (1 - t, p)

    across = pairs(lambda t, p: (1 - t, p))
    core = pairs(lambda t, p: (t, p ^ 1))
    outer = pairs(lambda t, p: beyond(t, p, t))
    corner = pairs(lambda t, p: beyond(t, p, 1 - t))

    plasma = plasma_state.reshape(6, rows, width)
    rhs = right_side.reshape(6, rows, width)
    res = resistivity.reshape(1, rows, width)
    blocks = jacobi_blocks.reshape(6, 6, rows, width)
    vmem = pl.BlockSpec(memory_space=pltpu.VMEM)
    shape = jax.ShapeDtypeStruct
    t0, own, ends = pl.pallas_call(
        first_kernel,
        out_shape=(
            vmem_array((6, rows, width), F32),
            vmem_array((49, rows, width), F32),
            vmem_array((2 * Q_ROWS, width), BF16),
        ),
        in_specs=[pl.BlockSpec(memory_space=pltpu.HBM)] * 4,
        out_specs=(vmem,) * 3,
        scratch_shapes=[pltpu.VMEM((Q_ROWS, width), F32), pltpu.SemaphoreType.DMA((9,))],
    )(*map(in_hbm, (plasma, rhs, blocks, res)))
    edge = ends[:Q_ROWS]
    ends = lax.ppermute(ends, AXES, across)
    slabs = (M_ROWS, P_ROWS, P_ROWS)
    middle, side, core_side = pl.pallas_call(
        pack_kernel,
        out_shape=tuple(vmem_array((size, width), BF16) for size in slabs),
        in_specs=[vmem] * 2,
        out_specs=(vmem,) * 3,
        scratch_shapes=[pltpu.VMEM((P_ROWS, width), F32), pltpu.VMEM((M_ROWS, width), F32)],
    )(in_vmem(t0), in_vmem(own))
    middle = lax.ppermute(middle, AXES, across)
    outer_p = lax.ppermute(side, AXES, outer)
    core_p = lax.ppermute(core_side, AXES, core)
    outer_q = lax.ppermute(edge, AXES, corner)
    core_q = lax.ppermute(ends[Q_ROWS:], AXES, core)
    other = pl.pallas_call(
        other_plane_kernel,
        out_shape=vmem_array((49, rows, width), F32),
        in_specs=[vmem] * 2,
        out_specs=vmem,
        scratch_shapes=[pltpu.VMEM((2 * Q_ROWS, width), F32), pltpu.VMEM((M_ROWS, width), F32)],
        cost_estimate=pl.CostEstimate(flops=0, bytes_accessed=1_000_000, transcendentals=0),
    )(in_vmem(middle), in_vmem(ends))
    plane, image = pl.pallas_call(
        own_plane_kernel,
        out_shape=(vmem_array((58, 16, width), F32), vmem_array((6, 16, width), F32)),
        in_specs=[vmem] * 4,
        out_specs=(vmem,) * 2,
        scratch_shapes=[pltpu.VMEM((P_ROWS, width), F32)] * 2,
        cost_estimate=pl.CostEstimate(flops=1000000000, bytes_accessed=1_000_000, transcendentals=0),
    )(*map(in_vmem, (own, t0, outer_p, core_p)))
    gram, tangents = pl.pallas_call(
        krylov_kernel,
        out_shape=(vmem_array((count, 1, 128), F32), vmem_array((18, rows, width), F32)),
        in_specs=[vmem] * 6,
        out_specs=(vmem,) * 2,
        scratch_shapes=[pltpu.VMEM((Q_ROWS, width), F32)] * 2 + [pltpu.VMEM((49, 16, width), F32)],
    )(*map(in_vmem, (own, plane, image, other, outer_q, core_q)))
    gram = lax.all_to_all(gram, AXES, 0, 0, tiled=True)
    inverse_root = float((6.0 * count * rows * width) ** -0.5)
    update, estimates = pl.pallas_call(
        functools.partial(finish_kernel, inverse_root),
        out_shape=(shape((6, rows, width), F32), shape((ITERS,), F32)),
        in_specs=[vmem] * 2,
        out_specs=(vmem, pl.BlockSpec(memory_space=pltpu.SMEM)),
    )(in_vmem(gram), in_vmem(tangents))
    return update.reshape(plasma_state.shape), estimates


def padded(cells, axis, dim, closed):
    count = lax.axis_size(axis)
    ends = count if closed else count - 1
    size = cells.shape[dim]
    head = lax.slice_in_dim(cells, 0, 1, axis=dim)
    tail = lax.slice_in_dim(cells, size - 1, size, axis=dim)
    before = lax.ppermute(tail, axis, [(i, (i + 1) % count) for i in range(ends)])
    after = lax.ppermute(head, axis, [((i + 1) % count, i) for i in range(ends)])
    return jnp.concatenate([before, cells, after], axis=dim)


def any_planes(plasma_state, right_side, resistivity, jacobi_blocks):
    cell_count = right_side.size * lax.axis_size("tor") * lax.axis_size("pol")
    fixed = jnp.full((3,) + resistivity.shape, viscosity, F32)
    diffusion = jnp.concatenate([jnp.broadcast_to(resistivity[None], fixed.shape), fixed])

    def around(cells):
        planes = padded(cells.astype(BF16), "tor", 1, True).astype(F32)
        planes = jnp.concatenate([planes[:, :1], cells, planes[:, -1:]], axis=1)
        deep = jnp.pad(cells, ((0, 0), (0, 0), (0, 0), (1, 1)))
        return planes, padded(cells, "pol", 2, False), deep

    plasma_around = around(plasma_state)
    vectors, tangents = [right_side], []
    for shift in SHIFTS:
        vector = vectors[-1]
        tangent = jnp.sum(jacobi_blocks * vector[None], axis=1)
        tangents.append(tangent)
        image = inverse_step * tangent
        laplace = jnp.zeros_like(tangent)
        for direction, (plasma, cells) in enumerate(zip(plasma_around, around(tangent))):
            dim = direction + 1
            flux = jnp.stack(linear_flux(plasma, cells, direction))
            size = cells.shape[dim]
            part = functools.partial(lax.slice_in_dim, axis=dim)
            image = image + 0.5 * (part(flux, 2, size) - part(flux, 0, size - 2))
            laplace = laplace + part(cells, 2, size) + part(cells, 0, size - 2) - 2.0 * tangent
        vectors.append(image - diffusion * laplace - shift * vector)
    local = jnp.stack([jnp.sum(vectors[i] * vectors[j]) for i, j in PAIRS])
    gram = lax.psum(local, AXES)
    factors, estimate_list = solve_from_gram({pair: gram[k] for k, pair in enumerate(PAIRS)})
    update = sum(factor * tangent for factor, tangent in zip(factors, tangents))
    return update, jnp.stack(estimate_list) / jnp.sqrt(F32(cell_count))


def solution(mesh):
    tor, pol = mesh.shape["tor"], mesh.shape["pol"]

    def shards(plasma_state, right_side, resistivity, jacobi_blocks):
        _, planes, rows, width = plasma_state.shape
        fast = tor == 2 and planes == 1 and pol % 2 == 0 and rows == 8 and width % 128 == 0
        if fast:
            return two_planes(pol, plasma_state, right_side, resistivity, jacobi_blocks)
        return any_planes(plasma_state, right_side, resistivity, jacobi_blocks)

    return jax.shard_map(
        shards,
        mesh=mesh,
        in_specs=(
            P(None, "tor", "pol", None),
            P(None, "tor", "pol", None),
            P("tor", "pol", None),
            P(None, None, "tor", "pol", None),
        ),
        out_specs=(P(None, "tor", "pol", None), P()),
        check_vma=False,
    )
```

```python
import functools

import jax
import jax.numpy as jnp
from jax import lax
from jax.experimental import pallas as pl
from jax.experimental.pallas import tpu as pltpu
from jax.sharding import PartitionSpec as P

ITERS = 3
SHIFTS = (1.0, 2.0, 3.0)
inverse_step = 1.0
viscosity = 0.2
epsilon = 1e-06
AXES = ("tor", "pol")
PAIRS = [(i, j) for i in range(ITERS + 1) for j in range(i, ITERS + 1)]
BF16 = jnp.bfloat16
F32 = jnp.float32


def linear_flux(plasma, tangent, direction):
    magnetic, velocity = plasma[0:3], plasma[3:6]
    tang_mag, tang_vel = tangent[0:3], tangent[3:6]
    pressure = magnetic[0] * tang_mag[0] + magnetic[1] * tang_mag[1] + magnetic[2] * tang_mag[2]
    components = []
    for i in range(3):
        components.append(
            tang_vel[direction] * magnetic[i]
            + velocity[direction] * tang_mag[i]
            - tang_mag[direction] * velocity[i]
            - magnetic[direction] * tang_vel[i]
        )
    for i in range(3):
        moment = (
            tang_vel[direction] * velocity[i]
            + velocity[direction] * tang_vel[i]
            - tang_mag[direction] * magnetic[i]
            - magnetic[direction] * tang_mag[i]
        )
        if i == direction:
            moment = moment + pressure
        components.append(moment)
    return components


def least_squares(columns, initial_norm):
    count = len(columns)
    rhs_list = [initial_norm] + [None] * count
    cosines = []
    sines = []
    triangle = []
    estimate_list = []
    for column in range(count):
        entries = list(columns[column])
        for i in range(column):
            first_value, second_value = entries[i], entries[i + 1]
            entries[i] = cosines[i] * first_value + sines[i] * second_value
            entries[i + 1] = -sines[i] * first_value + cosines[i] * second_value
        first_value, second_value = entries[column], entries[column + 1]
        radius = jnp.sqrt(first_value * first_value + second_value * second_value)
        cosine = first_value / radius
        sine_value = second_value / radius
        cosines.append(cosine)
        sines.append(sine_value)
        entries[column] = radius
        triangle.append(entries[: column + 1])
        previous = rhs_list[column]
        rhs_list[column] = cosine * previous
        rhs_list[column + 1] = -sine_value * previous
        estimate_list.append(jnp.abs(rhs_list[column + 1]))
    weights = [None] * count
    for column in reversed(range(count)):
        partial_value = rhs_list[column]
        for later in range(column + 1, count):
            partial_value = partial_value - triangle[later][column] * weights[later]
        weights[column] = partial_value / triangle[column][column]
    return weights, estimate_list


def solve_from_gram(gram):
    count = ITERS + 1

    def inner(left, right):
        total = None
        for i in range(count):
            row = None
            for j in range(count):
                if right[j] is None:
                    continue
                term = gram[(min(i, j), max(i, j))] * right[j]
                row = term if row is None else row + term
            if left[i] is None or row is None:
                continue
            term = left[i] * row
            total = term if total is None else total + term
        return total

    def minus(left, factor, right):
        out = []
        for a, b in zip(left, right):
            if b is None:
                out.append(a)
            else:
                out.append(a - factor * b)
        return out

    initial_norm = jnp.sqrt(gram[(0, 0)] + epsilon)
    basis = [[1.0 / initial_norm] + [None] * ITERS]
    columns = []
    for column in range(ITERS):
        vector = basis[column]
        image = []
        for i in range(count):
            entry = None
            if vector[i] is not None:
                entry = SHIFTS[i] * vector[i]
            if i > 0 and vector[i - 1] is not None:
                entry = vector[i - 1] if entry is None else entry + vector[i - 1]
            image.append(entry)
        coefficients = [inner(earlier, image) for earlier in basis]
        remainder = image
        for coefficient, earlier in zip(coefficients, basis):
            remainder = minus(remainder, coefficient, earlier)
        square = jnp.maximum(inner(remainder, remainder), 0.0)
        new_norm = jnp.sqrt(square + epsilon)
        columns.append(coefficients + [new_norm])
        if column + 1 < ITERS:
            scale = 1.0 / new_norm
            basis.append([None if r is None else r * scale for r in remainder])
    weights, estimate_list = least_squares(columns, initial_norm)
    factors = []
    for k in range(ITERS):
        total = None
        for weight, vector in zip(weights, basis):
            if vector[k] is not None:
                term = weight * vector[k]
                total = term if total is None else total + term
        factors.append(total)
    return factors, estimate_list


in_vmem = functools.partial(pltpu.with_memory_space_constraint, memory_space=pltpu.VMEM)
in_hbm = functools.partial(pltpu.with_memory_space_constraint, memory_space=pltpu.HBM)
vmem_array = pltpu.VMEM
P_ROWS, Q_ROWS = 128, 64
M_ROWS = 272


def tile_rows(value, count, first):
    return jnp.where(first, value[0:count], value[8 - count : 8])


def fill_slab_q(scr, deep, wide, first):
    scr[pl.ds(Q_ROWS - 8, 8), :] = jnp.zeros((8, deep[0].shape[1]), F32)
    for f, value in enumerate(deep):
        scr[pl.ds(2 * f, 2), :] = tile_rows(value, 2, first)
    for f, value in enumerate(wide):
        scr[pl.ds(24 + f, 1), :] = tile_rows(value, 1, first)
    return scr[...].astype(BF16)


def fill_slab_p(scr, deep, wide, first):
    scr[pl.ds(P_ROWS - 8, 8), :] = jnp.zeros((8, deep[0].shape[1]), F32)
    for f, value in enumerate(deep):
        scr[pl.ds(4 * f, 4), :] = tile_rows(value, 4, first)
    for f, value in enumerate(wide):
        scr[pl.ds(48 + 2 * f, 2), :] = tile_rows(value, 2, first)
    return scr[...].astype(BF16)


def first_kernel(
    plasma_hbm, rhs_hbm, blocks_hbm, res_hbm,
    t0_ref, own_ref, ends_ref, scr, sems,
):
    copies = [
        pltpu.make_async_copy(rhs_hbm, own_ref.at[pl.ds(43, 6)], sems.at[0]),
        pltpu.make_async_copy(plasma_hbm, own_ref.at[pl.ds(37, 6)], sems.at[1]),
        pltpu.make_async_copy(res_hbm, own_ref.at[pl.ds(36, 1)], sems.at[2]),
    ] + [pltpu.make_async_copy(blocks_hbm.at[a], own_ref.at[pl.ds(6 * a, 6)], sems.at[3 + a]) for a in range(6)]
    for copy in copies:
        copy.start()
    for copy in copies[:3]:
        copy.wait()
    vector = [own_ref[43 + b] for b in range(6)]
    t0 = []
    for a in range(6):
        copies[3 + a].wait()
        total = own_ref[6 * a] * vector[0]
        for b in range(1, 6):
            total = total + own_ref[6 * a + b] * vector[b]
        t0_ref[a] = total
        t0.append(total)
    deep = t0 + [own_ref[37 + i] for i in range(6)]
    wide = [own_ref[i] for i in range(37)]
    even = lax.axis_index("pol") % 2 == 0
    ends_ref[pl.ds(0, Q_ROWS), :] = fill_slab_q(scr, deep, wide, even)
    ends_ref[pl.ds(Q_ROWS, Q_ROWS), :] = fill_slab_q(scr, deep, wide, jnp.logical_not(even))


def middle_kernel(t0_ref, own_ref, middle_ref, scr_m):
    deep = [t0_ref[i] for i in range(6)] + [own_ref[37 + i] for i in range(6)]
    wide = [own_ref[i] for i in range(37)]
    scr_m[pl.ds(M_ROWS - 8, 8), :] = jnp.zeros((8, scr_m.shape[1]), F32)
    for f, value in enumerate(deep):
        scr_m[pl.ds(4 * f, 4), :] = value[2:6]
    for f, value in enumerate(wide):
        scr_m[pl.ds(48 + 6 * f, 6), :] = value[1:7]
    middle_ref[...] = scr_m[...].astype(BF16)


def pack_kernel(t0_ref, own_ref, side_ref, core_ref, scr):
    even = lax.axis_index("pol") % 2 == 0
    deep = [t0_ref[i] for i in range(6)] + [own_ref[37 + i] for i in range(6)]
    wide = [own_ref[i] for i in range(37)]
    side_ref[...] = fill_slab_p(scr, deep, wide, even)
    core_ref[...] = fill_slab_p(scr, deep, wide, jnp.logical_not(even))


def depth_next(x):
    width = x.shape[1]
    lanes = lax.broadcasted_iota(jnp.int32, x.shape, 1)
    return jnp.where(lanes == width - 1, 0.0, pltpu.roll(x, width - 1, 1))


def depth_prev(x):
    lanes = lax.broadcasted_iota(jnp.int32, x.shape, 1)
    return jnp.where(lanes == 0, 0.0, pltpu.roll(x, 1, 1))


def sums_of(plasma):
    magnetic, velocity = plasma[0:3], plasma[3:6]
    return (
        [0.25 * (v + b) for v, b in zip(velocity, magnetic)]
        + [0.25 * (v - b) for v, b in zip(velocity, magnetic)]
        + [0.5 * b for b in magnetic]
    )


def tangent_sums(state, tangent):
    tang_mag, tang_vel = tangent[0:3], tangent[3:6]
    half_pressure = state[6] * tang_mag[0] + state[7] * tang_mag[1] + state[8] * tang_mag[2]
    return (
        [w + b for w, b in zip(tang_vel, tang_mag)]
        + [w - b for w, b in zip(tang_vel, tang_mag)]
        + [half_pressure]
    )


def first_rows(values, rows):
    return [x[0:rows] for x in values]


def half_flux(state, sums, k):
    magnetic, velocity = [], []
    for i in range(3):
        plus = sums[3 + k] * state[i] + state[3 + k] * sums[i]
        minus = sums[k] * state[3 + i] + state[k] * sums[3 + i]
        magnetic.append(plus - minus)
        velocity.append(plus + minus + sums[6] if i == k else plus + minus)
    return magnetic + velocity


def row_next(x, rows):
    if rows == 16:
        return pltpu.roll(x, 15, 0)
    own = x[0:8]
    sublanes = lax.broadcasted_iota(jnp.int32, own.shape, 0)
    return pltpu.roll(jnp.where(sublanes == 0, x[8:16], own), 7, 0)


def row_prev(x, rows):
    if rows == 16:
        return pltpu.roll(x, 1, 0)
    own = x[0:8]
    sublanes = lax.broadcasted_iota(jnp.int32, own.shape, 0)
    return pltpu.roll(jnp.where(sublanes == 7, x[8:16], own), 1, 0)


def around(res):
    return res, row_prev(res, 16), row_next(res, 16), depth_prev(res), depth_next(res)


def in_plane(state, tangent, sums, diffusion, rows):
    flux_rows = half_flux(state, sums, 1)
    own = first_rows(tangent, rows)
    flux_depth = half_flux(first_rows(state, rows), first_rows(sums, rows), 2)
    out = []
    for i in range(6):
        here, above, below, west, east = diffusion if i < 3 else (viscosity,) * 5
        if i < 3:
            here, west, east = first_rows((here, west, east), rows)
        total = (inverse_step + 4.0 * here) * own[i]
        total = total + row_next(flux_rows[i] - above * tangent[i], rows)
        total = total - row_prev(flux_rows[i] + below * tangent[i], rows)
        total = total + depth_next(flux_depth[i] - west * own[i])
        total = total - depth_prev(flux_depth[i] + east * own[i])
        out.append(total)
    return out


def between_planes(image, tangent, after, before, res):
    rows = image[0].shape[0]
    (state_next, next_t, sums_next), (state_prev, prev_t, sums_prev) = [
        [first_rows(values, rows) for values in plane] for plane in (after, before)
    ]
    flux_next = half_flux(state_next, sums_next, 0)
    flux_prev = half_flux(state_prev, sums_prev, 0)
    out = []
    for i in range(6):
        laplace = next_t[i] + prev_t[i] - 2.0 * tangent[i][0:rows]
        total = image[i] + (flux_next[i] - flux_prev[i])
        out.append(total - (res[0:rows] if i < 3 else viscosity) * laplace)
    return out


def precondition(ref, vector):
    rows = vector[0].shape[0]
    out = []
    for a in range(6):
        total = ref[6 * a, 0:rows] * vector[0]
        for b in range(1, 6):
            total = total + ref[6 * a + b, 0:rows] * vector[b]
        out.append(total)
    return out


def put_halo(ref, at, below, above, offset, rows):
    if rows < 4:
        ref[at, 8:16] = jnp.zeros((8, ref.shape[-1]), F32)
    ref[at, 8 : 8 + rows] = below[pl.ds(offset, rows), :]
    ref[at, 16 - rows : 16] = above[pl.ds(offset, rows), :]


def sort_slabs(outer_ref, core_ref, below, above):
    place = lax.axis_index("pol")
    even = place % 2 == 0
    edge = jnp.logical_or(place == 0, place == lax.axis_size("pol") - 1)
    from_outer = jnp.where(edge, 0.0, outer_ref[...].astype(F32))
    from_core = core_ref[...].astype(F32)
    above[...] = jnp.where(even, from_outer, from_core)
    below[...] = jnp.where(even, from_core, from_outer)


def own_plane_kernel(own_ref, t0_ref, outer_ref, core_ref, plane_ref, image_ref, below, above):
    sort_slabs(outer_ref, core_ref, below, above)
    for i in range(37):
        plane_ref[i, 0:8] = own_ref[i]
        put_halo(plane_ref, i, below, above, 48 + 2 * i, 2)
    for i in range(6):
        plane_ref[37 + i, 0:8] = own_ref[37 + i]
        put_halo(plane_ref, 37 + i, below, above, 24 + 4 * i, 4)
        plane_ref[43 + i, 0:8] = t0_ref[i]
        put_halo(plane_ref, 43 + i, below, above, 4 * i, 4)
    state = sums_of([plane_ref[37 + i] for i in range(6)])
    for i, value in enumerate(state):
        plane_ref[49 + i] = value
    tangent = [plane_ref[43 + i] for i in range(6)]
    sums = tangent_sums(state, tangent)
    for i, value in enumerate(in_plane(state, tangent, sums, around(plane_ref[36]), 16)):
        image_ref[i] = value


def other_plane_kernel(middle_ref, ends_ref, other_ref, scr_e, scr_m):
    even = lax.axis_index("pol") % 2 == 0
    outer, inner = ends_ref[pl.ds(0, Q_ROWS), :].astype(F32), ends_ref[pl.ds(Q_ROWS, Q_ROWS), :].astype(F32)
    scr_e[pl.ds(0, Q_ROWS), :] = jnp.where(even, outer, inner)
    scr_e[pl.ds(Q_ROWS, Q_ROWS), :] = jnp.where(even, inner, outer)
    scr_m[...] = middle_ref[...].astype(F32)
    for f in range(12):
        at = 43 + f if f < 6 else 31 + f
        other_ref[at, 0:2] = scr_e[pl.ds(2 * f, 2), :]
        other_ref[at, 2:6] = scr_m[pl.ds(4 * f, 4), :]
        other_ref[at, 6:8] = scr_e[pl.ds(Q_ROWS + 2 * f, 2), :]
    for i in range(37):
        other_ref[i, 0:1] = scr_e[pl.ds(24 + i, 1), :]
        other_ref[i, 1:7] = scr_m[pl.ds(48 + 6 * i, 6), :]
        other_ref[i, 7:8] = scr_e[pl.ds(Q_ROWS + 24 + i, 1), :]


def krylov_kernel(
    own_ref, plane_ref, image_ref, other_ref, outer_ref, core_ref,
    gram_ref, t_ref, below, above, other_s,
):
    sort_slabs(outer_ref, core_ref, below, above)

    for i in range(49):
        other_s[i, 0:8] = other_ref[i]
        if i < 37:
            put_halo(other_s, i, below, above, 24 + i, 1)
        else:
            put_halo(other_s, i, below, above, 2 * (i - 31) if i < 43 else 2 * (i - 43), 2)

    res_p, res_q = plane_ref[36], other_s[36]
    diffusion_p, diffusion_q = around(res_p), around(res_q)
    state_p = [plane_ref[49 + i] for i in range(9)]
    state_q = sums_of([other_s[37 + i] for i in range(6)])
    tang_p = [plane_ref[43 + i] for i in range(6)]
    tang_q = [other_s[43 + i] for i in range(6)]
    krylov = [[own_ref[43 + i] for i in range(6)]]
    for i in range(6):
        t_ref[i] = tang_p[i][0:8]

    def shifted(tangents, shift, earlier):
        return [t - shift * e[0 : t.shape[0]] for t, e in zip(tangents, earlier)]

    plane_p = (state_p, tang_p, tangent_sums(state_p, tang_p))
    plane_q = (state_q, tang_q, tangent_sums(state_q, tang_q))
    image_p = [image_ref[i] for i in range(6)]
    image_q = in_plane(*plane_q, diffusion_q, 16)
    image_p = between_planes(image_p, tang_p, plane_q, plane_q, res_p)
    image_q = between_planes(image_q, tang_q, plane_p, plane_p, res_q)
    krylov.append([image_p[i][0:8] - SHIFTS[0] * krylov[0][i] for i in range(6)])
    next_p = shifted(precondition(plane_ref, image_p), SHIFTS[0], tang_p)
    next_q = shifted(precondition(other_s, image_q), SHIFTS[0], tang_q)
    for i in range(6):
        t_ref[6 + i] = next_p[i][0:8]

    plane_p = (state_p, next_p, tangent_sums(state_p, next_p))
    plane_q = (state_q, next_q, tangent_sums(state_q, next_q))
    image_p = in_plane(*plane_p, diffusion_p, 16)
    image_q = in_plane(*plane_q, diffusion_q, 8)
    image_p = between_planes(image_p, next_p, plane_q, plane_q, res_p)
    image_q = between_planes(image_q, next_q, plane_p, plane_p, res_q)
    krylov.append([image_p[i][0:8] - SHIFTS[1] * krylov[1][i] for i in range(6)])
    last_p = shifted(precondition(plane_ref, image_p), SHIFTS[1], next_p)
    last_q = shifted(precondition(other_s, image_q), SHIFTS[1], next_q)
    for i in range(6):
        t_ref[12 + i] = last_p[i][0:8]

    plane_p = (state_p, last_p, tangent_sums(state_p, last_p))
    half_q = first_rows(state_q, 8)
    plane_q = (half_q, last_q, tangent_sums(half_q, last_q))
    image_p = in_plane(*plane_p, diffusion_p, 8)
    image_p = between_planes(image_p, last_p, plane_q, plane_q, res_p)
    krylov.append([image_p[i] - SHIFTS[2] * krylov[2][i] for i in range(6)])

    rows = lax.broadcasted_iota(jnp.int32, (16, 128), 0)
    lanes = lax.broadcasted_iota(jnp.int32, (16, 128), 1)
    table = jnp.zeros((16, 128), F32)
    for k, (i, j) in enumerate(PAIRS):
        total = krylov[i][0] * krylov[j][0]
        for f in range(1, 6):
            total = total + krylov[i][f] * krylov[j][f]
        line = total[:, 0:128]
        for start in range(128, total.shape[1], 128):
            line = line + total[:, start : start + 128]
        table = jnp.where(rows == k, jnp.sum(line, axis=0, keepdims=True), table)
    sums = jnp.sum(table, axis=1, keepdims=True)
    out = jnp.sum(jnp.where(rows == lanes, sums, 0.0), axis=0, keepdims=True)
    gram_ref[...] = jnp.broadcast_to(out[None], gram_ref.shape)


def finish_kernel(inverse_root, gram_ref, t_ref, update_ref, estimates_ref):
    parts = [gram_ref[i] for i in range(gram_ref.shape[0])]
    while len(parts) > 1:
        parts = [a + b for a, b in zip(parts[0::2], parts[1::2])] + parts[len(parts) // 2 * 2 :]
    sums = parts[0]
    lanes = lax.broadcasted_iota(jnp.int32, sums.shape, 1)
    gram = {}
    for k, pair in enumerate(PAIRS):
        gram[pair] = jnp.sum(jnp.where(lanes == k, sums, 0.0), axis=1, keepdims=True)
    factors, estimate_list = solve_from_gram(gram)
    width = update_ref.shape[-1]
    wide = [jnp.broadcast_to(f, (8, width)) for f in factors]
    for i in range(6):
        update_ref[i] = wide[0] * t_ref[i] + wide[1] * t_ref[6 + i] + wide[2] * t_ref[12 + i]
    for k, value in enumerate(estimate_list):
        estimates_ref[k] = jnp.sum(value * inverse_root)


def two_planes(pol, plasma_state, right_side, resistivity, jacobi_blocks):
    rows, width = plasma_state.shape[2], plasma_state.shape[3]
    count = 2 * pol

    def pairs(partner):
        return [(t * pol + p, q * pol + r) for t in range(2) for p in range(pol) for q, r in [partner(t, p)]]

    def beyond(t, p, far):
        r = p - 1 if p % 2 == 0 else p + 1
        return (far, r) if 0 <= r < pol else (1 - t, p)

    across = pairs(lambda t, p: (1 - t, p))
    core = pairs(lambda t, p: (t, p ^ 1))
    outer = pairs(lambda t, p: beyond(t, p, t))
    corner = pairs(lambda t, p: beyond(t, p, 1 - t))

    plasma = plasma_state.reshape(6, rows, width)
    rhs = right_side.reshape(6, rows, width)
    res = resistivity.reshape(1, rows, width)
    blocks = jacobi_blocks.reshape(6, 6, rows, width)
    vmem = pl.BlockSpec(memory_space=pltpu.VMEM)
    shape = jax.ShapeDtypeStruct
    t0, own, ends = pl.pallas_call(
        first_kernel,
        out_shape=(
            vmem_array((6, rows, width), F32),
            vmem_array((49, rows, width), F32),
            vmem_array((2 * Q_ROWS, width), BF16),
        ),
        in_specs=[pl.BlockSpec(memory_space=pltpu.HBM)] * 4,
        out_specs=(vmem,) * 3,
        scratch_shapes=[pltpu.VMEM((Q_ROWS, width), F32), pltpu.SemaphoreType.DMA((9,))],
    )(*map(in_hbm, (plasma, rhs, blocks, res)))
    edge = ends[:Q_ROWS]
    ends = lax.ppermute(ends, AXES, across)
    middle = pl.pallas_call(
        middle_kernel,
        out_shape=vmem_array((M_ROWS, width), BF16),
        in_specs=[vmem] * 2,
        out_specs=vmem,
        scratch_shapes=[pltpu.VMEM((M_ROWS, width), F32)],
    )(in_vmem(t0), in_vmem(own))
    side, core_side = pl.pallas_call(
        pack_kernel,
        out_shape=(vmem_array((P_ROWS, width), BF16),) * 2,
        in_specs=[vmem] * 2,
        out_specs=(vmem,) * 2,
        scratch_shapes=[pltpu.VMEM((P_ROWS, width), F32)],
    )(in_vmem(t0), in_vmem(own))
    middle = lax.ppermute(middle, AXES, across)
    outer_p = lax.ppermute(side, AXES, outer)
    core_p = lax.ppermute(core_side, AXES, core)
    outer_q = lax.ppermute(edge, AXES, corner)
    core_q = lax.ppermute(ends[Q_ROWS:], AXES, core)
    other = pl.pallas_call(
        other_plane_kernel,
        out_shape=vmem_array((49, rows, width), F32),
        in_specs=[vmem] * 2,
        out_specs=vmem,
        scratch_shapes=[pltpu.VMEM((2 * Q_ROWS, width), F32), pltpu.VMEM((M_ROWS, width), F32)],
        cost_estimate=pl.CostEstimate(flops=0, bytes_accessed=1_000_000, transcendentals=0),
    )(in_vmem(middle), in_vmem(ends))
    plane, image = pl.pallas_call(
        own_plane_kernel,
        out_shape=(vmem_array((58, 16, width), F32), vmem_array((6, 16, width), F32)),
        in_specs=[vmem] * 4,
        out_specs=(vmem,) * 2,
        scratch_shapes=[pltpu.VMEM((P_ROWS, width), F32)] * 2,
        cost_estimate=pl.CostEstimate(flops=1000000000, bytes_accessed=1_000_000, transcendentals=0),
    )(*map(in_vmem, (own, t0, outer_p, core_p)))
    gram, tangents = pl.pallas_call(
        krylov_kernel,
        out_shape=(vmem_array((count, 1, 128), F32), vmem_array((18, rows, width), F32)),
        in_specs=[vmem] * 6,
        out_specs=(vmem,) * 2,
        scratch_shapes=[pltpu.VMEM((Q_ROWS, width), F32)] * 2 + [pltpu.VMEM((49, 16, width), F32)],
    )(*map(in_vmem, (own, plane, image, other, outer_q, core_q)))
    gram = lax.all_to_all(gram, AXES, 0, 0, tiled=True)
    inverse_root = float((6.0 * count * rows * width) ** -0.5)
    update, estimates = pl.pallas_call(
        functools.partial(finish_kernel, inverse_root),
        out_shape=(shape((6, rows, width), F32), shape((ITERS,), F32)),
        in_specs=[vmem] * 2,
        out_specs=(vmem, pl.BlockSpec(memory_space=pltpu.SMEM)),
    )(in_vmem(gram), in_vmem(tangents))
    return update.reshape(plasma_state.shape), estimates


def padded(cells, axis, dim, closed):
    count = lax.axis_size(axis)
    ends = count if closed else count - 1
    size = cells.shape[dim]
    head = lax.slice_in_dim(cells, 0, 1, axis=dim)
    tail = lax.slice_in_dim(cells, size - 1, size, axis=dim)
    before = lax.ppermute(tail, axis, [(i, (i + 1) % count) for i in range(ends)])
    after = lax.ppermute(head, axis, [((i + 1) % count, i) for i in range(ends)])
    return jnp.concatenate([before, cells, after], axis=dim)


def any_planes(plasma_state, right_side, resistivity, jacobi_blocks):
    cell_count = right_side.size * lax.axis_size("tor") * lax.axis_size("pol")
    fixed = jnp.full((3,) + resistivity.shape, viscosity, F32)
    diffusion = jnp.concatenate([jnp.broadcast_to(resistivity[None], fixed.shape), fixed])

    def around(cells):
        planes = padded(cells.astype(BF16), "tor", 1, True).astype(F32)
        planes = jnp.concatenate([planes[:, :1], cells, planes[:, -1:]], axis=1)
        deep = jnp.pad(cells, ((0, 0), (0, 0), (0, 0), (1, 1)))
        return planes, padded(cells, "pol", 2, False), deep

    plasma_around = around(plasma_state)
    vectors, tangents = [right_side], []
    for shift in SHIFTS:
        vector = vectors[-1]
        tangent = jnp.sum(jacobi_blocks * vector[None], axis=1)
        tangents.append(tangent)
        image = inverse_step * tangent
        laplace = jnp.zeros_like(tangent)
        for direction, (plasma, cells) in enumerate(zip(plasma_around, around(tangent))):
            dim = direction + 1
            flux = jnp.stack(linear_flux(plasma, cells, direction))
            size = cells.shape[dim]
            part = functools.partial(lax.slice_in_dim, axis=dim)
            image = image + 0.5 * (part(flux, 2, size) - part(flux, 0, size - 2))
            laplace = laplace + part(cells, 2, size) + part(cells, 0, size - 2) - 2.0 * tangent
        vectors.append(image - diffusion * laplace - shift * vector)
    local = jnp.stack([jnp.sum(vectors[i] * vectors[j]) for i, j in PAIRS])
    gram = lax.psum(local, AXES)
    factors, estimate_list = solve_from_gram({pair: gram[k] for k, pair in enumerate(PAIRS)})
    update = sum(factor * tangent for factor, tangent in zip(factors, tangents))
    return update, jnp.stack(estimate_list) / jnp.sqrt(F32(cell_count))


def solution(mesh):
    tor, pol = mesh.shape["tor"], mesh.shape["pol"]

    def shards(plasma_state, right_side, resistivity, jacobi_blocks):
        _, planes, rows, width = plasma_state.shape
        fast = tor == 2 and planes == 1 and pol % 2 == 0 and rows == 8 and width % 128 == 0
        if fast:
            return two_planes(pol, plasma_state, right_side, resistivity, jacobi_blocks)
        return any_planes(plasma_state, right_side, resistivity, jacobi_blocks)

    return jax.shard_map(
        shards,
        mesh=mesh,
        in_specs=(
            P(None, "tor", "pol", None),
            P(None, "tor", "pol", None),
            P("tor", "pol", None),
            P(None, None, "tor", "pol", None),
        ),
        out_specs=(P(None, "tor", "pol", None), P()),
        check_vma=False,
    )
```

```python
import functools

import jax
import jax.numpy as jnp
from jax import lax
from jax.experimental import pallas as pl
from jax.experimental.pallas import tpu as pltpu
from jax.sharding import PartitionSpec as P

ITERS = 3
SHIFTS = (1.0, 2.0, 3.0)
inverse_step = 1.0
viscosity = 0.2
epsilon = 1e-06
AXES = ("tor", "pol")
PAIRS = [(i, j) for i in range(ITERS + 1) for j in range(i, ITERS + 1)]
BF16 = jnp.bfloat16
F32 = jnp.float32


def linear_flux(plasma, tangent, direction):
    magnetic, velocity = plasma[0:3], plasma[3:6]
    tang_mag, tang_vel = tangent[0:3], tangent[3:6]
    pressure = magnetic[0] * tang_mag[0] + magnetic[1] * tang_mag[1] + magnetic[2] * tang_mag[2]
    components = []
    for i in range(3):
        components.append(
            tang_vel[direction] * magnetic[i]
            + velocity[direction] * tang_mag[i]
            - tang_mag[direction] * velocity[i]
            - magnetic[direction] * tang_vel[i]
        )
    for i in range(3):
        moment = (
            tang_vel[direction] * velocity[i]
            + velocity[direction] * tang_vel[i]
            - tang_mag[direction] * magnetic[i]
            - magnetic[direction] * tang_mag[i]
        )
        if i == direction:
            moment = moment + pressure
        components.append(moment)
    return components


def least_squares(columns, initial_norm):
    count = len(columns)
    rhs_list = [initial_norm] + [None] * count
    cosines = []
    sines = []
    triangle = []
    estimate_list = []
    for column in range(count):
        entries = list(columns[column])
        for i in range(column):
            first_value, second_value = entries[i], entries[i + 1]
            entries[i] = cosines[i] * first_value + sines[i] * second_value
            entries[i + 1] = -sines[i] * first_value + cosines[i] * second_value
        first_value, second_value = entries[column], entries[column + 1]
        radius = jnp.sqrt(first_value * first_value + second_value * second_value)
        cosine = first_value / radius
        sine_value = second_value / radius
        cosines.append(cosine)
        sines.append(sine_value)
        entries[column] = radius
        triangle.append(entries[: column + 1])
        previous = rhs_list[column]
        rhs_list[column] = cosine * previous
        rhs_list[column + 1] = -sine_value * previous
        estimate_list.append(jnp.abs(rhs_list[column + 1]))
    weights = [None] * count
    for column in reversed(range(count)):
        partial_value = rhs_list[column]
        for later in range(column + 1, count):
            partial_value = partial_value - triangle[later][column] * weights[later]
        weights[column] = partial_value / triangle[column][column]
    return weights, estimate_list


def solve_from_gram(gram):
    count = ITERS + 1

    def inner(left, right):
        total = None
        for i in range(count):
            row = None
            for j in range(count):
                if right[j] is None:
                    continue
                term = gram[(min(i, j), max(i, j))] * right[j]
                row = term if row is None else row + term
            if left[i] is None or row is None:
                continue
            term = left[i] * row
            total = term if total is None else total + term
        return total

    def minus(left, factor, right):
        out = []
        for a, b in zip(left, right):
            if b is None:
                out.append(a)
            else:
                out.append(a - factor * b)
        return out

    initial_norm = jnp.sqrt(gram[(0, 0)] + epsilon)
    basis = [[1.0 / initial_norm] + [None] * ITERS]
    columns = []
    for column in range(ITERS):
        vector = basis[column]
        image = []
        for i in range(count):
            entry = None
            if vector[i] is not None:
                entry = SHIFTS[i] * vector[i]
            if i > 0 and vector[i - 1] is not None:
                entry = vector[i - 1] if entry is None else entry + vector[i - 1]
            image.append(entry)
        coefficients = [inner(earlier, image) for earlier in basis]
        remainder = image
        for coefficient, earlier in zip(coefficients, basis):
            remainder = minus(remainder, coefficient, earlier)
        square = jnp.maximum(inner(remainder, remainder), 0.0)
        new_norm = jnp.sqrt(square + epsilon)
        columns.append(coefficients + [new_norm])
        if column + 1 < ITERS:
            scale = 1.0 / new_norm
            basis.append([None if r is None else r * scale for r in remainder])
    weights, estimate_list = least_squares(columns, initial_norm)
    factors = []
    for k in range(ITERS):
        total = None
        for weight, vector in zip(weights, basis):
            if vector[k] is not None:
                term = weight * vector[k]
                total = term if total is None else total + term
        factors.append(total)
    return factors, estimate_list


in_vmem = functools.partial(pltpu.with_memory_space_constraint, memory_space=pltpu.VMEM)
in_hbm = functools.partial(pltpu.with_memory_space_constraint, memory_space=pltpu.HBM)
vmem_array = pltpu.VMEM
P_ROWS, Q_ROWS = 128, 64
M_ROWS = 272


def tile_rows(value, count, first):
    return jnp.where(first, value[0:count], value[8 - count : 8])


def fill_slab_q(scr, deep, wide, first):
    scr[pl.ds(Q_ROWS - 8, 8), :] = jnp.zeros((8, deep[0].shape[1]), F32)
    for f, value in enumerate(deep):
        scr[pl.ds(2 * f, 2), :] = tile_rows(value, 2, first)
    for f, value in enumerate(wide):
        scr[pl.ds(24 + f, 1), :] = tile_rows(value, 1, first)
    return scr[...].astype(BF16)


def fill_slab_p(scr, deep, wide, first):
    scr[pl.ds(P_ROWS - 8, 8), :] = jnp.zeros((8, deep[0].shape[1]), F32)
    for f, value in enumerate(deep):
        scr[pl.ds(4 * f, 4), :] = tile_rows(value, 4, first)
    for f, value in enumerate(wide):
        scr[pl.ds(48 + 2 * f, 2), :] = tile_rows(value, 2, first)
    return scr[...].astype(BF16)


def first_kernel(
    plasma_hbm, rhs_hbm, blocks_hbm, res_hbm,
    t0_ref, own_ref, ends_ref, scr, sems,
):
    copies = [
        pltpu.make_async_copy(rhs_hbm, own_ref.at[pl.ds(43, 6)], sems.at[0]),
        pltpu.make_async_copy(plasma_hbm, own_ref.at[pl.ds(37, 6)], sems.at[1]),
        pltpu.make_async_copy(res_hbm, own_ref.at[pl.ds(36, 1)], sems.at[2]),
    ] + [pltpu.make_async_copy(blocks_hbm.at[a], own_ref.at[pl.ds(6 * a, 6)], sems.at[3 + a]) for a in range(6)]
    for copy in copies:
        copy.start()
    even = lax.axis_index("pol") % 2 == 0
    sides = ((scr.at[0], even), (scr.at[1], jnp.logical_not(even)))

    def put(offset, count, value):
        for slab, first in sides:
            slab[pl.ds(offset, count), :] = tile_rows(value, count, first)

    for copy in copies[:3]:
        copy.wait()
    for slab, _ in sides:
        slab[pl.ds(Q_ROWS - 8, 8), :] = jnp.zeros((8, scr.shape[-1]), F32)
    for i in range(6):
        put(12 + 2 * i, 2, own_ref[37 + i])
    put(60, 1, own_ref[36])
    vector = [own_ref[43 + b] for b in range(6)]
    for a in range(6):
        copies[3 + a].wait()
        total = own_ref[6 * a] * vector[0]
        for b in range(1, 6):
            total = total + own_ref[6 * a + b] * vector[b]
        t0_ref[a] = total
        put(2 * a, 2, total)
        for b in range(6):
            put(24 + 6 * a + b, 1, own_ref[6 * a + b])
    ends_ref[pl.ds(0, Q_ROWS), :] = scr[0].astype(BF16)
    ends_ref[pl.ds(Q_ROWS, Q_ROWS), :] = scr[1].astype(BF16)


def middle_kernel(t0_ref, own_ref, middle_ref, scr_m):
    deep = [t0_ref[i] for i in range(6)] + [own_ref[37 + i] for i in range(6)]
    wide = [own_ref[i] for i in range(37)]
    scr_m[pl.ds(M_ROWS - 8, 8), :] = jnp.zeros((8, scr_m.shape[1]), F32)
    for f, value in enumerate(deep):
        scr_m[pl.ds(4 * f, 4), :] = value[2:6]
    for f, value in enumerate(wide):
        scr_m[pl.ds(48 + 6 * f, 6), :] = value[1:7]
    middle_ref[...] = scr_m[...].astype(BF16)


def pack_kernel(t0_ref, own_ref, side_ref, core_ref, scr):
    even = lax.axis_index("pol") % 2 == 0
    deep = [t0_ref[i] for i in range(6)] + [own_ref[37 + i] for i in range(6)]
    wide = [own_ref[i] for i in range(37)]
    side_ref[...] = fill_slab_p(scr, deep, wide, even)
    core_ref[...] = fill_slab_p(scr, deep, wide, jnp.logical_not(even))


def depth_next(x):
    width = x.shape[1]
    lanes = lax.broadcasted_iota(jnp.int32, x.shape, 1)
    return jnp.where(lanes == width - 1, 0.0, pltpu.roll(x, width - 1, 1))


def depth_prev(x):
    lanes = lax.broadcasted_iota(jnp.int32, x.shape, 1)
    return jnp.where(lanes == 0, 0.0, pltpu.roll(x, 1, 1))


def sums_of(plasma):
    magnetic, velocity = plasma[0:3], plasma[3:6]
    return (
        [0.25 * (v + b) for v, b in zip(velocity, magnetic)]
        + [0.25 * (v - b) for v, b in zip(velocity, magnetic)]
        + [0.5 * b for b in magnetic]
    )


def tangent_sums(state, tangent):
    tang_mag, tang_vel = tangent[0:3], tangent[3:6]
    half_pressure = state[6] * tang_mag[0] + state[7] * tang_mag[1] + state[8] * tang_mag[2]
    return (
        [w + b for w, b in zip(tang_vel, tang_mag)]
        + [w - b for w, b in zip(tang_vel, tang_mag)]
        + [half_pressure]
    )


def first_rows(values, rows):
    return [x[0:rows] for x in values]


def half_flux(state, sums, k):
    magnetic, velocity = [], []
    for i in range(3):
        plus = sums[3 + k] * state[i] + state[3 + k] * sums[i]
        minus = sums[k] * state[3 + i] + state[k] * sums[3 + i]
        magnetic.append(plus - minus)
        velocity.append(plus + minus + sums[6] if i == k else plus + minus)
    return magnetic + velocity


def row_next(x, rows):
    if rows == 16:
        return pltpu.roll(x, 15, 0)
    own = x[0:8]
    sublanes = lax.broadcasted_iota(jnp.int32, own.shape, 0)
    return pltpu.roll(jnp.where(sublanes == 0, x[8:16], own), 7, 0)


def row_prev(x, rows):
    if rows == 16:
        return pltpu.roll(x, 1, 0)
    own = x[0:8]
    sublanes = lax.broadcasted_iota(jnp.int32, own.shape, 0)
    return pltpu.roll(jnp.where(sublanes == 7, x[8:16], own), 1, 0)


def around(res):
    return res, row_prev(res, 16), row_next(res, 16), depth_prev(res), depth_next(res)


def in_plane(state, tangent, sums, diffusion, rows):
    flux_rows = half_flux(state, sums, 1)
    own = first_rows(tangent, rows)
    flux_depth = half_flux(first_rows(state, rows), first_rows(sums, rows), 2)
    out = []
    for i in range(6):
        here, above, below, west, east = diffusion if i < 3 else (viscosity,) * 5
        if i < 3:
            here, west, east = first_rows((here, west, east), rows)
        total = (inverse_step + 4.0 * here) * own[i]
        total = total + row_next(flux_rows[i] - above * tangent[i], rows)
        total = total - row_prev(flux_rows[i] + below * tangent[i], rows)
        total = total + depth_next(flux_depth[i] - west * own[i])
        total = total - depth_prev(flux_depth[i] + east * own[i])
        out.append(total)
    return out


def between_planes(image, tangent, after, before, res):
    rows = image[0].shape[0]
    (state_next, next_t, sums_next), (state_prev, prev_t, sums_prev) = [
        [first_rows(values, rows) for values in plane] for plane in (after, before)
    ]
    flux_next = half_flux(state_next, sums_next, 0)
    flux_prev = half_flux(state_prev, sums_prev, 0)
    out = []
    for i in range(6):
        laplace = next_t[i] + prev_t[i] - 2.0 * tangent[i][0:rows]
        total = image[i] + (flux_next[i] - flux_prev[i])
        out.append(total - (res[0:rows] if i < 3 else viscosity) * laplace)
    return out


def precondition(ref, vector):
    rows = vector[0].shape[0]
    out = []
    for a in range(6):
        total = ref[6 * a, 0:rows] * vector[0]
        for b in range(1, 6):
            total = total + ref[6 * a + b, 0:rows] * vector[b]
        out.append(total)
    return out


def put_halo(ref, at, below, above, offset, rows):
    if rows < 4:
        ref[at, 8:16] = jnp.zeros((8, ref.shape[-1]), F32)
    ref[at, 8 : 8 + rows] = below[pl.ds(offset, rows), :]
    ref[at, 16 - rows : 16] = above[pl.ds(offset, rows), :]


def sort_slabs(outer_ref, core_ref, below, above):
    place = lax.axis_index("pol")
    even = place % 2 == 0
    edge = jnp.logical_or(place == 0, place == lax.axis_size("pol") - 1)
    from_outer = jnp.where(edge, 0.0, outer_ref[...].astype(F32))
    from_core = core_ref[...].astype(F32)
    above[...] = jnp.where(even, from_outer, from_core)
    below[...] = jnp.where(even, from_core, from_outer)


def own_plane_kernel(own_ref, t0_ref, outer_ref, core_ref, plane_ref, image_ref, below, above):
    sort_slabs(outer_ref, core_ref, below, above)
    for i in range(37):
        plane_ref[i, 0:8] = own_ref[i]
        put_halo(plane_ref, i, below, above, 48 + 2 * i, 2)
    for i in range(6):
        plane_ref[37 + i, 0:8] = own_ref[37 + i]
        put_halo(plane_ref, 37 + i, below, above, 24 + 4 * i, 4)
        plane_ref[43 + i, 0:8] = t0_ref[i]
        put_halo(plane_ref, 43 + i, below, above, 4 * i, 4)
    state = sums_of([plane_ref[37 + i] for i in range(6)])
    for i, value in enumerate(state):
        plane_ref[49 + i] = value
    tangent = [plane_ref[43 + i] for i in range(6)]
    sums = tangent_sums(state, tangent)
    for i, value in enumerate(in_plane(state, tangent, sums, around(plane_ref[36]), 16)):
        image_ref[i] = value


def other_plane_kernel(middle_ref, ends_ref, other_ref, scr_e, scr_m):
    even = lax.axis_index("pol") % 2 == 0
    outer, inner = ends_ref[pl.ds(0, Q_ROWS), :].astype(F32), ends_ref[pl.ds(Q_ROWS, Q_ROWS), :].astype(F32)
    scr_e[pl.ds(0, Q_ROWS), :] = jnp.where(even, outer, inner)
    scr_e[pl.ds(Q_ROWS, Q_ROWS), :] = jnp.where(even, inner, outer)
    scr_m[...] = middle_ref[...].astype(F32)
    for f in range(12):
        at = 43 + f if f < 6 else 31 + f
        other_ref[at, 0:2] = scr_e[pl.ds(2 * f, 2), :]
        other_ref[at, 2:6] = scr_m[pl.ds(4 * f, 4), :]
        other_ref[at, 6:8] = scr_e[pl.ds(Q_ROWS + 2 * f, 2), :]
    for i in range(37):
        other_ref[i, 0:1] = scr_e[pl.ds(24 + i, 1), :]
        other_ref[i, 1:7] = scr_m[pl.ds(48 + 6 * i, 6), :]
        other_ref[i, 7:8] = scr_e[pl.ds(Q_ROWS + 24 + i, 1), :]


def krylov_kernel(
    own_ref, plane_ref, image_ref, other_ref, outer_ref, core_ref,
    gram_ref, t_ref, below, above, other_s,
):
    sort_slabs(outer_ref, core_ref, below, above)

    for i in range(49):
        other_s[i, 0:8] = other_ref[i]
        if i < 37:
            put_halo(other_s, i, below, above, 24 + i, 1)
        else:
            put_halo(other_s, i, below, above, 2 * (i - 31) if i < 43 else 2 * (i - 43), 2)

    res_p, res_q = plane_ref[36], other_s[36]
    diffusion_p, diffusion_q = around(res_p), around(res_q)
    state_p = [plane_ref[49 + i] for i in range(9)]
    state_q = sums_of([other_s[37 + i] for i in range(6)])
    tang_p = [plane_ref[43 + i] for i in range(6)]
    tang_q = [other_s[43 + i] for i in range(6)]
    krylov = [[own_ref[43 + i] for i in range(6)]]
    for i in range(6):
        t_ref[i] = tang_p[i][0:8]

    def shifted(tangents, shift, earlier):
        return [t - shift * e[0 : t.shape[0]] for t, e in zip(tangents, earlier)]

    plane_p = (state_p, tang_p, tangent_sums(state_p, tang_p))
    plane_q = (state_q, tang_q, tangent_sums(state_q, tang_q))
    image_p = [image_ref[i] for i in range(6)]
    image_q = in_plane(*plane_q, diffusion_q, 16)
    image_p = between_planes(image_p, tang_p, plane_q, plane_q, res_p)
    image_q = between_planes(image_q, tang_q, plane_p, plane_p, res_q)
    krylov.append([image_p[i][0:8] - SHIFTS[0] * krylov[0][i] for i in range(6)])
    next_p = shifted(precondition(plane_ref, image_p), SHIFTS[0], tang_p)
    next_q = shifted(precondition(other_s, image_q), SHIFTS[0], tang_q)
    for i in range(6):
        t_ref[6 + i] = next_p[i][0:8]

    plane_p = (state_p, next_p, tangent_sums(state_p, next_p))
    plane_q = (state_q, next_q, tangent_sums(state_q, next_q))
    image_p = in_plane(*plane_p, diffusion_p, 16)
    image_q = in_plane(*plane_q, diffusion_q, 8)
    image_p = between_planes(image_p, next_p, plane_q, plane_q, res_p)
    image_q = between_planes(image_q, next_q, plane_p, plane_p, res_q)
    krylov.append([image_p[i][0:8] - SHIFTS[1] * krylov[1][i] for i in range(6)])
    last_p = shifted(precondition(plane_ref, image_p), SHIFTS[1], next_p)
    last_q = shifted(precondition(other_s, image_q), SHIFTS[1], next_q)
    for i in range(6):
        t_ref[12 + i] = last_p[i][0:8]

    plane_p = (state_p, last_p, tangent_sums(state_p, last_p))
    half_q = first_rows(state_q, 8)
    plane_q = (half_q, last_q, tangent_sums(half_q, last_q))
    image_p = in_plane(*plane_p, diffusion_p, 8)
    image_p = between_planes(image_p, last_p, plane_q, plane_q, res_p)
    krylov.append([image_p[i] - SHIFTS[2] * krylov[2][i] for i in range(6)])

    rows = lax.broadcasted_iota(jnp.int32, (16, 128), 0)
    lanes = lax.broadcasted_iota(jnp.int32, (16, 128), 1)
    table = jnp.zeros((16, 128), F32)
    for k, (i, j) in enumerate(PAIRS):
        total = krylov[i][0] * krylov[j][0]
        for f in range(1, 6):
            total = total + krylov[i][f] * krylov[j][f]
        line = total[:, 0:128]
        for start in range(128, total.shape[1], 128):
            line = line + total[:, start : start + 128]
        table = jnp.where(rows == k, jnp.sum(line, axis=0, keepdims=True), table)
    sums = jnp.sum(table, axis=1, keepdims=True)
    out = jnp.sum(jnp.where(rows == lanes, sums, 0.0), axis=0, keepdims=True)
    gram_ref[...] = jnp.broadcast_to(out[None], gram_ref.shape)


def finish_kernel(inverse_root, gram_ref, t_ref, update_ref, estimates_ref):
    parts = [gram_ref[i] for i in range(gram_ref.shape[0])]
    while len(parts) > 1:
        parts = [a + b for a, b in zip(parts[0::2], parts[1::2])] + parts[len(parts) // 2 * 2 :]
    sums = parts[0]
    lanes = lax.broadcasted_iota(jnp.int32, sums.shape, 1)
    gram = {}
    for k, pair in enumerate(PAIRS):
        gram[pair] = jnp.sum(jnp.where(lanes == k, sums, 0.0), axis=1, keepdims=True)
    factors, estimate_list = solve_from_gram(gram)
    width = update_ref.shape[-1]
    wide = [jnp.broadcast_to(f, (8, width)) for f in factors]
    for i in range(6):
        update_ref[i] = wide[0] * t_ref[i] + wide[1] * t_ref[6 + i] + wide[2] * t_ref[12 + i]
    for k, value in enumerate(estimate_list):
        estimates_ref[k] = jnp.sum(value * inverse_root)


def two_planes(pol, plasma_state, right_side, resistivity, jacobi_blocks):
    rows, width = plasma_state.shape[2], plasma_state.shape[3]
    count = 2 * pol

    def pairs(partner):
        return [(t * pol + p, q * pol + r) for t in range(2) for p in range(pol) for q, r in [partner(t, p)]]

    def beyond(t, p, far):
        r = p - 1 if p % 2 == 0 else p + 1
        return (far, r) if 0 <= r < pol else (1 - t, p)

    across = pairs(lambda t, p: (1 - t, p))
    core = pairs(lambda t, p: (t, p ^ 1))
    outer = pairs(lambda t, p: beyond(t, p, t))
    corner = pairs(lambda t, p: beyond(t, p, 1 - t))

    plasma = plasma_state.reshape(6, rows, width)
    rhs = right_side.reshape(6, rows, width)
    res = resistivity.reshape(1, rows, width)
    blocks = jacobi_blocks.reshape(6, 6, rows, width)
    vmem = pl.BlockSpec(memory_space=pltpu.VMEM)
    shape = jax.ShapeDtypeStruct
    t0, own, ends = pl.pallas_call(
        first_kernel,
        out_shape=(
            vmem_array((6, rows, width), F32),
            vmem_array((49, rows, width), F32),
            vmem_array((2 * Q_ROWS, width), BF16),
        ),
        in_specs=[pl.BlockSpec(memory_space=pltpu.HBM)] * 4,
        out_specs=(vmem,) * 3,
        scratch_shapes=[pltpu.VMEM((2, Q_ROWS, width), F32), pltpu.SemaphoreType.DMA((9,))],
    )(*map(in_hbm, (plasma, rhs, blocks, res)))
    edge = ends[:Q_ROWS]
    ends = lax.ppermute(ends, AXES, across)
    middle = pl.pallas_call(
        middle_kernel,
        out_shape=vmem_array((M_ROWS, width), BF16),
        in_specs=[vmem] * 2,
        out_specs=vmem,
        scratch_shapes=[pltpu.VMEM((M_ROWS, width), F32)],
    )(in_vmem(t0), in_vmem(own))
    side, core_side = pl.pallas_call(
        pack_kernel,
        out_shape=(vmem_array((P_ROWS, width), BF16),) * 2,
        in_specs=[vmem] * 2,
        out_specs=(vmem,) * 2,
        scratch_shapes=[pltpu.VMEM((P_ROWS, width), F32)],
    )(in_vmem(t0), in_vmem(own))
    middle = lax.ppermute(middle, AXES, across)
    outer_p = lax.ppermute(side, AXES, outer)
    core_p = lax.ppermute(core_side, AXES, core)
    outer_q = lax.ppermute(edge, AXES, corner)
    core_q = lax.ppermute(ends[Q_ROWS:], AXES, core)
    other = pl.pallas_call(
        other_plane_kernel,
        out_shape=vmem_array((49, rows, width), F32),
        in_specs=[vmem] * 2,
        out_specs=vmem,
        scratch_shapes=[pltpu.VMEM((2 * Q_ROWS, width), F32), pltpu.VMEM((M_ROWS, width), F32)],
        cost_estimate=pl.CostEstimate(flops=0, bytes_accessed=1_000_000, transcendentals=0),
    )(in_vmem(middle), in_vmem(ends))
    plane, image = pl.pallas_call(
        own_plane_kernel,
        out_shape=(vmem_array((58, 16, width), F32), vmem_array((6, 16, width), F32)),
        in_specs=[vmem] * 4,
        out_specs=(vmem,) * 2,
        scratch_shapes=[pltpu.VMEM((P_ROWS, width), F32)] * 2,
        cost_estimate=pl.CostEstimate(flops=1000000000, bytes_accessed=1_000_000, transcendentals=0),
    )(*map(in_vmem, (own, t0, outer_p, core_p)))
    gram, tangents = pl.pallas_call(
        krylov_kernel,
        out_shape=(vmem_array((count, 1, 128), F32), vmem_array((18, rows, width), F32)),
        in_specs=[vmem] * 6,
        out_specs=(vmem,) * 2,
        scratch_shapes=[pltpu.VMEM((Q_ROWS, width), F32)] * 2 + [pltpu.VMEM((49, 16, width), F32)],
    )(*map(in_vmem, (own, plane, image, other, outer_q, core_q)))
    gram = lax.all_to_all(gram, AXES, 0, 0, tiled=True)
    inverse_root = float((6.0 * count * rows * width) ** -0.5)
    update, estimates = pl.pallas_call(
        functools.partial(finish_kernel, inverse_root),
        out_shape=(shape((6, rows, width), F32), shape((ITERS,), F32)),
        in_specs=[vmem] * 2,
        out_specs=(vmem, pl.BlockSpec(memory_space=pltpu.SMEM)),
    )(in_vmem(gram), in_vmem(tangents))
    return update.reshape(plasma_state.shape), estimates


def padded(cells, axis, dim, closed):
    count = lax.axis_size(axis)
    ends = count if closed else count - 1
    size = cells.shape[dim]
    head = lax.slice_in_dim(cells, 0, 1, axis=dim)
    tail = lax.slice_in_dim(cells, size - 1, size, axis=dim)
    before = lax.ppermute(tail, axis, [(i, (i + 1) % count) for i in range(ends)])
    after = lax.ppermute(head, axis, [((i + 1) % count, i) for i in range(ends)])
    return jnp.concatenate([before, cells, after], axis=dim)


def any_planes(plasma_state, right_side, resistivity, jacobi_blocks):
    cell_count = right_side.size * lax.axis_size("tor") * lax.axis_size("pol")
    fixed = jnp.full((3,) + resistivity.shape, viscosity, F32)
    diffusion = jnp.concatenate([jnp.broadcast_to(resistivity[None], fixed.shape), fixed])

    def around(cells):
        planes = padded(cells.astype(BF16), "tor", 1, True).astype(F32)
        planes = jnp.concatenate([planes[:, :1], cells, planes[:, -1:]], axis=1)
        deep = jnp.pad(cells, ((0, 0), (0, 0), (0, 0), (1, 1)))
        return planes, padded(cells, "pol", 2, False), deep

    plasma_around = around(plasma_state)
    vectors, tangents = [right_side], []
    for shift in SHIFTS:
        vector = vectors[-1]
        tangent = jnp.sum(jacobi_blocks * vector[None], axis=1)
        tangents.append(tangent)
        image = inverse_step * tangent
        laplace = jnp.zeros_like(tangent)
        for direction, (plasma, cells) in enumerate(zip(plasma_around, around(tangent))):
            dim = direction + 1
            flux = jnp.stack(linear_flux(plasma, cells, direction))
            size = cells.shape[dim]
            part = functools.partial(lax.slice_in_dim, axis=dim)
            image = image + 0.5 * (part(flux, 2, size) - part(flux, 0, size - 2))
            laplace = laplace + part(cells, 2, size) + part(cells, 0, size - 2) - 2.0 * tangent
        vectors.append(image - diffusion * laplace - shift * vector)
    local = jnp.stack([jnp.sum(vectors[i] * vectors[j]) for i, j in PAIRS])
    gram = lax.psum(local, AXES)
    factors, estimate_list = solve_from_gram({pair: gram[k] for k, pair in enumerate(PAIRS)})
    update = sum(factor * tangent for factor, tangent in zip(factors, tangents))
    return update, jnp.stack(estimate_list) / jnp.sqrt(F32(cell_count))


def solution(mesh):
    tor, pol = mesh.shape["tor"], mesh.shape["pol"]

    def shards(plasma_state, right_side, resistivity, jacobi_blocks):
        _, planes, rows, width = plasma_state.shape
        fast = tor == 2 and planes == 1 and pol % 2 == 0 and rows == 8 and width % 128 == 0
        if fast:
            return two_planes(pol, plasma_state, right_side, resistivity, jacobi_blocks)
        return any_planes(plasma_state, right_side, resistivity, jacobi_blocks)

    return jax.shard_map(
        shards,
        mesh=mesh,
        in_specs=(
            P(None, "tor", "pol", None),
            P(None, "tor", "pol", None),
            P("tor", "pol", None),
            P(None, None, "tor", "pol", None),
        ),
        out_specs=(P(None, "tor", "pol", None), P()),
        check_vma=False,
    )
```
